128 devices in a mesh: rad: 32 (over x, z_hi, y), az: 4 (over z_lo, core).
Axes of the slice: x: 4, y: 4, z: 4 (z_hi: 2, z_lo: 2; z = z_hi * 2 + z_lo), core: 2. Of those that a mesh axis runs over, the one named last changes fastest.
Arguments:
- surface_mass: float32 [1024, 16384], P('rad', 'az'), may hold values from 0.5 to 2
- outward_drift: float32 [1024, 16384], P('rad', 'az'), may hold values from -1.2 to 1.2
- leftover_angular_drift: float32 [1024, 16384], P('rad', 'az'), may hold values from -1.2 to 1.2
- angular_offsets: int32 [1024], P('rad'), may hold values from 0 to 16383
- planetesimal_loop_number: int32 [32], replicated, may hold values from 0 to 1023
- planetesimal_angle_bin: int32 [32], replicated, may hold values from 0 to 16383
- planetesimal_weights: float32 [32], replicated, may hold values from 0.001 to 0.01
Outputs:
- transported_density: float32 [1024, 16384], P('rad', 'az')
- kicked_radial_velocity: float32 [1024, 16384], P('rad', 'az')
- kicked_azimuthal_velocity: float32 [1024, 16384], P('rad', 'az')
- embryo_disk_acceleration: float32 [2, 32], replicated
The draws below stay inside these ranges and needn't reach their ends.
All inputs are finite; a program needn't handle non-finite values.
Results may differ from the reference program's by a relative error of at most 0.0003.
Values sent between devices are 32-bit elements; how exact they have to be, the bound alone decides.
No kernel may reach another device: no remote copies, remote signals or barrier semaphores. Data moves between devices by JAX's collectives and lax.ppermute only.
A program may use at most 64 MiB of HBM per device.

```python
import math
import jax
import jax.numpy as jnp
from jax import lax

ANGULAR_BINS = 16384
MODES = 256
EMB = 32
LOOP_COUNT = 1024


def place_ends(array, rng, least, top_value):
    longest = array.shape.index(max(array.shape))
    spots = []
    for shift in (0, 1):
        where = [jax.random.randint(jax.random.fold_in(rng, axis), (), 0, length) for axis, length in enumerate(array.shape)]
        where[longest] = (where[longest] + shift) % array.shape[longest]
        spots.append(tuple(where))
    return array.at[spots[0]].set(least).at[spots[1]].set(top_value)


def level_of(stream_key, extent, cuts, smallest, top_value):
    gain = 1.0
    for axis_at, shards_of in cuts:
        heights = jax.random.uniform(jax.random.fold_in(jax.random.fold_in(stream_key, 6), axis_at), (shards_of,), jnp.float32, smallest / len(cuts), top_value / len(cuts))
        gain = gain * jnp.repeat(jnp.exp(heights), extent[axis_at] // shards_of).reshape((-1,) + (1,) * (len(extent) - 1 - axis_at))
    return gain


def centred(key, extent, deviation, most, shards=(), kind=jnp.bfloat16):
    entries = jax.random.normal(key, extent, jnp.float32) * deviation
    if len(shards) > 0:
        entries = level_of(key, extent, shards, -0.22, 0.18) * entries
    return jnp.clip(entries, min=-most, max=most).astype(kind)


def setup_inputs(seed: int = 0) -> dict:
    streams_of = jax.random.split(jax.random.key(seed), 8)
    surface_mass = jnp.clip(jnp.exp(math.log(2.0) - 1.3862944 * jax.random.uniform(streams_of[0], (LOOP_COUNT, ANGULAR_BINS), jnp.float32) ** level_of(streams_of[0], (LOOP_COUNT, ANGULAR_BINS), ((0, 32), (1, 4)), -0.2, 0.2)), 0.5, 2.0)
    outward_drift = centred(streams_of[1], (LOOP_COUNT, ANGULAR_BINS), 0.3, 1.2, ((0, 32), (1, 4)), jnp.float32)
    leftover_angular_drift = centred(streams_of[2], (LOOP_COUNT, ANGULAR_BINS), 0.3, 1.2, ((0, 32), (1, 4)), jnp.float32)
    angular_offsets = place_ends(jax.random.randint(streams_of[3], (LOOP_COUNT,), 0, ANGULAR_BINS), jax.random.fold_in(streams_of[3], 1), 0, ANGULAR_BINS - 1).astype(jnp.int32)
    planetesimal_loop_number = place_ends(jax.random.randint(streams_of[4], (EMB,), 0, LOOP_COUNT), jax.random.fold_in(streams_of[4], 1), 0, LOOP_COUNT - 1).astype(jnp.int32)
    planetesimal_angle_bin = place_ends(jax.random.randint(streams_of[5], (EMB,), 0, ANGULAR_BINS), jax.random.fold_in(streams_of[5], 1), 0, ANGULAR_BINS - 1).astype(jnp.int32)
    planetesimal_weights = jnp.clip(jnp.exp(jax.random.uniform(streams_of[6], (EMB,), jnp.float32, math.log(0.001), math.log(0.01))), 0.001, 0.01)
    return dict(surface_mass=surface_mass, outward_drift=outward_drift, leftover_angular_drift=leftover_angular_drift, angular_offsets=angular_offsets, planetesimal_loop_number=planetesimal_loop_number, planetesimal_angle_bin=planetesimal_angle_bin, planetesimal_weights=planetesimal_weights)


gravity = 1.0
timestep_length = 0.05
courant = 0.4
softening = 0.02

def mode_tables(first, count):
    columns = first + jnp.arange(count, dtype=jnp.int32)
    orders = jnp.arange(MODES, dtype=jnp.int32)
    phases = orders[:, None] * (2 * columns[None, :] + 1) % (2 * ANGULAR_BINS)
    angles = phases.astype(jnp.float32) * (jnp.pi / ANGULAR_BINS)
    return jnp.concatenate([jnp.cos(angles), jnp.sin(angles)], axis=0)

def column_angles(first, count):
    columns = first + jnp.arange(count, dtype=jnp.int32)
    return (2 * columns + 1).astype(jnp.float32) * (jnp.pi / ANGULAR_BINS)

def cycle_radius(first, count, cell_step):
    cycles = first + jnp.arange(count, dtype=jnp.int32)
    return jnp.exp((cycles.astype(jnp.float32) + 0.5) * cell_step)

def donor_flux(orbital_speeds, upstream, downstream):
    return jnp.where(orbital_speeds > 0, orbital_speeds * upstream, orbital_speeds * downstream)

def reference(surface_mass, outward_drift, leftover_angular_drift, angular_offsets, planetesimal_loop_number, planetesimal_angle_bin, planetesimal_weights):
    cycle_total = surface_mass.shape[0]
    cell_step = 2.0 * jnp.pi / ANGULAR_BINS
    highest = lax.Precision.HIGHEST
    columns = jnp.arange(ANGULAR_BINS, dtype=jnp.int32)
    upwind_surface_mass = (columns[None, :] - angular_offsets[:, None]) % ANGULAR_BINS
    single_density = jnp.take_along_axis(surface_mass, upwind_surface_mass, axis=1)
    single_radial_velocity = jnp.take_along_axis(outward_drift, upwind_surface_mass, axis=1)
    lone_angular_drift = jnp.take_along_axis(leftover_angular_drift, upwind_surface_mass, axis=1)
    orbital_speeds = 0.5 * (lone_angular_drift + jnp.roll(lone_angular_drift, -1, axis=1))
    fluxes = donor_flux(orbital_speeds, single_density, jnp.roll(single_density, -1, axis=1))
    dens_two = single_density - courant * (fluxes - jnp.roll(fluxes, 1, axis=1))
    orbital_speeds = 0.5 * (single_radial_velocity[:-1] + single_radial_velocity[1:])
    inner = donor_flux(orbital_speeds, dens_two[:-1], dens_two[1:])
    zero_row = jnp.zeros_like(inner[:1])
    fluxes = jnp.concatenate([zero_row, inner, zero_row], axis=0)
    transported_density = dens_two - courant * (fluxes[1:] - fluxes[:-1])
    tables = mode_tables(0, ANGULAR_BINS)
    spectra = jnp.einsum('rc,mc->rm', transported_density, tables, precision=highest) * cell_step
    decays = (jnp.arange(MODES, dtype=jnp.float32) + 0.5) * cell_step
    decays_both = jnp.concatenate([decays, decays])
    factor = jnp.exp(-decays_both)

    def sweep(carried, cycle_row):
        carried = cycle_row + factor * carried
        return (carried, carried)
    start = jnp.zeros_like(spectra[0])
    _, lower_sum = lax.scan(sweep, start, spectra)
    _, upper_sum = lax.scan(sweep, start, spectra[::-1])
    upper_sum = upper_sum[::-1]
    even_part = decays_both * (lower_sum + upper_sum - spectra)
    odd_part = decays_both * (lower_sum - upper_sum)
    orders = jnp.arange(MODES, dtype=jnp.float32)
    doubled = jnp.where(orders > 0, 2.0, 1.0)
    radial_weight = jnp.concatenate([doubled * decays, doubled * decays])
    azim_weight = jnp.concatenate([doubled * orders, -doubled * orders])
    radial_coef = odd_part * radial_weight
    azim_coef = jnp.concatenate([even_part[:, MODES:], even_part[:, :MODES]], axis=1) * azim_weight
    radius = cycle_radius(0, cycle_total, cell_step)
    radial_disk = -(gravity / cell_step) / radius[:, None] * jnp.dot(radial_coef, tables, precision=highest)
    azimuthal_disk_pull = gravity / radius[:, None] * jnp.dot(azim_coef, tables, precision=highest)
    cell_angles = column_angles(0, ANGULAR_BINS)
    cos_cell = jnp.cos(cell_angles)[None, :]
    sin_cell = jnp.sin(cell_angles)[None, :]
    embryo_angles = (2 * planetesimal_angle_bin + 1).astype(jnp.float32) * (jnp.pi / ANGULAR_BINS)
    embryo_radii = jnp.exp((planetesimal_loop_number.astype(jnp.float32) + 0.5) * cell_step)
    column_radius = radius[:, None]
    area = (radius * radius * cell_step * cell_step)[:, None]

    def visit(carried, member):
        embryo_radius, embryo_cos, embryo_sin, embryo_weight = member
        cos_gap = cos_cell * embryo_cos + sin_cell * embryo_sin
        sin_gap = sin_cell * embryo_cos - cos_cell * embryo_sin
        squared = column_radius * column_radius + embryo_radius * embryo_radius - 2.0 * column_radius * embryo_radius * cos_gap + softening * embryo_radius * (softening * embryo_radius)
        inverse = lax.rsqrt(squared)
        cubed = inverse * inverse * inverse
        pulled = embryo_weight * cubed
        radial_sum = carried[0] - pulled * (column_radius - embryo_radius * cos_gap)
        azim_sum = carried[1] - pulled * embryo_radius * sin_gap
        weighted = transported_density * area * cubed
        push_x = jnp.sum(weighted * (column_radius * cos_cell - embryo_radius * embryo_cos))
        push_y = jnp.sum(weighted * (column_radius * sin_cell - embryo_radius * embryo_sin))
        return ((radial_sum, azim_sum), jnp.stack([push_x, push_y]))
    initial = (jnp.zeros_like(transported_density), jnp.zeros_like(transported_density))
    members = (embryo_radii, jnp.cos(embryo_angles), jnp.sin(embryo_angles), planetesimal_weights)
    (radial_emb, azimuthal_embryo_pull), gravity_pushes = lax.scan(visit, initial, members)
    kicked_radial_velocity = single_radial_velocity + timestep_length * (radial_disk + radial_emb)
    kicked_azimuthal_velocity = lone_angular_drift + timestep_length * (azimuthal_disk_pull + azimuthal_embryo_pull)
    return (transported_density, kicked_radial_velocity, kicked_azimuthal_velocity, jnp.transpose(gravity_pushes))
```

```python
import functools

import jax
import jax.numpy as jnp
import ml_dtypes
import numpy as np
from jax import lax
from jax.experimental import pallas as pl
from jax.experimental.pallas import tpu as pltpu
from jax.sharding import Mesh
from jax.sharding import PartitionSpec as P

ANGULAR_BINS = 16384
MODES = 256
EMB = 32
RAD = ("rad_0", "rad_1", "rad_2")
AZ = ("az_0", "az_1")
F32 = jnp.float32
BF16 = jnp.bfloat16

gravity = 1.0
timestep_length = 0.05
courant = 0.4
softening = 0.02
cell_step = 2.0 * np.pi / ANGULAR_BINS

ROWS = 32
CHUNKS = 32
GROUPS = 4
SPAN = 8 * CHUNKS
RING = 8 * (5 * CHUNKS + 8)
WIDE = 256
BLOCKS = 16


def split_bf16(table):
    high = table.astype(np.float32).astype(ml_dtypes.bfloat16)
    low = (table - high.astype(np.float64)).astype(np.float32).astype(ml_dtypes.bfloat16)
    return high, low


def constant_tables():
    orders = np.arange(MODES)
    inner = np.arange(WIDE)
    phases = orders[None, :] * (2 * inner[:, None] + 1) % (2 * ANGULAR_BINS) * (np.pi / ANGULAR_BINS)
    basis = np.concatenate([np.cos(phases), np.sin(phases)], axis=1)
    starts = np.arange(ANGULAR_BINS // WIDE) * WIDE
    turns = orders[None, :] * starts[:, None] % ANGULAR_BINS * (2 * np.pi / ANGULAR_BINS)
    twiddle = np.concatenate([np.cos(turns), np.sin(turns)], axis=1).astype(np.float32)
    halves = (2 * np.arange(ANGULAR_BINS) + 1) * (0.5 * np.pi / ANGULAR_BINS)
    wholes = 2 * halves
    angles = np.stack([np.cos(halves), np.sin(halves), np.cos(wholes), np.sin(wholes)])
    angles = angles.reshape(4, 4, CHUNKS, 128).transpose(1, 0, 2, 3).reshape(16, CHUNKS, 128)
    decays = np.tile((orders + 0.5) * cell_step, 2)
    rows = np.arange(ROWS)
    lift = np.exp(-decays[None, :] * (rows[:, None] + 1))
    drop = np.exp(-decays[None, :] * (ROWS - rows[:, None]))
    doubled = np.tile(np.where(orders > 0, 2.0, 1.0), 2)
    radial = -(gravity / cell_step) * doubled * decays * decays
    azim = gravity * np.concatenate([orders * doubled[:MODES], -orders * doubled[:MODES]])
    azim = azim * decays
    vectors = np.zeros((8, 2 * MODES))
    vectors[0] = np.exp(-decays)
    vectors[1] = radial
    vectors[2] = azim
    return (
        split_bf16(basis),
        split_bf16(basis.T),
        twiddle,
        angles.astype(np.float32),
        lift.astype(np.float32),
        drop.astype(np.float32),
        vectors.astype(np.float32),
        decays,
    )


def to_tiles(value):
    return value.reshape(GROUPS, 8, CHUNKS, 128).transpose(0, 2, 1, 3).reshape(GROUPS, SPAN, 128)


def from_tiles(value):
    return value.reshape(GROUPS, CHUNKS, 8, 128).transpose(0, 2, 1, 3).reshape(ROWS, CHUNKS * 128)


def vmem():
    return pl.BlockSpec(memory_space=pltpu.VMEM)


def smem():
    return pl.BlockSpec(memory_space=pltpu.SMEM)


def anywhere():
    return pl.BlockSpec(memory_space=pl.ANY)


def params():
    return pltpu.CompilerParams(vmem_limit_bytes=40 * 1024 * 1024)


def cost(us):
    return pl.CostEstimate(flops=int(us * 1e6), bytes_accessed=int(us * 2.5e6), transcendentals=0)


def donor_flux(speeds, upstream, downstream):
    return jnp.where(speeds > 0, speeds * upstream, speeds * downstream)


def azimuth_kernel(dens_ref, phi_ref, vrad_ref, left_ref, right_ref, offs_ref, out_ref, up_ref, down_ref):
    lane = lax.broadcasted_iota(jnp.int32, (1, 8, 128), 2)

    def following(value):
        turned = pltpu.roll(value, 127, 2)
        return jnp.where(lane == 127, turned[1:], turned[:-1])

    def widened(ref, group, base):
        rows = slice(base + 8 * group, base + 8 * group + 8)
        middle = ref[group].reshape(CHUNKS, 8, 128)
        return jnp.concatenate([left_ref[rows, :][None], middle, right_ref[rows, :][None]], axis=0)

    for group in range(GROUPS):
        dens = widened(dens_ref, group, 0)
        phi = widened(phi_ref, group, ROWS)
        speeds = 0.5 * (phi[:-1] + following(phi))
        flux = donor_flux(speeds, dens[:-1], following(dens))
        turned = pltpu.roll(flux, 1, 2)
        before = jnp.where(lane == 0, turned[:-1], turned[1:])
        stepped = dens[1:-1] - courant * (flux[1:] - before)
        out_ref[group] = stepped.reshape(SPAN, 128)
    up_ref[0:32, :] = out_ref[3, pl.ds(7, CHUNKS, stride=8), :]
    up_ref[32:64, :] = vrad_ref[3, pl.ds(7, CHUNKS, stride=8), :]
    up_ref[64:72, :] = jnp.full((8, 128), offs_ref[31].astype(F32), F32)
    down_ref[0:32, :] = out_ref[0, pl.ds(0, CHUNKS, stride=8), :]
    down_ref[32:64, :] = vrad_ref[0, pl.ds(0, CHUNKS, stride=8), :]
    down_ref[64:72, :] = jnp.full((8, 128), offs_ref[0].astype(F32), F32)


def fill_ring(own_ref, mate_ref, cross_ref, far_ref, ring_ref, sems, unit):
    odd = lax.axis_index(AZ) % 2
    places = ((own_ref, 0), (own_ref, 4), (cross_ref, 2), (mate_ref, 1 + 2 * odd), (far_ref, 3 - 2 * odd))
    copies = []
    for index, (source, place) in enumerate(places):
        where = pl.ds(pl.multiple_of(place * unit, unit), unit)
        copies.append(pltpu.make_async_copy(source, ring_ref.at[:, where, :], sems.at[index]))
    for copy in copies:
        copy.start()
    return copies


def shift_row(ring_ref, group, step, row, offset):
    start = ANGULAR_BINS - offset
    chunk = start // 128
    turn = (128 - start % 128) % 128
    lane = lax.broadcasted_iota(jnp.int32, (CHUNKS, 128), 1)
    first = ring_ref[group, pl.ds(chunk * step + row, CHUNKS, stride=step), :]
    second = ring_ref[group, pl.ds((chunk + 1) * step + row, CHUNKS, stride=step), :]
    return jnp.where(
        lane < 128 - start % 128, pltpu.roll(first, turn, 1), pltpu.roll(second, turn, 1)
    )


def shift_kernel(offs_ref, own_ref, mate_ref, cross_ref, far_ref, out_ref, ring_ref, sems):
    for copy in fill_ring(own_ref, mate_ref, cross_ref, far_ref, ring_ref, sems, SPAN):
        copy.wait()

    @pl.loop(0, GROUPS)
    def _(group):
        for row in range(8):
            moved = shift_row(ring_ref, group, 8, row, offs_ref[group * 8 + row])
            out_ref[group, pl.ds(row, CHUNKS, stride=8), :] = moved


def shifted(offsets, own, mate, cross, far, name):
    return pl.pallas_call(
        shift_kernel,
        out_shape=jax.ShapeDtypeStruct((GROUPS, SPAN, 128), F32),
        in_specs=[smem(), anywhere(), anywhere(), anywhere(), anywhere()],
        out_specs=vmem(),
        scratch_shapes=[pltpu.VMEM((GROUPS, RING, 128), F32), pltpu.SemaphoreType.DMA((5,))],
        compiler_params=params(),
        cost_estimate=cost(2),
        name=name,
    )(offsets, own, mate, cross, far)


def split_value(value):
    high = value.astype(BF16)
    return high, (value - high.astype(F32)).astype(BF16)


def dot(left, right):
    return jnp.dot(left, right, preferred_element_type=F32)


def transport_kernel(
    offs_ref, own_ref, mate_ref, cross_ref, far_ref,
    edge_own_ref, edge_mate_ref, edge_cross_ref, edge_far_ref,
    vrad_ref, high_ref, low_ref, twiddle_ref,
    dens_ref, spectra_ref,
    ring_ref, edge_ref, moved_ref, speed_ref, sems, edge_sems,
):
    copies = fill_ring(own_ref, mate_ref, cross_ref, far_ref, ring_ref, sems, SPAN)
    copies += fill_ring(
        edge_own_ref, edge_mate_ref, edge_cross_ref, edge_far_ref, edge_ref, edge_sems, CHUNKS
    )
    for copy in copies:
        copy.wait()

    @pl.loop(0, GROUPS)
    def _(group):
        for row in range(8):
            moved = shift_row(ring_ref, group, 8, row, offs_ref[group * 8 + row])
            moved_ref[group + 1, pl.ds(row, CHUNKS, stride=8), :] = moved

    for side, (place, row) in enumerate(((0, 7), (5, 0))):
        offset = offs_ref[ROWS + side]
        moved_ref[place, pl.ds(row, CHUNKS, stride=8), :] = shift_row(edge_ref, 2 * side, 1, 0, offset)
        speed_ref[side, pl.ds(row, CHUNKS, stride=8), :] = shift_row(edge_ref, 2 * side + 1, 1, 0, offset)

    sub = lax.broadcasted_iota(jnp.int32, (1, 8, 128), 1)
    own_index = lax.axis_index(RAD)
    bottom = own_index == 0
    top = own_index == lax.axis_size(RAD) - 1

    def above(value, following):
        return jnp.where(sub == 7, pltpu.roll(following, 7, 1), pltpu.roll(value, 7, 1))

    def below(value, previous):
        return jnp.where(sub == 0, pltpu.roll(previous, 1, 1), pltpu.roll(value, 1, 1))

    step = 4
    for group in range(GROUPS):

        @pl.loop(0, CHUNKS // step)
        def _(part):
            where = pl.ds(pl.multiple_of(part * 8 * step, 8 * step), 8 * step)

            def tiles(ref, index):
                return ref[index, where, :].reshape(step, 8, 128)

            dens = tiles(moved_ref, group + 1)
            dens_above = above(dens, tiles(moved_ref, group + 2))
            dens_below = below(dens, tiles(moved_ref, group))
            speed = tiles(vrad_ref, group)
            upper = tiles(vrad_ref, group + 1) if group < 3 else tiles(speed_ref, 1)
            lower = tiles(vrad_ref, group - 1) if group > 0 else tiles(speed_ref, 0)
            flux_above = donor_flux(0.5 * (speed + above(speed, upper)), dens, dens_above)
            flux_below = donor_flux(0.5 * (below(speed, lower) + speed), dens_below, dens)
            if group == 3:
                flux_above = jnp.where((sub == 7) & top, 0.0, flux_above)
            if group == 0:
                flux_below = jnp.where((sub == 0) & bottom, 0.0, flux_below)
            stepped = dens - courant * (flux_above - flux_below)
            dens_ref[group, where, :] = stepped.reshape(8 * step, 128)

    sector = lax.axis_index(AZ)
    cos_sum = jnp.zeros((ROWS, MODES), F32)
    sin_sum = jnp.zeros((ROWS, MODES), F32)
    together = 4
    for first in range(0, BLOCKS, together):
        pieces = []
        for block in range(first, first + together):
            halves = [
                dens_ref[:, 8 * chunk : 8 * chunk + 8, :].reshape(ROWS, 128)
                for chunk in (2 * block, 2 * block + 1)
            ]
            pieces.append(jnp.concatenate(halves, axis=1))
        high, low = split_value(jnp.concatenate(pieces, axis=0))
        part = dot(high, high_ref[...]) + (dot(low, high_ref[...]) + dot(high, low_ref[...]))
        for index in range(together):
            turn = twiddle_ref[pl.ds(sector * BLOCKS + first + index, 1), :]
            cosine, sine = turn[:, :MODES], turn[:, MODES:]
            rows = slice(index * ROWS, index * ROWS + ROWS)
            cos_part, sin_part = part[rows, :MODES], part[rows, MODES:]
            cos_sum += cosine * cos_part - sine * sin_part
            sin_sum += sine * cos_part + cosine * sin_part
    spectra_ref[:, :MODES] = cos_sum * cell_step
    spectra_ref[:, MODES:] = sin_sum * cell_step


def field_kernel(
    members_ref, radius_ref, angles_ref, radial_ref, azim_ref,
    gap_ref, pull_ref, chord_ref, lift_ref, side_ref,
):
    sector = lax.axis_index(AZ)
    half_cos = angles_ref[sector * 4]
    half_sin = angles_ref[sector * 4 + 1]
    radius = radius_ref[...]

    @pl.loop(0, EMB)
    def _(member):
        embryo_radius = members_ref[0, member]
        weight = members_ref[1, member]
        cosine = members_ref[2, member]
        sine = members_ref[3, member]
        gap = radius - embryo_radius
        soft = softening * embryo_radius
        rows = pl.ds(pl.multiple_of(member * 32, 32), 32)
        gap_ref[rows, :] = gap * gap + soft * soft
        pull_ref[rows, :] = weight * gap
        near = half_sin * cosine - half_cos * sine
        far = half_cos * cosine + half_sin * sine
        chord = (2.0 * embryo_radius) * (near * near)
        chord_ref[rows, :] = chord
        lift_ref[rows, :] = weight * chord
        side_ref[rows, :] = (2.0 * weight * embryo_radius) * (near * far)

    twice = [2.0 * radius[8 * g : 8 * g + 8] for g in range(GROUPS)]

    @pl.loop(0, CHUNKS)
    def _(chunk):
        zero = jnp.zeros((8, 128), F32)

        def visit(member, carried):
            radial, azim = list(carried[0]), list(carried[1])
            row = pl.ds(member * 32 + chunk, 1)
            chord = jnp.broadcast_to(chord_ref[row, :], (8, 128))
            lift = jnp.broadcast_to(lift_ref[row, :], (8, 128))
            side = jnp.broadcast_to(side_ref[row, :], (8, 128))
            for g in range(GROUPS):
                rows = pl.ds(pl.multiple_of(member * 32 + 8 * g, 8), 8)
                inverse = lax.rsqrt(gap_ref[rows, :] + twice[g] * chord)
                cubed = inverse * inverse * inverse
                radial[g] = radial[g] + cubed * (pull_ref[rows, :] + lift)
                azim[g] = azim[g] + cubed * side
            return tuple(radial), tuple(azim)

        radial, azim = lax.fori_loop(
            0, EMB, visit, ((zero,) * GROUPS, (zero,) * GROUPS), unroll=4
        )
        where = pl.ds(pl.multiple_of(chunk * 8, 8), 8)
        for g in range(GROUPS):
            radial_ref[g, where, :] = radial[g]
            azim_ref[g, where, :] = azim[g]


def push_kernel(
    members_ref, radius_ref, angles_ref, dens_ref, out_ref,
    mass_ref,
):
    sector = lax.axis_index(AZ)
    radius = radius_ref[...]
    pieces = [radius[8 * g : 8 * g + 8] for g in range(GROUPS)]
    twice = [2.0 * piece for piece in pieces]
    for g in range(GROUPS):
        area = pieces[g] * pieces[g] * (cell_step * cell_step)
        mass_ref[g] = (dens_ref[g].reshape(CHUNKS, 8, 128) * area[None]).reshape(SPAN, 128)
    half_cos = angles_ref[sector * 4]
    half_sin = angles_ref[sector * 4 + 1]

    def chunk_row(index, chunk):
        return jnp.broadcast_to(angles_ref[index, chunk : chunk + 1, :], (8, 128))

    @pl.loop(0, EMB)
    def _(member):
        embryo_radius = members_ref[0, member]
        cosine = members_ref[2, member]
        sine = members_ref[3, member]
        soft = softening * embryo_radius
        gaps = []
        for g in range(GROUPS):
            gap = pieces[g] - embryo_radius
            gaps.append(gap * gap + soft * soft)
        near = half_sin * cosine - half_cos * sine
        chords = (2.0 * embryo_radius) * (near * near)
        push_x = jnp.zeros((8, 128), F32)
        push_y = jnp.zeros((8, 128), F32)
        total = jnp.zeros((8, 128), F32)
        for chunk in range(CHUNKS):
            chord = jnp.broadcast_to(chords[chunk : chunk + 1, :], (8, 128))
            plain = jnp.zeros((8, 128), F32)
            moved = jnp.zeros((8, 128), F32)
            for g in range(GROUPS):
                inverse = lax.rsqrt(gaps[g] + twice[g] * chord)
                cubed = inverse * inverse * inverse
                term = cubed * mass_ref[g, 8 * chunk : 8 * chunk + 8, :]
                plain = plain + term
                moved = moved + pieces[g] * term
            push_x = push_x + moved * chunk_row(sector * 4 + 2, chunk)
            push_y = push_y + moved * chunk_row(sector * 4 + 3, chunk)
            total = total + plain
        place_x = embryo_radius * members_ref[4, member]
        place_y = embryo_radius * members_ref[5, member]
        out_ref[pl.ds(member, 1), :] = jnp.sum(push_x - place_x * total, axis=0, keepdims=True)
        out_ref[pl.ds(EMB + member, 1), :] = jnp.sum(push_y - place_y * total, axis=0, keepdims=True)


def moment_kernel(a_ref, b_ref, c_ref, d_ref, push_ref, lift_ref, drop_ref, vectors_ref, spectra_ref, packed_ref):
    spectra = (a_ref[...] + b_ref[...]) + (c_ref[...] + d_ref[...])
    spectra_ref[...] = spectra
    factor = vectors_ref[0:1, :]
    up = jnp.sum(spectra * drop_ref[...], axis=0, keepdims=True) / factor
    down = jnp.sum(spectra * lift_ref[...], axis=0, keepdims=True) / factor
    for part in range(4):
        packed_ref[part : part + 1, :] = up[:, 128 * part : 128 * part + 128]
        packed_ref[4 + part : 5 + part, :] = down[:, 128 * part : 128 * part + 128]
    packed_ref[8:72, :] = push_ref[...]


def kick_kernel(
    spectra_ref, terms_ref_0, terms_ref_1, terms_ref_2, terms_ref_3, terms_ref_4, terms_ref_5, terms_ref_6,
    weights_ref, radius_ref, vectors_ref, lift_ref, drop_ref, twiddle_ref, high_ref, low_ref,
    radial_ref, azim_ref, vrad_ref, vphi_ref,
    out_radial_ref, out_azim_ref,
    lower_ref, upper_ref,
):
    terms = (
        terms_ref_0, terms_ref_1, terms_ref_2, terms_ref_3, terms_ref_4, terms_ref_5, terms_ref_6,
    )
    outside = jnp.zeros((8, 128), F32)
    for index, term in enumerate(terms):
        outside += weights_ref[index] * term[0:8, :]
    lower = jnp.concatenate([outside[k : k + 1] for k in range(4)], axis=1)
    upper = jnp.concatenate([outside[k : k + 1] for k in range(4, 8)], axis=1)
    factor = vectors_ref[0:1, :]
    spectra = spectra_ref[...]
    for row in range(ROWS):
        lower = spectra[row : row + 1] + factor * lower
        lower_ref[row : row + 1, :] = lower
        back = ROWS - 1 - row
        upper = spectra[back : back + 1] + factor * upper
        upper_ref[back : back + 1, :] = upper
    lower = lower_ref[...]
    upper = upper_ref[...]
    inverse = 1.0 / radius_ref[:, 0:1]
    even = lower + upper - spectra
    odd = lower - upper
    radial = odd * vectors_ref[1:2, :] * inverse
    swapped = jnp.concatenate([even[:, MODES:], even[:, :MODES]], axis=1)
    azim = swapped * vectors_ref[2:3, :] * inverse
    sector = lax.axis_index(AZ)
    for block in range(BLOCKS):
        turn = twiddle_ref[pl.ds(sector * BLOCKS + block, 1), :]
        cosine, sine = turn[:, :MODES], turn[:, MODES:]
        pieces = []
        for coef in (radial, azim):
            cos_coef, sin_coef = coef[:, :MODES], coef[:, MODES:]
            pieces.append(
                jnp.concatenate(
                    [cos_coef * cosine + sin_coef * sine, sin_coef * cosine - cos_coef * sine], axis=1
                )
            )
        high, low = split_value(jnp.concatenate(pieces, axis=0))
        part = dot(high, high_ref[...]) + (dot(low, high_ref[...]) + dot(high, low_ref[...]))
        for half in range(2):
            where = slice(8 * (2 * block + half), 8 * (2 * block + half) + 8)
            columns = slice(128 * half, 128 * half + 128)
            disk = part[:ROWS, columns].reshape(GROUPS, 8, 128)
            out_radial_ref[:, where, :] = vrad_ref[:, where, :] + timestep_length * (
                disk - radial_ref[:, where, :]
            )
            disk = part[ROWS:, columns].reshape(GROUPS, 8, 128)
            out_azim_ref[:, where, :] = vphi_ref[:, where, :] + timestep_length * (
                disk - azim_ref[:, where, :]
            )


def across(value, axis, target):
    count = lax.axis_size(axis)
    return lax.ppermute(value, axis, [(source, target(source)) for source in range(count)])


def after(value, *others):
    return lax.optimization_barrier((value, *others))[0]


def stage_weights(decays):
    x, z, y = (lax.axis_index(name) for name in RAD)
    rate = jnp.asarray((decays * ROWS).astype(np.float32)).reshape(4, 128)
    ones = jnp.ones((64, 128), F32)

    def decayed(count):
        return jnp.where(count >= 0, jnp.exp(-rate * jnp.maximum(count, 0).astype(F32)), 0.0)

    joins, sides = [], []
    for shift in range(4):
        source = (y - shift) % 4
        joins.append(jnp.concatenate([decayed(3 - source), decayed(source), ones]))
        if shift:
            sides.append(jnp.concatenate([decayed(y - 1 - source), decayed(source - y - 1)]))
    pair = []
    for source in (z, 1 - z):
        pair.append(jnp.concatenate([decayed(4 * (1 - source)), decayed(4 * source), ones]))
    never = jnp.int32(-1)
    sides.append(
        jnp.concatenate(
            [decayed(jnp.where(z == 1, y, never)), decayed(jnp.where(z == 0, 3 - y, never))]
        )
    )
    for shift in range(1, 4):
        source = (x - shift) % 4
        gap = x - source
        within = 4 * z + y
        sides.append(
            jnp.concatenate(
                [
                    decayed(jnp.where(gap > 0, 8 * (gap - 1) + within, never)),
                    decayed(jnp.where(gap < 0, 8 * (-gap - 1) + 7 - within, never)),
                ]
            )
        )
    return jnp.stack(joins), jnp.stack(pair), jnp.stack(sides)


def on_device(
    surface_mass,
    outward_drift,
    leftover_angular_drift,
    angular_offsets,
    planetesimal_loop_number,
    planetesimal_angle_bin,
    planetesimal_weights,
):
    (basis_high, basis_low), (back_high, back_low), twiddle, angles, lift, drop, vectors, decays = (
        constant_tables()
    )
    tiles = jax.ShapeDtypeStruct((GROUPS, SPAN, 128), F32)
    dens = to_tiles(surface_mass)
    vrad = to_tiles(outward_drift)
    vphi = to_tiles(leftover_angular_drift)

    ends = jnp.concatenate([surface_mass[:, -128:], leftover_angular_drift[:, -128:]])
    begins = jnp.concatenate([surface_mass[:, :128], leftover_angular_drift[:, :128]])
    left = across(ends, AZ, lambda i: (i + 1) % 4)
    right = across(begins, AZ, lambda i: (i - 1) % 4)
    vrad_cross = across(vrad, AZ, lambda i: i ^ 2)
    vrad_mate = across(vrad, AZ, lambda i: i ^ 1)

    cell = np.float32(cell_step)
    cycles = lax.axis_index(RAD) * ROWS + jnp.arange(ROWS, dtype=jnp.int32)
    radius = jnp.broadcast_to(jnp.exp((cycles.astype(F32) + 0.5) * cell)[:, None], (ROWS, 128))
    embryo_angles = (2 * planetesimal_angle_bin + 1).astype(F32) * np.float32(np.pi / ANGULAR_BINS)
    members = jnp.stack(
        [
            jnp.exp((planetesimal_loop_number.astype(F32) + 0.5) * cell),
            planetesimal_weights,
            jnp.cos(0.5 * embryo_angles),
            jnp.sin(0.5 * embryo_angles),
            jnp.cos(embryo_angles),
            jnp.sin(embryo_angles),
        ]
    )
    joins, pair, sides = stage_weights(decays)

    dens_two, edge_up, edge_down = pl.pallas_call(
        azimuth_kernel,
        out_shape=(tiles, jax.ShapeDtypeStruct((72, 128), F32), jax.ShapeDtypeStruct((72, 128), F32)),
        in_specs=[vmem()] * 5 + [smem()],
        out_specs=(vmem(), vmem(), vmem()),
        compiler_params=params(),
        cost_estimate=cost(1),
        name="azimuth",
    )(dens, vphi, vrad, left, right, angular_offsets)

    rad_count = lax.axis_size(RAD)
    edge_low = lax.ppermute(edge_up, RAD, [(i, i + 1) for i in range(rad_count - 1)])
    edge_high = lax.ppermute(edge_down, RAD, [(i + 1, i) for i in range(rad_count - 1)])
    edges = jnp.concatenate([edge_low[:64], edge_high[:64]]).reshape(4, CHUNKS, 128)
    offsets = jnp.concatenate(
        [angular_offsets, edge_low[64:65, 0].astype(jnp.int32), edge_high[64:65, 0].astype(jnp.int32)]
    )
    edges_cross, edges_mate, edges_far = (
        across(edges, AZ, lambda i, k=k: i ^ k) for k in (2, 1, 3)
    )

    dens_mate = across(dens_two, AZ, lambda i: i ^ 1)
    dens_two_later = after(dens_two, vrad_cross)
    dens_cross = across(dens_two_later, AZ, lambda i: i ^ 2)
    vrad_far = across(vrad_cross, AZ, lambda i: i ^ 1)
    vrad_one = shifted(angular_offsets, vrad, vrad_mate, vrad_cross, vrad_far, "shift_vrad")

    radial_field, azim_field = pl.pallas_call(
        field_kernel,
        out_shape=(tiles, tiles),
        in_specs=[smem(), vmem(), vmem()],
        out_specs=(vmem(), vmem()),
        scratch_shapes=[pltpu.VMEM((EMB * 32, 128), F32)] * 5,
        compiler_params=params(),
        cost_estimate=cost(6),
        name="field",
    )(members, radius, angles)

    dens_far = across(dens_cross, AZ, lambda i: i ^ 1)
    vphi_later = after(vphi, dens_cross)
    vphi_cross = across(vphi_later, AZ, lambda i: i ^ 2)
    vphi_mate = across(vphi_later, AZ, lambda i: i ^ 1)

    transported, part = pl.pallas_call(
        transport_kernel,
        out_shape=(tiles, jax.ShapeDtypeStruct((ROWS, 2 * MODES), F32)),
        in_specs=[smem()] + [anywhere()] * 8 + [vmem()] * 4,
        out_specs=(vmem(), vmem()),
        scratch_shapes=[
            pltpu.VMEM((GROUPS, RING, 128), F32),
            pltpu.VMEM((4, RING // 8, 128), F32),
            pltpu.VMEM((GROUPS + 2, SPAN, 128), F32),
            pltpu.VMEM((2, SPAN, 128), F32),
            pltpu.SemaphoreType.DMA((5,)),
            pltpu.SemaphoreType.DMA((5,)),
        ],
        compiler_params=params(),
        cost_estimate=cost(3),
        name="transport",
    )(
        offsets, dens_two, dens_mate, dens_cross, dens_far,
        edges, edges_mate, edges_cross, edges_far,
        vrad_one, basis_high, basis_low, twiddle,
    )

    others = [across(part, AZ, lambda i, k=k: i ^ k) for k in (2, 3, 1)]
    push = pl.pallas_call(
        push_kernel,
        out_shape=jax.ShapeDtypeStruct((2 * EMB, 128), F32),
        in_specs=[smem(), vmem(), vmem(), vmem()],
        out_specs=vmem(),
        scratch_shapes=[pltpu.VMEM((GROUPS, SPAN, 128), F32)],
        compiler_params=params(),
        cost_estimate=cost(6),
        name="push",
    )(members, radius, angles, transported)

    packed_shape = jax.ShapeDtypeStruct((72, 128), F32)
    spectra, packed = pl.pallas_call(
        moment_kernel,
        out_shape=(jax.ShapeDtypeStruct((ROWS, 2 * MODES), F32), packed_shape),
        in_specs=[vmem()] * 8,
        out_specs=(vmem(), vmem()),
        compiler_params=params(),
        cost_estimate=cost(1),
        name="moments",
    )(part, *others, push, lift, drop, vectors)

    def from_shift(value, axis, shift):
        return across(value, axis, lambda i: (i + shift) % lax.axis_size(axis))

    near = [from_shift(packed, "rad_2", shift) for shift in (1, 2, 3)]
    four = joins[0] * packed + joins[1] * near[0] + joins[2] * near[1] + joins[3] * near[2]
    other = from_shift(four, "rad_1", 1)
    eight = pair[0] * four + pair[1] * other
    distant = [from_shift(eight, "rad_0", shift) for shift in (1, 2, 3)]
    push_part = eight[8:] + distant[0][8:] + distant[1][8:] + distant[2][8:]
    push_others = [across(push_part, AZ, lambda i, k=k: i ^ k) for k in (2, 3, 1)]

    vphi_far = across(vphi_cross, AZ, lambda i: i ^ 1)
    vphi_one = shifted(angular_offsets, vphi_later, vphi_mate, vphi_cross, vphi_far, "shift_vphi")

    kicked_radial, kicked_azim = pl.pallas_call(
        kick_kernel,
        out_shape=(tiles, tiles),
        in_specs=[vmem()] * 20,
        out_specs=(vmem(), vmem()),
        scratch_shapes=[pltpu.VMEM((ROWS, 2 * MODES), F32)] * 2,
        compiler_params=params(),
        cost_estimate=cost(5),
        name="kick",
    )(
        spectra, *near, other, *distant,
        sides, radius, vectors, lift, drop, twiddle, back_high, back_low,
        radial_field, azim_field, vrad_one, vphi_one,
    )

    push_sum = (push_part + push_others[0]) + (push_others[1] + push_others[2])
    embryo_disk_acceleration = jnp.sum(push_sum, axis=1).reshape(2, EMB)
    return (
        from_tiles(transported),
        from_tiles(kicked_radial),
        from_tiles(kicked_azim),
        embryo_disk_acceleration,
    )


def solution(mesh):
    torus = Mesh(mesh.devices.reshape(4, 2, 4, 2, 2), RAD + AZ)
    placed = (P(RAD, AZ), P(RAD, AZ), P(RAD, AZ), P(RAD), P(), P(), P())
    return jax.shard_map(
        on_device,
        mesh=torus,
        in_specs=placed,
        out_specs=(P(RAD, AZ), P(RAD, AZ), P(RAD, AZ), P()),
        check_vma=False,
    )
```

```python
import functools

import jax
import jax.numpy as jnp
import ml_dtypes
import numpy as np
from jax import lax
from jax.experimental import pallas as pl
from jax.experimental.pallas import tpu as pltpu
from jax.sharding import Mesh
from jax.sharding import PartitionSpec as P

ANGULAR_BINS = 16384
MODES = 256
EMB = 32
RAD = ("rad_0", "rad_1", "rad_2")
AZ = ("az_0", "az_1")
F32 = jnp.float32
BF16 = jnp.bfloat16

gravity = 1.0
timestep_length = 0.05
courant = 0.4
softening = 0.02
cell_step = 2.0 * np.pi / ANGULAR_BINS

ROWS = 32
CHUNKS = 32
GROUPS = 4
SPAN = 8 * CHUNKS
RING = 8 * (5 * CHUNKS + 8)
WIDE = 256
BLOCKS = 16


def split_bf16(table):
    high = table.astype(np.float32).astype(ml_dtypes.bfloat16)
    low = (table - high.astype(np.float64)).astype(np.float32).astype(ml_dtypes.bfloat16)
    return high, low


def constant_tables():
    orders = np.arange(MODES)
    inner = np.arange(WIDE)
    phases = orders[None, :] * (2 * inner[:, None] + 1) % (2 * ANGULAR_BINS) * (np.pi / ANGULAR_BINS)
    basis = np.concatenate([np.cos(phases), np.sin(phases)], axis=1)
    starts = np.arange(ANGULAR_BINS // WIDE) * WIDE
    turns = orders[None, :] * starts[:, None] % ANGULAR_BINS * (2 * np.pi / ANGULAR_BINS)
    twiddle = np.concatenate([np.cos(turns), np.sin(turns)], axis=1).astype(np.float32)
    halves = (2 * np.arange(ANGULAR_BINS) + 1) * (0.5 * np.pi / ANGULAR_BINS)
    wholes = 2 * halves
    angles = np.stack([np.cos(halves), np.sin(halves), np.cos(wholes), np.sin(wholes)])
    angles = angles.reshape(4, 4, CHUNKS, 128).transpose(1, 0, 2, 3).reshape(16, CHUNKS, 128)
    decays = np.tile((orders + 0.5) * cell_step, 2)
    rows = np.arange(ROWS)
    lift = np.exp(-decays[None, :] * (rows[:, None] + 1))
    drop = np.exp(-decays[None, :] * (ROWS - rows[:, None]))
    doubled = np.tile(np.where(orders > 0, 2.0, 1.0), 2)
    radial = -(gravity / cell_step) * doubled * decays * decays
    azim = gravity * np.concatenate([orders * doubled[:MODES], -orders * doubled[:MODES]])
    azim = azim * decays
    vectors = np.zeros((8, 2 * MODES))
    vectors[0] = np.exp(-decays)
    vectors[1] = radial
    vectors[2] = azim
    return (
        split_bf16(basis),
        split_bf16(basis.T),
        twiddle,
        angles.astype(np.float32),
        lift.astype(np.float32),
        drop.astype(np.float32),
        vectors.astype(np.float32),
        np.tile((decays * ROWS).astype(np.float32).reshape(4, 128), (2, 1)),
    )


def to_tiles(value):
    return value.reshape(GROUPS, 8, CHUNKS, 128).transpose(0, 2, 1, 3).reshape(GROUPS, SPAN, 128)


def from_tiles(value):
    return value.reshape(GROUPS, CHUNKS, 8, 128).transpose(0, 2, 1, 3).reshape(ROWS, CHUNKS * 128)


def vmem():
    return pl.BlockSpec(memory_space=pltpu.VMEM)


def smem():
    return pl.BlockSpec(memory_space=pltpu.SMEM)


def anywhere():
    return pl.BlockSpec(memory_space=pl.ANY)


def params():
    return pltpu.CompilerParams(vmem_limit_bytes=40 * 1024 * 1024)


def cost(us):
    return pl.CostEstimate(flops=int(us * 1e6), bytes_accessed=int(us * 2.5e6), transcendentals=0)


def donor_flux(speeds, upstream, downstream):
    return jnp.where(speeds > 0, speeds * upstream, speeds * downstream)


def azimuth_kernel(dens_ref, phi_ref, vrad_ref, left_ref, right_ref, offs_ref, out_ref, up_ref, down_ref):
    lane = lax.broadcasted_iota(jnp.int32, (1, 8, 128), 2)

    def following(value):
        turned = pltpu.roll(value, 127, 2)
        return jnp.where(lane == 127, turned[1:], turned[:-1])

    def widened(ref, group, base):
        rows = slice(base + 8 * group, base + 8 * group + 8)
        middle = ref[group].reshape(CHUNKS, 8, 128)
        return jnp.concatenate([left_ref[rows, :][None], middle, right_ref[rows, :][None]], axis=0)

    for group in range(GROUPS):
        dens = widened(dens_ref, group, 0)
        phi = widened(phi_ref, group, ROWS)
        speeds = 0.5 * (phi[:-1] + following(phi))
        flux = donor_flux(speeds, dens[:-1], following(dens))
        turned = pltpu.roll(flux, 1, 2)
        before = jnp.where(lane == 0, turned[:-1], turned[1:])
        stepped = dens[1:-1] - courant * (flux[1:] - before)
        out_ref[group] = stepped.reshape(SPAN, 128)
    up_ref[0:32, :] = out_ref[3, pl.ds(7, CHUNKS, stride=8), :]
    up_ref[32:64, :] = vrad_ref[3, pl.ds(7, CHUNKS, stride=8), :]
    up_ref[64:72, :] = jnp.full((8, 128), offs_ref[31].astype(F32), F32)
    down_ref[0:32, :] = out_ref[0, pl.ds(0, CHUNKS, stride=8), :]
    down_ref[32:64, :] = vrad_ref[0, pl.ds(0, CHUNKS, stride=8), :]
    down_ref[64:72, :] = jnp.full((8, 128), offs_ref[0].astype(F32), F32)


def fill_ring(own_ref, mate_ref, cross_ref, far_ref, ring_ref, sems, unit):
    odd = lax.axis_index(AZ) % 2
    places = ((own_ref, 0), (own_ref, 4), (cross_ref, 2), (mate_ref, 1 + 2 * odd), (far_ref, 3 - 2 * odd))
    copies = []
    for index, (source, place) in enumerate(places):
        where = pl.ds(pl.multiple_of(place * unit, unit), unit)
        copies.append(pltpu.make_async_copy(source, ring_ref.at[:, where, :], sems.at[index]))
    for copy in copies:
        copy.start()
    return copies


def shift_row(ring_ref, group, step, row, offset):
    start = ANGULAR_BINS - offset
    chunk = start // 128
    turn = (128 - start % 128) % 128
    lane = lax.broadcasted_iota(jnp.int32, (CHUNKS, 128), 1)
    first = ring_ref[group, pl.ds(chunk * step + row, CHUNKS, stride=step), :]
    second = ring_ref[group, pl.ds((chunk + 1) * step + row, CHUNKS, stride=step), :]
    return jnp.where(
        lane < 128 - start % 128, pltpu.roll(first, turn, 1), pltpu.roll(second, turn, 1)
    )


def shift_kernel(offs_ref, own_ref, mate_ref, cross_ref, far_ref, out_ref, ring_ref, sems):
    for copy in fill_ring(own_ref, mate_ref, cross_ref, far_ref, ring_ref, sems, SPAN):
        copy.wait()

    @pl.loop(0, GROUPS)
    def _(group):
        for row in range(8):
            moved = shift_row(ring_ref, group, 8, row, offs_ref[group * 8 + row])
            out_ref[group, pl.ds(row, CHUNKS, stride=8), :] = moved


def shifted(offsets, own, mate, cross, far, name):
    return pl.pallas_call(
        shift_kernel,
        out_shape=jax.ShapeDtypeStruct((GROUPS, SPAN, 128), F32),
        in_specs=[smem(), anywhere(), anywhere(), anywhere(), anywhere()],
        out_specs=vmem(),
        scratch_shapes=[pltpu.VMEM((GROUPS, RING, 128), F32), pltpu.SemaphoreType.DMA((5,))],
        compiler_params=params(),
        cost_estimate=cost(2),
        name=name,
    )(offsets, own, mate, cross, far)


def split_value(value):
    high = value.astype(BF16)
    return high, (value - high.astype(F32)).astype(BF16)


def dot(left, right):
    return jnp.dot(left, right, preferred_element_type=F32)


def transport_kernel(
    offs_ref, own_ref, mate_ref, cross_ref, far_ref,
    edge_own_ref, edge_mate_ref, edge_cross_ref, edge_far_ref,
    vrad_ref, high_ref, low_ref, twiddle_ref,
    dens_ref, spectra_ref,
    ring_ref, edge_ref, moved_ref, speed_ref, sems, edge_sems,
):
    copies = fill_ring(own_ref, mate_ref, cross_ref, far_ref, ring_ref, sems, SPAN)
    copies += fill_ring(
        edge_own_ref, edge_mate_ref, edge_cross_ref, edge_far_ref, edge_ref, edge_sems, CHUNKS
    )
    for copy in copies:
        copy.wait()

    @pl.loop(0, GROUPS)
    def _(group):
        for row in range(8):
            moved = shift_row(ring_ref, group, 8, row, offs_ref[group * 8 + row])
            moved_ref[group + 1, pl.ds(row, CHUNKS, stride=8), :] = moved

    for side, (place, row) in enumerate(((0, 7), (5, 0))):
        offset = offs_ref[ROWS + side]
        moved_ref[place, pl.ds(row, CHUNKS, stride=8), :] = shift_row(edge_ref, 2 * side, 1, 0, offset)
        speed_ref[side, pl.ds(row, CHUNKS, stride=8), :] = shift_row(edge_ref, 2 * side + 1, 1, 0, offset)

    sub = lax.broadcasted_iota(jnp.int32, (1, 8, 128), 1)
    own_index = lax.axis_index(RAD)
    bottom = own_index == 0
    top = own_index == lax.axis_size(RAD) - 1

    def above(value, following):
        return jnp.where(sub == 7, pltpu.roll(following, 7, 1), pltpu.roll(value, 7, 1))

    def below(value, previous):
        return jnp.where(sub == 0, pltpu.roll(previous, 1, 1), pltpu.roll(value, 1, 1))

    step = 4
    for group in range(GROUPS):

        @pl.loop(0, CHUNKS // step)
        def _(part):
            where = pl.ds(pl.multiple_of(part * 8 * step, 8 * step), 8 * step)

            def tiles(ref, index):
                return ref[index, where, :].reshape(step, 8, 128)

            dens = tiles(moved_ref, group + 1)
            dens_above = above(dens, tiles(moved_ref, group + 2))
            dens_below = below(dens, tiles(moved_ref, group))
            speed = tiles(vrad_ref, group)
            upper = tiles(vrad_ref, group + 1) if group < 3 else tiles(speed_ref, 1)
            lower = tiles(vrad_ref, group - 1) if group > 0 else tiles(speed_ref, 0)
            flux_above = donor_flux(0.5 * (speed + above(speed, upper)), dens, dens_above)
            flux_below = donor_flux(0.5 * (below(speed, lower) + speed), dens_below, dens)
            if group == 3:
                flux_above = jnp.where((sub == 7) & top, 0.0, flux_above)
            if group == 0:
                flux_below = jnp.where((sub == 0) & bottom, 0.0, flux_below)
            stepped = dens - courant * (flux_above - flux_below)
            dens_ref[group, where, :] = stepped.reshape(8 * step, 128)

    sector = lax.axis_index(AZ)
    cos_sum = jnp.zeros((ROWS, MODES), F32)
    sin_sum = jnp.zeros((ROWS, MODES), F32)
    together = 4
    for first in range(0, BLOCKS, together):
        pieces = []
        for block in range(first, first + together):
            halves = [
                dens_ref[:, 8 * chunk : 8 * chunk + 8, :].reshape(ROWS, 128)
                for chunk in (2 * block, 2 * block + 1)
            ]
            pieces.append(jnp.concatenate(halves, axis=1))
        high, low = split_value(jnp.concatenate(pieces, axis=0))
        part = dot(high, high_ref[...]) + (dot(low, high_ref[...]) + dot(high, low_ref[...]))
        for index in range(together):
            turn = twiddle_ref[pl.ds(sector * BLOCKS + first + index, 1), :]
            cosine, sine = turn[:, :MODES], turn[:, MODES:]
            rows = slice(index * ROWS, index * ROWS + ROWS)
            cos_part, sin_part = part[rows, :MODES], part[rows, MODES:]
            cos_sum += cosine * cos_part - sine * sin_part
            sin_sum += sine * cos_part + cosine * sin_part
    spectra_ref[:, :MODES] = cos_sum * cell_step
    spectra_ref[:, MODES:] = sin_sum * cell_step


def field_kernel(
    members_ref, radius_ref, angles_ref, radial_ref, azim_ref,
    gap_ref, pull_ref, chord_ref, lift_ref, side_ref,
):
    sector = lax.axis_index(AZ)
    half_cos = angles_ref[sector * 4]
    half_sin = angles_ref[sector * 4 + 1]
    radius = radius_ref[...]

    @pl.loop(0, EMB)
    def _(member):
        embryo_radius = members_ref[0, member]
        weight = members_ref[1, member]
        cosine = members_ref[2, member]
        sine = members_ref[3, member]
        gap = radius - embryo_radius
        soft = softening * embryo_radius
        rows = pl.ds(pl.multiple_of(member * 32, 32), 32)
        gap_ref[rows, :] = gap * gap + soft * soft
        pull_ref[rows, :] = weight * gap
        near = half_sin * cosine - half_cos * sine
        far = half_cos * cosine + half_sin * sine
        chord = (2.0 * embryo_radius) * (near * near)
        chord_ref[rows, :] = chord
        lift_ref[rows, :] = weight * chord
        side_ref[rows, :] = (2.0 * weight * embryo_radius) * (near * far)

    twice = [2.0 * radius[8 * g : 8 * g + 8] for g in range(GROUPS)]

    @pl.loop(0, CHUNKS)
    def _(chunk):
        zero = jnp.zeros((8, 128), F32)

        def visit(member, carried):
            radial, azim = list(carried[0]), list(carried[1])
            row = pl.ds(member * 32 + chunk, 1)
            chord = jnp.broadcast_to(chord_ref[row, :], (8, 128))
            lift = jnp.broadcast_to(lift_ref[row, :], (8, 128))
            side = jnp.broadcast_to(side_ref[row, :], (8, 128))
            for g in range(GROUPS):
                rows = pl.ds(pl.multiple_of(member * 32 + 8 * g, 8), 8)
                inverse = lax.rsqrt(gap_ref[rows, :] + twice[g] * chord)
                cubed = inverse * inverse * inverse
                radial[g] = radial[g] + cubed * (pull_ref[rows, :] + lift)
                azim[g] = azim[g] + cubed * side
            return tuple(radial), tuple(azim)

        radial, azim = lax.fori_loop(
            0, EMB, visit, ((zero,) * GROUPS, (zero,) * GROUPS), unroll=4
        )
        where = pl.ds(pl.multiple_of(chunk * 8, 8), 8)
        for g in range(GROUPS):
            radial_ref[g, where, :] = radial[g]
            azim_ref[g, where, :] = azim[g]


def push_kernel(members_ref, radius_ref, angles_ref, dens_ref, out_ref, mass_ref, chord_ref):
    sector = lax.axis_index(AZ)
    radius = radius_ref[...]
    pieces = [radius[8 * g : 8 * g + 8] for g in range(GROUPS)]
    halves = [0.5 / piece for piece in pieces]
    for g in range(GROUPS):
        scale = lax.rsqrt(2.0 * pieces[g])
        area = pieces[g] * pieces[g] * (cell_step * cell_step) * (scale * scale * scale)
        mass_ref[g] = (dens_ref[g].reshape(CHUNKS, 8, 128) * area[None]).reshape(SPAN, 128)
    half_cos = angles_ref[sector * 4]
    half_sin = angles_ref[sector * 4 + 1]

    @pl.loop(0, EMB)
    def _(member):
        embryo_radius = members_ref[0, member]
        cosine = members_ref[2, member]
        sine = members_ref[3, member]
        soft = softening * embryo_radius
        gaps = []
        for g in range(GROUPS):
            gap = pieces[g] - embryo_radius
            gaps.append((gap * gap + soft * soft) * halves[g])
        near = half_sin * cosine - half_cos * sine
        chord_ref[...] = (2.0 * embryo_radius) * (near * near)
        push_x = jnp.zeros((8, 128), F32)
        push_y = jnp.zeros((8, 128), F32)
        total = jnp.zeros((8, 128), F32)
        for chunk in range(CHUNKS):
            chord = jnp.broadcast_to(chord_ref[chunk : chunk + 1, :], (8, 128))
            plain, moved = None, None
            for g in range(GROUPS):
                inverse = lax.rsqrt(gaps[g] + chord)
                cubed = inverse * inverse * inverse
                term = cubed * mass_ref[g, 8 * chunk : 8 * chunk + 8, :]
                plain = term if g == 0 else plain + term
                moved = pieces[g] * term if g == 0 else moved + pieces[g] * term
            row = slice(chunk, chunk + 1)
            push_x = push_x + moved * jnp.broadcast_to(angles_ref[sector * 4 + 2, row, :], (8, 128))
            push_y = push_y + moved * jnp.broadcast_to(angles_ref[sector * 4 + 3, row, :], (8, 128))
            total = total + plain
        place_x = embryo_radius * members_ref[4, member]
        place_y = embryo_radius * members_ref[5, member]
        out_ref[pl.ds(member, 1), :] = jnp.sum(push_x - place_x * total, axis=0, keepdims=True)
        out_ref[pl.ds(EMB + member, 1), :] = jnp.sum(push_y - place_y * total, axis=0, keepdims=True)


def moment_kernel(
    a_ref, b_ref, c_ref, d_ref, push_a_ref, push_b_ref, push_c_ref, push_d_ref,
    lift_ref, drop_ref, vectors_ref, spectra_ref, packed_ref,
):
    spectra = (a_ref[...] + b_ref[...]) + (c_ref[...] + d_ref[...])
    spectra_ref[...] = spectra
    factor = vectors_ref[0:1, :]
    up = jnp.sum(spectra * drop_ref[...], axis=0, keepdims=True) / factor
    down = jnp.sum(spectra * lift_ref[...], axis=0, keepdims=True) / factor
    for part in range(4):
        packed_ref[part : part + 1, :] = up[:, 128 * part : 128 * part + 128]
        packed_ref[4 + part : 5 + part, :] = down[:, 128 * part : 128 * part + 128]
    push = (push_a_ref[...] + push_b_ref[...]) + (push_c_ref[...] + push_d_ref[...])
    push = jnp.broadcast_to(jnp.sum(push, axis=1, keepdims=True), (2 * EMB, 128))
    row = lax.broadcasted_iota(jnp.int32, (2 * EMB, 128), 0)
    lane = lax.broadcasted_iota(jnp.int32, (2 * EMB, 128), 1)
    push = jnp.sum(jnp.where(row == lane, push, 0.0), axis=0, keepdims=True)
    packed_ref[8:16, :] = jnp.broadcast_to(push, (8, 128))


def kick_kernel(
    spectra_ref, near_1_ref, near_2_ref, near_3_ref, other_ref, distant_1_ref, distant_2_ref, distant_3_ref,
    eight_ref, rate_ref, radius_ref, vectors_ref, lift_ref, drop_ref, twiddle_ref, high_ref, low_ref,
    radial_ref, azim_ref, vrad_ref, vphi_ref,
    out_radial_ref, out_azim_ref, out_push_ref,
    lower_ref, upper_ref,
):
    x, z, y = (lax.axis_index(name) for name in RAD)
    counts = []
    for shift in range(1, 4):
        source = (y - shift) % 4
        counts.append((y - 1 - source, source - y - 1))
    counts.append((jnp.where(z == 1, y, -1), jnp.where(z == 0, 3 - y, -1)))
    for shift in range(1, 4):
        gap = x - (x - shift) % 4
        within = 4 * z + y
        counts.append(
            (
                jnp.where(gap > 0, 8 * (gap - 1) + within, -1),
                jnp.where(gap < 0, 8 * (-gap - 1) + 7 - within, -1),
            )
        )
    distant = (distant_1_ref, distant_2_ref, distant_3_ref)
    row = lax.broadcasted_iota(jnp.int32, (8, 128), 0)
    outside = jnp.zeros((8, 128), F32)
    for count, term in zip(counts, (near_1_ref, near_2_ref, near_3_ref, other_ref) + distant):
        many = jnp.where(row < 4, count[0], count[1])
        weight = jnp.exp(-rate_ref[...] * jnp.maximum(many, 0).astype(F32))
        outside += jnp.where(many >= 0, weight, 0.0) * term[0:8, :]
    push = (eight_ref[8:9, :] + distant[1][8:9, :]) + (distant[0][8:9, :] + distant[2][8:9, :])
    out_push_ref[0:1, :] = push[:, :EMB]
    out_push_ref[1:2, :] = push[:, EMB : 2 * EMB]
    lower = jnp.concatenate([outside[k : k + 1] for k in range(4)], axis=1)
    upper = jnp.concatenate([outside[k : k + 1] for k in range(4, 8)], axis=1)
    factor = vectors_ref[0:1, :]
    spectra = spectra_ref[...]
    for row in range(ROWS):
        lower = spectra[row : row + 1] + factor * lower
        lower_ref[row : row + 1, :] = lower
        back = ROWS - 1 - row
        upper = spectra[back : back + 1] + factor * upper
        upper_ref[back : back + 1, :] = upper
    lower = lower_ref[...]
    upper = upper_ref[...]
    inverse = 1.0 / radius_ref[:, 0:1]
    even = lower + upper - spectra
    odd = lower - upper
    radial = odd * vectors_ref[1:2, :] * inverse
    swapped = jnp.concatenate([even[:, MODES:], even[:, :MODES]], axis=1)
    azim = swapped * vectors_ref[2:3, :] * inverse
    sector = lax.axis_index(AZ)
    for block in range(BLOCKS):
        turn = twiddle_ref[pl.ds(sector * BLOCKS + block, 1), :]
        cosine, sine = turn[:, :MODES], turn[:, MODES:]
        pieces = []
        for coef in (radial, azim):
            cos_coef, sin_coef = coef[:, :MODES], coef[:, MODES:]
            pieces.append(
                jnp.concatenate(
                    [cos_coef * cosine + sin_coef * sine, sin_coef * cosine - cos_coef * sine], axis=1
                )
            )
        high, low = split_value(jnp.concatenate(pieces, axis=0))
        part = dot(high, high_ref[...]) + (dot(low, high_ref[...]) + dot(high, low_ref[...]))
        for half in range(2):
            where = slice(8 * (2 * block + half), 8 * (2 * block + half) + 8)
            columns = slice(128 * half, 128 * half + 128)
            disk = part[:ROWS, columns].reshape(GROUPS, 8, 128)
            out_radial_ref[:, where, :] = vrad_ref[:, where, :] + timestep_length * (
                disk - radial_ref[:, where, :]
            )
            disk = part[ROWS:, columns].reshape(GROUPS, 8, 128)
            out_azim_ref[:, where, :] = vphi_ref[:, where, :] + timestep_length * (
                disk - azim_ref[:, where, :]
            )


def across(value, axis, target):
    count = lax.axis_size(axis)
    return lax.ppermute(value, axis, [(source, target(source)) for source in range(count)])


def after(value, *others):
    return lax.optimization_barrier((value, *others))[0]


def decayed(rate, up_count, down_count):
    count = jnp.stack([up_count] * 4 + [down_count] * 4 + [0] * 8).astype(F32)
    return jnp.exp(-rate * count[:, None])


def on_device(
    surface_mass,
    outward_drift,
    leftover_angular_drift,
    angular_offsets,
    planetesimal_loop_number,
    planetesimal_angle_bin,
    planetesimal_weights,
):
    (basis_high, basis_low), (back_high, back_low), twiddle, angles, lift, drop, vectors, rate = (
        constant_tables()
    )
    tiles = jax.ShapeDtypeStruct((GROUPS, SPAN, 128), F32)
    dens = to_tiles(surface_mass)
    vrad = to_tiles(outward_drift)
    vphi = to_tiles(leftover_angular_drift)

    ends = jnp.concatenate([surface_mass[:, -128:], leftover_angular_drift[:, -128:]])
    begins = jnp.concatenate([surface_mass[:, :128], leftover_angular_drift[:, :128]])
    left = across(ends, AZ, lambda i: (i + 1) % 4)
    right = across(begins, AZ, lambda i: (i - 1) % 4)
    vrad_cross = across(after(vrad, left, right), AZ, lambda i: i ^ 2)
    vrad_mate = across(vrad, AZ, lambda i: i ^ 1)

    cell = np.float32(cell_step)
    cycles = lax.axis_index(RAD) * ROWS + jnp.arange(ROWS, dtype=jnp.int32)
    radius = jnp.broadcast_to(jnp.exp((cycles.astype(F32) + 0.5) * cell)[:, None], (ROWS, 128))
    embryo_angles = (2 * planetesimal_angle_bin + 1).astype(F32) * np.float32(np.pi / ANGULAR_BINS)
    members = jnp.stack(
        [
            jnp.exp((planetesimal_loop_number.astype(F32) + 0.5) * cell),
            planetesimal_weights,
            jnp.cos(0.5 * embryo_angles),
            jnp.sin(0.5 * embryo_angles),
            jnp.cos(embryo_angles),
            jnp.sin(embryo_angles),
        ]
    )

    dens_two, edge_up, edge_down = pl.pallas_call(
        azimuth_kernel,
        out_shape=(tiles, jax.ShapeDtypeStruct((72, 128), F32), jax.ShapeDtypeStruct((72, 128), F32)),
        in_specs=[vmem()] * 5 + [smem()],
        out_specs=(vmem(), vmem(), vmem()),
        compiler_params=params(),
        cost_estimate=cost(1),
        name="azimuth",
    )(dens, vphi, vrad, left, right, angular_offsets)

    rad_count = lax.axis_size(RAD)
    edge_low = lax.ppermute(edge_up, RAD, [(i, i + 1) for i in range(rad_count - 1)])
    edge_high = lax.ppermute(edge_down, RAD, [(i + 1, i) for i in range(rad_count - 1)])
    edges = jnp.concatenate([edge_low[:64], edge_high[:64]]).reshape(4, CHUNKS, 128)
    offsets = jnp.concatenate(
        [angular_offsets, edge_low[64:65, 0].astype(jnp.int32), edge_high[64:65, 0].astype(jnp.int32)]
    )
    edges_cross, edges_mate, edges_far = (
        across(edges, AZ, lambda i, k=k: i ^ k) for k in (2, 1, 3)
    )

    dens_mate = across(dens_two, AZ, lambda i: i ^ 1)
    dens_two_later = after(dens_two, vrad_cross, edge_low, edge_high)
    dens_cross = across(dens_two_later, AZ, lambda i: i ^ 2)
    vrad_far = across(vrad_cross, AZ, lambda i: i ^ 1)
    vrad_one = shifted(angular_offsets, vrad, vrad_mate, vrad_cross, vrad_far, "shift_vrad")

    radial_field, azim_field = pl.pallas_call(
        field_kernel,
        out_shape=(tiles, tiles),
        in_specs=[smem(), vmem(), vmem()],
        out_specs=(vmem(), vmem()),
        scratch_shapes=[pltpu.VMEM((EMB * 32, 128), F32)] * 5,
        compiler_params=params(),
        cost_estimate=cost(6),
        name="field",
    )(members, radius, angles)

    dens_cross = after(
        dens_cross, edges_cross, edges_mate, edges_far, dens_mate, vrad_one, radial_field
    )
    dens_far = across(dens_cross, AZ, lambda i: i ^ 1)
    vphi_later = after(vphi, dens_cross)
    vphi_cross = across(vphi_later, AZ, lambda i: i ^ 2)
    vphi_mate = across(vphi_later, AZ, lambda i: i ^ 1)

    transported, part = pl.pallas_call(
        transport_kernel,
        out_shape=(tiles, jax.ShapeDtypeStruct((ROWS, 2 * MODES), F32)),
        in_specs=[smem()] + [anywhere()] * 8 + [vmem()] * 4,
        out_specs=(vmem(), vmem()),
        scratch_shapes=[
            pltpu.VMEM((GROUPS, RING, 128), F32),
            pltpu.VMEM((4, RING // 8, 128), F32),
            pltpu.VMEM((GROUPS + 2, SPAN, 128), F32),
            pltpu.VMEM((2, SPAN, 128), F32),
            pltpu.SemaphoreType.DMA((5,)),
            pltpu.SemaphoreType.DMA((5,)),
        ],
        compiler_params=params(),
        cost_estimate=cost(3),
        name="transport",
    )(
        offsets, dens_two, dens_mate, dens_cross, dens_far,
        edges, edges_mate, edges_cross, edges_far,
        vrad_one, basis_high, basis_low, twiddle,
    )

    push = pl.pallas_call(
        push_kernel,
        out_shape=jax.ShapeDtypeStruct((2 * EMB, 128), F32),
        in_specs=[smem(), vmem(), vmem(), vmem()],
        out_specs=vmem(),
        scratch_shapes=[pltpu.VMEM((GROUPS, SPAN, 128), F32), pltpu.VMEM((CHUNKS, 128), F32)],
        compiler_params=params(),
        cost_estimate=cost(6),
        name="push",
    )(members, radius, angles, transported)
    part_later, push_later = lax.optimization_barrier((part, push, vphi_cross))[:2]
    part_others = [across(part_later, AZ, lambda i, k=k: i ^ k) for k in (2, 3, 1)]
    push_others = [across(push_later, AZ, lambda i, k=k: i ^ k) for k in (2, 3, 1)]

    spectra, packed = pl.pallas_call(
        moment_kernel,
        out_shape=(
            jax.ShapeDtypeStruct((ROWS, 2 * MODES), F32),
            jax.ShapeDtypeStruct((16, 128), F32),
        ),
        in_specs=[vmem()] * 11,
        out_specs=(vmem(), vmem()),
        compiler_params=params(),
        cost_estimate=cost(1),
        name="moments",
    )(part, *part_others, push, *push_others, lift, drop, vectors)

    def from_shift(value, axis, shift):
        return across(value, axis, lambda i: (i + shift) % lax.axis_size(axis))

    _, z, y = (lax.axis_index(name) for name in RAD)
    rates = np.concatenate([rate, np.zeros((8, 128), np.float32)])
    near = [from_shift(packed, "rad_2", shift) for shift in (1, 2, 3)]
    parts = []
    for shift, piece in enumerate([packed] + near):
        source = (y - shift) % 4
        parts.append(decayed(rates, 3 - source, source) * piece)
    four = (parts[0] + parts[2]) + (parts[1] + parts[3])
    other = from_shift(four, "rad_1", 1)
    eight = decayed(rates, 4 * (1 - z), 4 * z) * four + decayed(rates, 4 * z, 4 * (1 - z)) * other
    distant = [from_shift(eight, "rad_0", shift) for shift in (1, 2, 3)]

    vphi_far = across(vphi_cross, AZ, lambda i: i ^ 1)
    vphi_one = shifted(angular_offsets, vphi_later, vphi_mate, vphi_cross, vphi_far, "shift_vphi")

    kicked_radial, kicked_azim, embryo_disk_acceleration = pl.pallas_call(
        kick_kernel,
        out_shape=(tiles, tiles, jax.ShapeDtypeStruct((2, EMB), F32)),
        in_specs=[vmem()] * 21,
        out_specs=(vmem(), vmem(), vmem()),
        scratch_shapes=[pltpu.VMEM((ROWS, 2 * MODES), F32)] * 2,
        compiler_params=params(),
        cost_estimate=cost(5),
        name="kick",
    )(
        spectra, *near, other, *distant, eight,
        rate, radius, vectors, lift, drop, twiddle, back_high, back_low,
        radial_field, azim_field, vrad_one, vphi_one,
    )
    return (
        from_tiles(transported),
        from_tiles(kicked_radial),
        from_tiles(kicked_azim),
        embryo_disk_acceleration,
    )


def solution(mesh):
    torus = Mesh(mesh.devices.reshape(4, 2, 4, 2, 2), RAD + AZ)
    placed = (P(RAD, AZ), P(RAD, AZ), P(RAD, AZ), P(RAD), P(), P(), P())
    return jax.shard_map(
        on_device,
        mesh=torus,
        in_specs=placed,
        out_specs=(P(RAD, AZ), P(RAD, AZ), P(RAD, AZ), P()),
        check_vma=False,
    )
```

```python
import functools

import jax
import jax.numpy as jnp
import ml_dtypes
import numpy as np
from jax import lax
from jax.experimental import pallas as pl
from jax.experimental.pallas import tpu as pltpu
from jax.sharding import Mesh
from jax.sharding import PartitionSpec as P

ANGULAR_BINS = 16384
MODES = 256
EMB = 32
RAD = ("rad_0", "rad_1", "rad_2")
AZ = ("az_0", "az_1")
F32 = jnp.float32
BF16 = jnp.bfloat16

gravity = 1.0
timestep_length = 0.05
courant = 0.4
softening = 0.02
cell_step = 2.0 * np.pi / ANGULAR_BINS

ROWS = 32
CHUNKS = 32
GROUPS = 4
SPAN = 8 * CHUNKS
RING = 8 * (5 * CHUNKS + 8)
WIDE = 256
BLOCKS = 16


def split_bf16(table):
    high = table.astype(np.float32).astype(ml_dtypes.bfloat16)
    low = (table - high.astype(np.float64)).astype(np.float32).astype(ml_dtypes.bfloat16)
    return high, low


def constant_tables():
    orders = np.arange(MODES)
    inner = np.arange(WIDE)
    phases = orders[None, :] * (2 * inner[:, None] + 1) % (2 * ANGULAR_BINS) * (np.pi / ANGULAR_BINS)
    basis = np.concatenate([np.cos(phases), np.sin(phases)], axis=1)
    starts = np.arange(ANGULAR_BINS // WIDE) * WIDE
    turns = orders[None, :] * starts[:, None] % ANGULAR_BINS * (2 * np.pi / ANGULAR_BINS)
    twiddle = np.concatenate([np.cos(turns), np.sin(turns)], axis=1).astype(np.float32)
    halves = (2 * np.arange(ANGULAR_BINS) + 1) * (0.5 * np.pi / ANGULAR_BINS)
    wholes = 2 * halves
    angles = np.stack([np.cos(halves), np.sin(halves), np.cos(wholes), np.sin(wholes)])
    angles = angles.reshape(4, 4, CHUNKS, 128).transpose(1, 0, 2, 3).reshape(16, CHUNKS, 128)
    decays = np.tile((orders + 0.5) * cell_step, 2)
    rows = np.arange(ROWS)
    lift = np.exp(-decays[None, :] * (rows[:, None] + 1))
    drop = np.exp(-decays[None, :] * (ROWS - rows[:, None]))
    doubled = np.tile(np.where(orders > 0, 2.0, 1.0), 2)
    radial = -(gravity / cell_step) * doubled * decays * decays
    azim = gravity * np.concatenate([orders * doubled[:MODES], -orders * doubled[:MODES]])
    azim = azim * decays
    vectors = np.zeros((8, 2 * MODES))
    vectors[0] = np.exp(-decays)
    vectors[1] = radial
    vectors[2] = azim
    return (
        split_bf16(basis),
        split_bf16(basis.T),
        twiddle,
        angles.astype(np.float32),
        lift.astype(np.float32),
        drop.astype(np.float32),
        vectors.astype(np.float32),
        np.tile((decays * ROWS).astype(np.float32).reshape(4, 128), (2, 1)),
    )


def to_tiles(value):
    return value.reshape(GROUPS, 8, CHUNKS, 128).transpose(0, 2, 1, 3).reshape(GROUPS, SPAN, 128)


def from_tiles(value):
    return value.reshape(GROUPS, CHUNKS, 8, 128).transpose(0, 2, 1, 3).reshape(ROWS, CHUNKS * 128)


def vmem():
    return pl.BlockSpec(memory_space=pltpu.VMEM)


def smem():
    return pl.BlockSpec(memory_space=pltpu.SMEM)


def anywhere():
    return pl.BlockSpec(memory_space=pl.ANY)


def params():
    return pltpu.CompilerParams(vmem_limit_bytes=14 * 1024 * 1024)


def cost(us):
    return pl.CostEstimate(flops=int(us * 1e6), bytes_accessed=int(us * 2.5e6), transcendentals=0)


def donor_flux(speeds, upstream, downstream):
    return jnp.where(speeds > 0, speeds * upstream, speeds * downstream)


def azimuth_kernel(
    dens_ref, phi_ref, vrad_ref, left_ref, right_ref, offs_ref, out_ref, up_ref, down_ref,
    dens_buf, phi_buf, vrad_buf, sems,
):
    lane = lax.broadcasted_iota(jnp.int32, (1, 8, 128), 2)
    copies = []
    for group in range(GROUPS):
        copies.append(
            (
                pltpu.make_async_copy(dens_ref.at[group], dens_buf.at[group], sems.at[2 * group]),
                pltpu.make_async_copy(phi_ref.at[group], phi_buf.at[group], sems.at[2 * group + 1]),
            )
        )
    ends = (
        pltpu.make_async_copy(vrad_ref.at[0], vrad_buf.at[0], sems.at[8]),
        pltpu.make_async_copy(vrad_ref.at[3], vrad_buf.at[1], sems.at[9]),
    )
    for pair in copies + [ends]:
        for copy in pair:
            copy.start()

    def following(value):
        turned = pltpu.roll(value, 127, 2)
        return jnp.where(lane == 127, turned[1:], turned[:-1])

    def widened(ref, group, base):
        rows = slice(base + 8 * group, base + 8 * group + 8)
        middle = ref[group].reshape(CHUNKS, 8, 128)
        return jnp.concatenate([left_ref[rows, :][None], middle, right_ref[rows, :][None]], axis=0)

    for group in range(GROUPS):
        for copy in copies[group]:
            copy.wait()
        dens = widened(dens_buf, group, 0)
        phi = widened(phi_buf, group, ROWS)
        speeds = 0.5 * (phi[:-1] + following(phi))
        flux = donor_flux(speeds, dens[:-1], following(dens))
        turned = pltpu.roll(flux, 1, 2)
        before = jnp.where(lane == 0, turned[:-1], turned[1:])
        stepped = dens[1:-1] - courant * (flux[1:] - before)
        out_ref[group] = stepped.reshape(SPAN, 128)
    for copy in ends:
        copy.wait()
    for side, (ref, group, row) in enumerate(((down_ref, 0, 0), (up_ref, 3, 7))):
        ref[pl.ds(0, CHUNKS, stride=2), :] = out_ref[group, pl.ds(row, CHUNKS, stride=8), :]
        ref[pl.ds(1, CHUNKS, stride=2), :] = vrad_buf[side, pl.ds(row, CHUNKS, stride=8), :]
        ref[64:72, :] = jnp.full((8, 128), offs_ref[8 * group + row].astype(F32), F32)


def fill_ring(group, own_ref, mate_ref, cross_ref, far_ref, ring_ref, unit):
    odd = lax.axis_index(AZ) % 2
    places = ((own_ref, 0), (own_ref, 4), (cross_ref, 2), (mate_ref, 1 + 2 * odd), (far_ref, 3 - 2 * odd))
    for source, place in places:
        where = pl.ds(pl.multiple_of(place * unit, unit), unit)
        ring_ref[where, :] = source[group, 0:unit, :]


def shift_row(ring_ref, step, row, offset):
    start = ANGULAR_BINS - offset
    chunk = start // 128
    turn = (128 - start % 128) % 128
    lane = lax.broadcasted_iota(jnp.int32, (CHUNKS, 128), 1)
    first = ring_ref[pl.ds(chunk * step + row, CHUNKS, stride=step), :]
    second = ring_ref[pl.ds((chunk + 1) * step + row, CHUNKS, stride=step), :]
    return jnp.where(
        lane < 128 - start % 128, pltpu.roll(first, turn, 1), pltpu.roll(second, turn, 1)
    )


def shift_kernel(offs_ref, own_ref, mate_ref, cross_ref, far_ref, out_ref, ring_ref):
    @pl.loop(0, GROUPS)
    def _(group):
        fill_ring(group, own_ref, mate_ref, cross_ref, far_ref, ring_ref, SPAN)
        for row in range(8):
            moved = shift_row(ring_ref, 8, row, offs_ref[group * 8 + row])
            out_ref[group, pl.ds(row, CHUNKS, stride=8), :] = moved


def shifted(offsets, own, mate, cross, far, name):
    return pl.pallas_call(
        shift_kernel,
        out_shape=jax.ShapeDtypeStruct((GROUPS, SPAN, 128), F32),
        in_specs=[smem(), vmem(), vmem(), vmem(), vmem()],
        out_specs=vmem(),
        scratch_shapes=[pltpu.VMEM((RING, 128), F32)],
        compiler_params=params(),
        cost_estimate=cost(2),
        name=name,
    )(offsets, own, mate, cross, far)


def split_value(value):
    high = value.astype(BF16)
    return high, (value - high.astype(F32)).astype(BF16)


def dot(left, right):
    return jnp.dot(left, right, preferred_element_type=F32)


def transport_kernel(
    offs_ref, own_ref, mate_ref, cross_ref, far_ref,
    edge_own_ref, edge_mate_ref, edge_cross_ref, edge_far_ref,
    vrad_ref, high_ref, low_ref, twiddle_ref,
    whole_ref, dens_ref, spectra_ref,
    ring_ref, edge_ref, moved_ref, speed_ref, whole_sem,
):
    for side, (place, row) in enumerate(((0, 7), (5, 0))):
        fill_ring(
            side, edge_own_ref, edge_mate_ref, edge_cross_ref, edge_far_ref, edge_ref, 2 * CHUNKS
        )
        offset = jnp.max(edge_own_ref[side, 64:72, :]).astype(jnp.int32)
        moved_ref[place, pl.ds(row, CHUNKS, stride=8), :] = shift_row(edge_ref, 2, 0, offset)
        speed_ref[side, pl.ds(row, CHUNKS, stride=8), :] = shift_row(edge_ref, 2, 1, offset)

    @pl.loop(0, GROUPS)
    def _(group):
        fill_ring(group, own_ref, mate_ref, cross_ref, far_ref, ring_ref, SPAN)
        for row in range(8):
            moved = shift_row(ring_ref, 8, row, offs_ref[group * 8 + row])
            moved_ref[group + 1, pl.ds(row, CHUNKS, stride=8), :] = moved

    sub = lax.broadcasted_iota(jnp.int32, (1, 8, 128), 1)
    own_index = lax.axis_index(RAD)
    bottom = own_index == 0
    top = own_index == lax.axis_size(RAD) - 1

    def above(value, following):
        return jnp.where(sub == 7, pltpu.roll(following, 7, 1), pltpu.roll(value, 7, 1))

    def below(value, previous):
        return jnp.where(sub == 0, pltpu.roll(previous, 1, 1), pltpu.roll(value, 1, 1))

    step = 4
    for group in range(GROUPS):

        @pl.loop(0, CHUNKS // step)
        def _(part):
            where = pl.ds(pl.multiple_of(part * 8 * step, 8 * step), 8 * step)

            def tiles(ref, index):
                return ref[index, where, :].reshape(step, 8, 128)

            dens = tiles(moved_ref, group + 1)
            dens_above = above(dens, tiles(moved_ref, group + 2))
            dens_below = below(dens, tiles(moved_ref, group))
            speed = tiles(vrad_ref, group)
            upper = tiles(vrad_ref, group + 1) if group < 3 else tiles(speed_ref, 1)
            lower = tiles(vrad_ref, group - 1) if group > 0 else tiles(speed_ref, 0)
            flux_above = donor_flux(0.5 * (speed + above(speed, upper)), dens, dens_above)
            flux_below = donor_flux(0.5 * (below(speed, lower) + speed), dens_below, dens)
            if group == 3:
                flux_above = jnp.where((sub == 7) & top, 0.0, flux_above)
            if group == 0:
                flux_below = jnp.where((sub == 0) & bottom, 0.0, flux_below)
            stepped = dens - courant * (flux_above - flux_below)
            dens_ref[group, where, :] = stepped.reshape(8 * step, 128)

    whole = pltpu.make_async_copy(dens_ref, whole_ref, whole_sem)
    whole.start()
    sector = lax.axis_index(AZ)
    cos_sum = jnp.zeros((ROWS, MODES), F32)
    sin_sum = jnp.zeros((ROWS, MODES), F32)
    together = 4
    for first in range(0, BLOCKS, together):
        pieces = []
        for block in range(first, first + together):
            halves = [
                dens_ref[:, 8 * chunk : 8 * chunk + 8, :].reshape(ROWS, 128)
                for chunk in (2 * block, 2 * block + 1)
            ]
            pieces.append(jnp.concatenate(halves, axis=1))
        high, low = split_value(jnp.concatenate(pieces, axis=0))
        part = dot(high, high_ref[...]) + (dot(low, high_ref[...]) + dot(high, low_ref[...]))
        for index in range(together):
            turn = twiddle_ref[pl.ds(sector * BLOCKS + first + index, 1), :]
            cosine, sine = turn[:, :MODES], turn[:, MODES:]
            rows = slice(index * ROWS, index * ROWS + ROWS)
            cos_part, sin_part = part[rows, :MODES], part[rows, MODES:]
            cos_sum += cosine * cos_part - sine * sin_part
            sin_sum += sine * cos_part + cosine * sin_part
    spectra_ref[:, :MODES] = cos_sum * cell_step
    spectra_ref[:, MODES:] = sin_sum * cell_step
    whole.wait()


def field_kernel(
    members_ref, radius_ref, angles_ref, radial_ref, azim_ref,
    gap_ref, chord_ref, lift_ref, side_ref,
):
    sector = lax.axis_index(AZ)
    half_cos = angles_ref[sector * 4]
    half_sin = angles_ref[sector * 4 + 1]
    radius = radius_ref[...]
    halves = 0.5 / radius

    @pl.loop(0, EMB, unroll=4)
    def _(member):
        embryo_radius = members_ref[0, member]
        scale = members_ref[1, member]
        cosine = members_ref[2, member]
        sine = members_ref[3, member]
        gap = radius - embryo_radius
        soft = softening * embryo_radius
        rows = pl.ds(pl.multiple_of(member * 32, 32), 32)
        gap_ref[rows, :] = (gap * gap + soft * soft) * halves * scale
        near = half_sin * cosine - half_cos * sine
        far = half_cos * cosine + half_sin * sine
        chord = (2.0 * embryo_radius) * (near * near)
        chord_ref[rows, :] = chord * scale
        lift_ref[rows, :] = chord - embryo_radius
        side_ref[rows, :] = (2.0 * embryo_radius) * (near * far)

    pieces = [radius[8 * g : 8 * g + 8] for g in range(GROUPS)]
    ends = []
    for g in range(GROUPS):
        root = lax.rsqrt(2.0 * pieces[g])
        ends.append(root * root * root)
    together = 2

    @pl.loop(0, CHUNKS // together)
    def _(part):
        zero = jnp.zeros((8, 128), F32)

        def visit(member, carried):
            radial, azim = list(carried[0]), list(carried[1])
            rows = []
            for k in range(together):
                row = pl.ds(member * 32 + part * together + k, 1)
                rows.append(
                    [jnp.broadcast_to(ref[row, :], (8, 128)) for ref in (chord_ref, lift_ref, side_ref)]
                )
            for g in range(GROUPS):
                gap = gap_ref[pl.ds(pl.multiple_of(member * 32 + 8 * g, 8), 8), :]
                for k in range(together):
                    chord, lift, side = rows[k]
                    inverse = lax.rsqrt(gap + chord)
                    cubed = inverse * inverse * inverse
                    at = k * GROUPS + g
                    radial[at] = radial[at] + cubed * (pieces[g] + lift)
                    azim[at] = azim[at] + cubed * side
            return tuple(radial), tuple(azim)

        count = together * GROUPS
        radial, azim = lax.fori_loop(0, EMB, visit, ((zero,) * count, (zero,) * count), unroll=4)
        for k in range(together):
            where = pl.ds(pl.multiple_of((part * together + k) * 8, 8), 8)
            for g in range(GROUPS):
                radial_ref[g, where, :] = radial[k * GROUPS + g] * ends[g]
                azim_ref[g, where, :] = azim[k * GROUPS + g] * ends[g]


def push_kernel(
    members_ref, radius_ref, angles_ref, dens_ref, spectra_ref, out_ref, mass_ref, chord_ref
):
    for part in range(4):
        out_ref[ROWS * part : ROWS * part + ROWS, :] = spectra_ref[:, 128 * part : 128 * part + 128]
    sector = lax.axis_index(AZ)
    radius = radius_ref[...]
    pieces = [radius[8 * g : 8 * g + 8] for g in range(GROUPS)]
    halves = [0.5 / piece for piece in pieces]
    for g in range(GROUPS):
        scale = lax.rsqrt(2.0 * pieces[g])
        area = pieces[g] * pieces[g] * (cell_step * cell_step) * (scale * scale * scale)
        mass_ref[g] = (dens_ref[g].reshape(CHUNKS, 8, 128) * area[None]).reshape(SPAN, 128)
    half_cos = angles_ref[sector * 4]
    half_sin = angles_ref[sector * 4 + 1]

    @pl.loop(0, EMB)
    def _(member):
        embryo_radius = members_ref[0, member]
        cosine = members_ref[2, member]
        sine = members_ref[3, member]
        soft = softening * embryo_radius
        gaps = []
        for g in range(GROUPS):
            gap = pieces[g] - embryo_radius
            gaps.append((gap * gap + soft * soft) * halves[g])
        near = half_sin * cosine - half_cos * sine
        chord_ref[...] = (2.0 * embryo_radius) * (near * near)
        push_x = jnp.zeros((8, 128), F32)
        push_y = jnp.zeros((8, 128), F32)
        total = jnp.zeros((8, 128), F32)
        for chunk in range(CHUNKS):
            chord = jnp.broadcast_to(chord_ref[chunk : chunk + 1, :], (8, 128))
            plain, moved = None, None
            for g in range(GROUPS):
                inverse = lax.rsqrt(gaps[g] + chord)
                cubed = inverse * inverse * inverse
                term = cubed * mass_ref[g, 8 * chunk : 8 * chunk + 8, :]
                plain = term if g == 0 else plain + term
                moved = pieces[g] * term if g == 0 else moved + pieces[g] * term
            row = slice(chunk, chunk + 1)
            push_x = push_x + moved * jnp.broadcast_to(angles_ref[sector * 4 + 2, row, :], (8, 128))
            push_y = push_y + moved * jnp.broadcast_to(angles_ref[sector * 4 + 3, row, :], (8, 128))
            total = total + plain
        place_x = embryo_radius * members_ref[4, member]
        place_y = embryo_radius * members_ref[5, member]
        out_ref[pl.ds(4 * ROWS + member, 1), :] = jnp.sum(push_x - place_x * total, axis=0, keepdims=True)
        out_ref[pl.ds(4 * ROWS + EMB + member, 1), :] = jnp.sum(push_y - place_y * total, axis=0, keepdims=True)


def moment_kernel(a_ref, b_ref, c_ref, d_ref, lift_ref, drop_ref, vectors_ref, spectra_ref, packed_ref, one_ref):
    total = (a_ref[...] + b_ref[...]) + (c_ref[...] + d_ref[...])
    for part in range(4):
        columns = slice(128 * part, 128 * part + 128)
        spectra = total[ROWS * part : ROWS * part + ROWS]
        spectra_ref[:, columns] = spectra
        factor = vectors_ref[0:1, columns]
        up = jnp.sum(spectra * drop_ref[:, columns], axis=0, keepdims=True) / factor
        down = jnp.sum(spectra * lift_ref[:, columns], axis=0, keepdims=True) / factor
        one_ref[part : part + 1, :] = up
        one_ref[4 + part : 5 + part, :] = down
    push = total[4 * ROWS :]
    push = jnp.broadcast_to(jnp.sum(push, axis=1, keepdims=True), (2 * EMB, 128))
    row = lax.broadcasted_iota(jnp.int32, (2 * EMB, 128), 0)
    lane = lax.broadcasted_iota(jnp.int32, (2 * EMB, 128), 1)
    push = jnp.sum(jnp.where(row == lane, push, 0.0), axis=0, keepdims=True)
    one_ref[8:16, :] = jnp.broadcast_to(push, (8, 128))
    one = one_ref[...]
    for copy in range(packed_ref.shape[0]):
        packed_ref[copy] = one


def kick_kernel(
    spectra_ref, moments_ref, rate_ref, radius_ref, vectors_ref, lift_ref, drop_ref, twiddle_ref, high_ref, low_ref,
    radial_ref, azim_ref, vrad_ref, vphi_ref,
    whole_radial_ref, whole_azim_ref, out_push_ref,
    lower_ref, upper_ref, out_radial_ref, out_azim_ref, sems,
):
    own_index = lax.axis_index(RAD)
    row = lax.broadcasted_iota(jnp.int32, (8, 128), 0)
    outside = jnp.zeros((8, 128), F32)
    push = jnp.zeros((1, 128), F32)
    for source in range(moments_ref.shape[0]):
        many = jnp.where(row < 4, own_index - 1 - source, source - own_index - 1)
        weight = jnp.exp(-rate_ref[...] * jnp.maximum(many, 0).astype(F32))
        outside += jnp.where(many >= 0, weight, 0.0) * moments_ref[source, 0:8, :]
        push += moments_ref[source, 8:9, :]
    out_push_ref[0:1, :] = push[:, :EMB]
    out_push_ref[1:2, :] = push[:, EMB : 2 * EMB]
    lower = jnp.concatenate([outside[k : k + 1] for k in range(4)], axis=1)
    upper = jnp.concatenate([outside[k : k + 1] for k in range(4, 8)], axis=1)
    factor = vectors_ref[0:1, :]
    spectra = spectra_ref[...]
    for row in range(ROWS):
        lower = spectra[row : row + 1] + factor * lower
        lower_ref[row : row + 1, :] = lower
        back = ROWS - 1 - row
        upper = spectra[back : back + 1] + factor * upper
        upper_ref[back : back + 1, :] = upper
    lower = lower_ref[...]
    upper = upper_ref[...]
    inverse = 1.0 / radius_ref[:, 0:1]
    even = lower + upper - spectra
    odd = lower - upper
    radial = odd * vectors_ref[1:2, :] * inverse
    swapped = jnp.concatenate([even[:, MODES:], even[:, :MODES]], axis=1)
    azim = swapped * vectors_ref[2:3, :] * inverse
    sector = lax.axis_index(AZ)
    copies = []
    for block in range(BLOCKS):
        turn = twiddle_ref[pl.ds(sector * BLOCKS + block, 1), :]
        cosine, sine = turn[:, :MODES], turn[:, MODES:]
        pieces = []
        for coef in (radial, azim):
            cos_coef, sin_coef = coef[:, :MODES], coef[:, MODES:]
            pieces.append(
                jnp.concatenate(
                    [cos_coef * cosine + sin_coef * sine, sin_coef * cosine - cos_coef * sine], axis=1
                )
            )
        high, low = split_value(jnp.concatenate(pieces, axis=0))
        part = dot(high, high_ref[...]) + (dot(low, high_ref[...]) + dot(high, low_ref[...]))
        for half in range(2):
            where = slice(8 * (2 * block + half), 8 * (2 * block + half) + 8)
            columns = slice(128 * half, 128 * half + 128)
            disk = part[:ROWS, columns].reshape(GROUPS, 8, 128)
            out_radial_ref[:, where, :] = vrad_ref[:, where, :] + timestep_length * (
                disk - radial_ref[:, where, :]
            )
            disk = part[ROWS:, columns].reshape(GROUPS, 8, 128)
            out_azim_ref[:, where, :] = vphi_ref[:, where, :] + timestep_length * (
                disk - azim_ref[:, where, :]
            )
        if block % 4 == 3:
            quarter = block // 4
            rows = slice(64 * quarter, 64 * quarter + 64)
            for index, (source, target) in enumerate(
                ((out_radial_ref, whole_radial_ref), (out_azim_ref, whole_azim_ref))
            ):
                copies.append(
                    pltpu.make_async_copy(
                        source.at[:, rows, :], target.at[:, rows, :], sems.at[index, quarter]
                    )
                )
                copies[-1].start()
    for copy in copies:
        copy.wait()


def across(value, axis, target):
    count = lax.axis_size(axis)
    return lax.ppermute(value, axis, [(source, target(source)) for source in range(count)])


def after(value, *others):
    return lax.optimization_barrier((value, *others))[0]


def on_device(
    surface_mass,
    outward_drift,
    leftover_angular_drift,
    angular_offsets,
    planetesimal_loop_number,
    planetesimal_angle_bin,
    planetesimal_weights,
):
    (basis_high, basis_low), (back_high, back_low), twiddle, angles, lift, drop, vectors, rate = (
        constant_tables()
    )
    tiles = jax.ShapeDtypeStruct((GROUPS, SPAN, 128), F32)
    dens = to_tiles(surface_mass)
    vrad = to_tiles(outward_drift)
    vphi = to_tiles(leftover_angular_drift)

    ends = jnp.concatenate([surface_mass[:, -128:], leftover_angular_drift[:, -128:]])
    begins = jnp.concatenate([surface_mass[:, :128], leftover_angular_drift[:, :128]])
    left = across(ends, AZ, lambda i: (i + 1) % 4)
    right = across(begins, AZ, lambda i: (i - 1) % 4)
    vrad_cross = across(after(vrad, left, right), AZ, lambda i: i ^ 2)
    vrad_mate = across(vrad, AZ, lambda i: i ^ 1)

    cell = np.float32(cell_step)
    cycles = lax.axis_index(RAD) * ROWS + jnp.arange(ROWS, dtype=jnp.int32)
    radius = jnp.broadcast_to(jnp.exp((cycles.astype(F32) + 0.5) * cell)[:, None], (ROWS, 128))
    embryo_angles = (2 * planetesimal_angle_bin + 1).astype(F32) * np.float32(np.pi / ANGULAR_BINS)
    members = jnp.stack(
        [
            jnp.exp((planetesimal_loop_number.astype(F32) + 0.5) * cell),
            jnp.exp(np.float32(-2.0 / 3.0) * jnp.log(planetesimal_weights)),
            jnp.cos(0.5 * embryo_angles),
            jnp.sin(0.5 * embryo_angles),
            jnp.cos(embryo_angles),
            jnp.sin(embryo_angles),
        ]
    )

    dens_two, edge_up, edge_down = pl.pallas_call(
        azimuth_kernel,
        out_shape=(tiles, jax.ShapeDtypeStruct((72, 128), F32), jax.ShapeDtypeStruct((72, 128), F32)),
        in_specs=[pl.BlockSpec(memory_space=pltpu.HBM)] * 3 + [vmem()] * 2 + [smem()],
        out_specs=(vmem(), vmem(), vmem()),
        scratch_shapes=[
            pltpu.VMEM((GROUPS, SPAN, 128), F32),
            pltpu.VMEM((GROUPS, SPAN, 128), F32),
            pltpu.VMEM((2, SPAN, 128), F32),
            pltpu.SemaphoreType.DMA((10,)),
        ],
        compiler_params=params(),
        cost_estimate=cost(1),
        name="azimuth",
    )(dens, vphi, vrad, left, right, angular_offsets)

    rad_count = lax.axis_size(RAD)
    edge_low = lax.ppermute(edge_up, RAD, [(i, i + 1) for i in range(rad_count - 1)])
    edge_high = lax.ppermute(edge_down, RAD, [(i + 1, i) for i in range(rad_count - 1)])
    edges = jnp.stack([edge_low, edge_high])
    edges_cross, edges_mate, edges_far = (
        across(edges, AZ, lambda i, k=k: i ^ k) for k in (2, 1, 3)
    )

    dens_mate = across(dens_two, AZ, lambda i: i ^ 1)
    dens_two_later = after(dens_two, vrad_cross, edge_low, edge_high)
    dens_cross = across(dens_two_later, AZ, lambda i: i ^ 2)
    vrad_far = across(vrad_cross, AZ, lambda i: i ^ 1)
    vrad_one = shifted(angular_offsets, vrad, vrad_mate, vrad_cross, vrad_far, "shift_vrad")

    radial_field, azim_field = pl.pallas_call(
        field_kernel,
        out_shape=(tiles, tiles),
        in_specs=[smem(), vmem(), vmem()],
        out_specs=(vmem(), vmem()),
        scratch_shapes=[pltpu.VMEM((EMB * 32, 128), F32)] * 4,
        compiler_params=params(),
        cost_estimate=cost(6),
        name="field",
    )(members, radius, angles)

    dens_cross = after(
        dens_cross, edges_cross, edges_mate, edges_far, dens_mate, vrad_one, radial_field
    )
    dens_far = across(dens_cross, AZ, lambda i: i ^ 1)
    vphi_later = after(vphi, dens_cross)
    vphi_cross = across(vphi_later, AZ, lambda i: i ^ 2)
    vphi_mate = across(vphi_later, AZ, lambda i: i ^ 1)

    transported, stepped, part = pl.pallas_call(
        transport_kernel,
        out_shape=(tiles, tiles, jax.ShapeDtypeStruct((ROWS, 2 * MODES), F32)),
        in_specs=[smem()] + [vmem()] * 12,
        out_specs=(anywhere(), vmem(), vmem()),
        scratch_shapes=[
            pltpu.VMEM((RING, 128), F32),
            pltpu.VMEM((2 * RING // 8, 128), F32),
            pltpu.VMEM((GROUPS + 2, SPAN, 128), F32),
            pltpu.VMEM((2, SPAN, 128), F32),
            pltpu.SemaphoreType.DMA,
        ],
        compiler_params=params(),
        cost_estimate=cost(3),
        name="transport",
    )(
        angular_offsets, dens_two, dens_mate, dens_cross, dens_far,
        edges, edges_mate, edges_cross, edges_far,
        vrad_one, basis_high, basis_low, twiddle,
    )

    joined_shape = jax.ShapeDtypeStruct((4 * ROWS + 2 * EMB, 128), F32)
    joined = pl.pallas_call(
        push_kernel,
        out_shape=joined_shape,
        in_specs=[smem()] + [vmem()] * 4,
        out_specs=vmem(),
        scratch_shapes=[pltpu.VMEM((GROUPS, SPAN, 128), F32), pltpu.VMEM((CHUNKS, 128), F32)],
        compiler_params=params(),
        cost_estimate=cost(6),
        name="push",
    )(members, radius, angles, stepped, part)
    joined = after(joined, vphi_cross)
    others = [across(joined, AZ, lambda i, k=k: i ^ k) for k in (2, 3, 1)]

    vphi_far = across(after(vphi_cross, joined), AZ, lambda i: i ^ 1)
    vphi_one = shifted(angular_offsets, vphi_later, vphi_mate, vphi_cross, vphi_far, "shift_vphi")

    others[0] = after(others[0], vphi_one)
    spectra, packed = pl.pallas_call(
        moment_kernel,
        out_shape=(
            jax.ShapeDtypeStruct((ROWS, 2 * MODES), F32),
            jax.ShapeDtypeStruct((rad_count, 16, 128), F32),
        ),
        in_specs=[vmem()] * 7,
        out_specs=(vmem(), vmem()),
        scratch_shapes=[pltpu.VMEM((16, 128), F32)],
        compiler_params=params(),
        cost_estimate=cost(1),
        name="moments",
    )(joined, *others, lift, drop, vectors)
    gathered = lax.all_to_all(packed, RAD, split_axis=0, concat_axis=0, tiled=True)

    kicked_radial, kicked_azim, embryo_disk_acceleration = pl.pallas_call(
        kick_kernel,
        out_shape=(tiles, tiles, jax.ShapeDtypeStruct((2, EMB), F32)),
        in_specs=[vmem()] * 14,
        out_specs=(anywhere(), anywhere(), vmem()),
        scratch_shapes=[
            pltpu.VMEM((ROWS, 2 * MODES), F32),
            pltpu.VMEM((ROWS, 2 * MODES), F32),
            pltpu.VMEM((GROUPS, SPAN, 128), F32),
            pltpu.VMEM((GROUPS, SPAN, 128), F32),
            pltpu.SemaphoreType.DMA((2, 4)),
        ],
        compiler_params=params(),
        cost_estimate=cost(5),
        name="kick",
    )(
        spectra, gathered, rate, radius, vectors, lift, drop, twiddle, back_high, back_low,
        radial_field, azim_field, vrad_one, vphi_one,
    )
    return (
        from_tiles(transported),
        from_tiles(kicked_radial),
        from_tiles(kicked_azim),
        embryo_disk_acceleration,
    )


def solution(mesh):
    torus = Mesh(mesh.devices.reshape(4, 2, 4, 2, 2), RAD + AZ)
    placed = (P(RAD, AZ), P(RAD, AZ), P(RAD, AZ), P(RAD), P(), P(), P())
    return jax.shard_map(
        on_device,
        mesh=torus,
        in_specs=placed,
        out_specs=(P(RAD, AZ), P(RAD, AZ), P(RAD, AZ), P()),
        check_vma=False,
    )
```

```python
import functools

import jax
import jax.numpy as jnp
import ml_dtypes
import numpy as np
from jax import lax
from jax.experimental import pallas as pl
from jax.experimental.pallas import tpu as pltpu
from jax.sharding import Mesh
from jax.sharding import PartitionSpec as P

ANGULAR_BINS = 16384
MODES = 256
EMB = 32
RAD = ("rad_0", "rad_1", "rad_2")
AZ = ("az_0", "az_1")
F32 = jnp.float32
BF16 = jnp.bfloat16

gravity = 1.0
timestep_length = 0.05
courant = 0.4
softening = 0.02
cell_step = 2.0 * np.pi / ANGULAR_BINS

ROWS = 32
CHUNKS = 32
GROUPS = 4
SPAN = 8 * CHUNKS
RING = 8 * (5 * CHUNKS + 8)
WIDE = 256
BLOCKS = 16


def split_bf16(table):
    high = table.astype(np.float32).astype(ml_dtypes.bfloat16)
    low = (table - high.astype(np.float64)).astype(np.float32).astype(ml_dtypes.bfloat16)
    return high, low


def constant_tables():
    orders = np.arange(MODES)
    inner = np.arange(WIDE)
    phases = orders[None, :] * (2 * inner[:, None] + 1) % (2 * ANGULAR_BINS) * (np.pi / ANGULAR_BINS)
    basis = np.concatenate([np.cos(phases), np.sin(phases)], axis=1)
    starts = np.arange(ANGULAR_BINS // WIDE) * WIDE
    turns = orders[None, :] * starts[:, None] % ANGULAR_BINS * (2 * np.pi / ANGULAR_BINS)
    twiddle = np.concatenate([np.cos(turns), np.sin(turns)], axis=1).astype(np.float32)
    halves = (2 * np.arange(ANGULAR_BINS) + 1) * (0.5 * np.pi / ANGULAR_BINS)
    wholes = 2 * halves
    angles = np.stack([np.cos(halves), np.sin(halves), np.cos(wholes), np.sin(wholes)])
    angles = angles.reshape(4, 4, CHUNKS, 128).transpose(1, 0, 2, 3).reshape(16, CHUNKS, 128)
    decays = np.tile((orders + 0.5) * cell_step, 2)
    rows = np.arange(ROWS)
    lift = np.exp(-decays[None, :] * (rows[:, None] + 1))
    drop = np.exp(-decays[None, :] * (ROWS - rows[:, None]))
    doubled = np.tile(np.where(orders > 0, 2.0, 1.0), 2)
    radial = -(gravity / cell_step) * doubled * decays * decays
    azim = gravity * np.concatenate([orders * doubled[:MODES], -orders * doubled[:MODES]])
    azim = azim * decays
    vectors = np.zeros((8, 2 * MODES))
    vectors[0] = np.exp(-decays)
    vectors[1] = radial
    vectors[2] = azim
    return (
        split_bf16(basis),
        split_bf16(basis.T),
        twiddle,
        angles.astype(np.float32),
        lift.astype(np.float32),
        drop.astype(np.float32),
        vectors.astype(np.float32),
        np.tile((decays * ROWS).astype(np.float32).reshape(4, 128), (2, 1)),
    )


def to_tiles(value):
    return value.reshape(GROUPS, 8, CHUNKS, 128).transpose(0, 2, 1, 3).reshape(GROUPS, SPAN, 128)


def from_tiles(value):
    return value.reshape(GROUPS, CHUNKS, 8, 128).transpose(0, 2, 1, 3).reshape(ROWS, CHUNKS * 128)


def vmem():
    return pl.BlockSpec(memory_space=pltpu.VMEM)


def smem():
    return pl.BlockSpec(memory_space=pltpu.SMEM)


def anywhere():
    return pl.BlockSpec(memory_space=pl.ANY)


def hbm(value):
    return pltpu.with_memory_space_constraint(value, pltpu.HBM)


def params():
    return pltpu.CompilerParams(vmem_limit_bytes=14 * 1024 * 1024)


def cost(us):
    return pl.CostEstimate(flops=int(us * 1e6), bytes_accessed=int(us * 2.5e6), transcendentals=0)


def donor_flux(speeds, upstream, downstream):
    return jnp.where(speeds > 0, speeds * upstream, speeds * downstream)


def border_kernel(dens_ref, phi_ref, vrad_ref, out_ref, buf_ref, sems):
    copies = []
    for index, ref in enumerate((dens_ref, phi_ref, vrad_ref)):
        for side, group in enumerate((0, GROUPS - 1)):
            at = 2 * index + side
            copies.append(pltpu.make_async_copy(ref.at[group], buf_ref.at[at], sems.at[at]))
    for copy in copies:
        copy.start()
    for copy in copies:
        copy.wait()
    for side, row in enumerate((0, 7)):
        for index in range(3):
            rows = buf_ref[2 * index + side, pl.ds(row, CHUNKS, stride=8), :]
            out_ref[side, pl.ds(index, CHUNKS, stride=3), :] = rows


def azimuth_kernel(dens_ref, phi_ref, mate_ref, far_ref, out_ref, dens_buf, phi_buf, sems):
    lane = lax.broadcasted_iota(jnp.int32, (1, 8, 128), 2)
    copies = []
    for group in range(GROUPS):
        copies.append(
            (
                pltpu.make_async_copy(dens_ref.at[group], dens_buf.at[group], sems.at[2 * group]),
                pltpu.make_async_copy(phi_ref.at[group], phi_buf.at[group], sems.at[2 * group + 1]),
            )
        )
    for pair in copies:
        for copy in pair:
            copy.start()

    odd = lax.axis_index(AZ) % 2 == 1

    def following(value):
        turned = pltpu.roll(value, 127, 2)
        return jnp.where(lane == 127, turned[1:], turned[:-1])

    def widened(ref, group, base):
        middle = ref[group].reshape(CHUNKS, 8, 128)
        mate, far = mate_ref[base + group][None], far_ref[base + group][None]
        return jnp.concatenate(
            [jnp.where(odd, mate, far), middle, jnp.where(odd, far, mate)], axis=0
        )

    for group in range(GROUPS):
        for copy in copies[group]:
            copy.wait()
        dens = widened(dens_buf, group, 0)
        phi = widened(phi_buf, group, GROUPS)
        speeds = 0.5 * (phi[:-1] + following(phi))
        flux = donor_flux(speeds, dens[:-1], following(dens))
        turned = pltpu.roll(flux, 1, 2)
        before = jnp.where(lane == 0, turned[:-1], turned[1:])
        stepped = dens[1:-1] - courant * (flux[1:] - before)
        out_ref[group] = stepped.reshape(SPAN, 128)


def fill_ring(group, own_ref, mate_ref, cross_ref, far_ref, ring_ref, unit):
    odd = lax.axis_index(AZ) % 2
    places = ((own_ref, 0), (own_ref, 4), (cross_ref, 2), (mate_ref, 1 + 2 * odd), (far_ref, 3 - 2 * odd))
    for source, place in places:
        where = pl.ds(pl.multiple_of(place * unit, unit), unit)
        ring_ref[where, :] = source[group, 0:unit, :]


def shift_row(ring_ref, step, row, offset):
    start = ANGULAR_BINS - offset
    chunk = start // 128
    turn = (128 - start % 128) % 128
    lane = lax.broadcasted_iota(jnp.int32, (CHUNKS, 128), 1)
    first = ring_ref[pl.ds(chunk * step + row, CHUNKS, stride=step), :]
    second = ring_ref[pl.ds((chunk + 1) * step + row, CHUNKS, stride=step), :]
    return jnp.where(
        lane < 128 - start % 128, pltpu.roll(first, turn, 1), pltpu.roll(second, turn, 1)
    )


def shift_kernel(offs_ref, own_ref, mate_ref, cross_ref, far_ref, out_ref, ring_ref):
    @pl.loop(0, GROUPS)
    def _(group):
        fill_ring(group, own_ref, mate_ref, cross_ref, far_ref, ring_ref, SPAN)
        for row in range(8):
            moved = shift_row(ring_ref, 8, row, offs_ref[group * 8 + row])
            out_ref[group, pl.ds(row, CHUNKS, stride=8), :] = moved


def shifted(offsets, own, mate, cross, far, name):
    return pl.pallas_call(
        shift_kernel,
        out_shape=jax.ShapeDtypeStruct((GROUPS, SPAN, 128), F32),
        in_specs=[smem(), vmem(), vmem(), vmem(), vmem()],
        out_specs=vmem(),
        scratch_shapes=[pltpu.VMEM((RING, 128), F32)],
        compiler_params=params(),
        cost_estimate=cost(2),
        name=name,
    )(offsets, own, mate, cross, far)


def edge_kernel(
    offs_ref, own_ref, mate_ref, cross_ref, far_ref, up_ref, down_ref, ring_ref, flux_ref, line_ref
):
    unit = 3 * CHUNKS
    length = 5 * CHUNKS
    lane = lax.broadcasted_iota(jnp.int32, (length, 128), 1)
    for side, ref in enumerate((down_ref, up_ref)):
        fill_ring(side, own_ref, mate_ref, cross_ref, far_ref, ring_ref, unit)
        ring_ref[5 * unit : 5 * unit + 24, :] = ring_ref[unit : unit + 24, :]
        offset = offs_ref[(ROWS - 1) * side]

        def following(index):
            here = pltpu.roll(ring_ref[pl.ds(index, length, stride=3), :], 127, 1)
            there = pltpu.roll(ring_ref[pl.ds(index + 3, length, stride=3), :], 127, 1)
            return jnp.where(lane == 127, there, here)

        dens = ring_ref[pl.ds(0, length, stride=3), :]
        phi = ring_ref[pl.ds(1, length, stride=3), :]
        flux = donor_flux(0.5 * (phi + following(1)), dens, following(0))
        flux_ref[8 : 8 + length, :] = flux
        before = pltpu.roll(flux_ref[7 : 7 + length, :], 1, 1)
        before = jnp.where(lane == 0, before, pltpu.roll(flux, 1, 1))
        line_ref[0:length, :] = dens - courant * (flux - before)
        ref[0:CHUNKS, :] = shift_row(line_ref, 1, 0, offset)
        ref[CHUNKS : 2 * CHUNKS, :] = shift_row(ring_ref, 3, 2, offset)


def split_value(value):
    high = value.astype(BF16)
    return high, (value - high.astype(F32)).astype(BF16)


def dot(left, right):
    return jnp.dot(left, right, preferred_element_type=F32)


def transport_kernel(
    moved_ref, low_edge_ref, high_edge_ref, vrad_ref, high_ref, low_ref, twiddle_ref,
    whole_ref, dens_ref, spectra_ref,
    other_ref, speed_ref, whole_sem,
):
    for side, (ref, row) in enumerate(((low_edge_ref, 7), (high_edge_ref, 0))):
        other_ref[side, pl.ds(row, CHUNKS, stride=8), :] = ref[0:CHUNKS, :]
        speed_ref[side, pl.ds(row, CHUNKS, stride=8), :] = ref[CHUNKS : 2 * CHUNKS, :]

    sub = lax.broadcasted_iota(jnp.int32, (1, 8, 128), 1)
    own_index = lax.axis_index(RAD)
    bottom = own_index == 0
    top = own_index == lax.axis_size(RAD) - 1

    def above(value, following):
        return jnp.where(sub == 7, pltpu.roll(following, 7, 1), pltpu.roll(value, 7, 1))

    def below(value, previous):
        return jnp.where(sub == 0, pltpu.roll(previous, 1, 1), pltpu.roll(value, 1, 1))

    step = 4
    for group in range(GROUPS):

        @pl.loop(0, CHUNKS // step)
        def _(part):
            where = pl.ds(pl.multiple_of(part * 8 * step, 8 * step), 8 * step)

            def tiles(ref, index):
                return ref[index, where, :].reshape(step, 8, 128)

            dens = tiles(moved_ref, group)
            upper = tiles(moved_ref, group + 1) if group < 3 else tiles(other_ref, 1)
            lower = tiles(moved_ref, group - 1) if group > 0 else tiles(other_ref, 0)
            dens_above = above(dens, upper)
            dens_below = below(dens, lower)
            speed = tiles(vrad_ref, group)
            upper = tiles(vrad_ref, group + 1) if group < 3 else tiles(speed_ref, 1)
            lower = tiles(vrad_ref, group - 1) if group > 0 else tiles(speed_ref, 0)
            flux_above = donor_flux(0.5 * (speed + above(speed, upper)), dens, dens_above)
            flux_below = donor_flux(0.5 * (below(speed, lower) + speed), dens_below, dens)
            if group == 3:
                flux_above = jnp.where((sub == 7) & top, 0.0, flux_above)
            if group == 0:
                flux_below = jnp.where((sub == 0) & bottom, 0.0, flux_below)
            stepped = dens - courant * (flux_above - flux_below)
            dens_ref[group, where, :] = stepped.reshape(8 * step, 128)

    whole = pltpu.make_async_copy(dens_ref, whole_ref, whole_sem)
    whole.start()
    sector = lax.axis_index(AZ)
    cos_sum = jnp.zeros((ROWS, MODES), F32)
    sin_sum = jnp.zeros((ROWS, MODES), F32)
    together = 8
    for first in range(0, BLOCKS, together):
        pieces = []
        for block in range(first, first + together):
            halves = [
                dens_ref[:, 8 * chunk : 8 * chunk + 8, :].reshape(ROWS, 128)
                for chunk in (2 * block, 2 * block + 1)
            ]
            pieces.append(jnp.concatenate(halves, axis=1))
        high, low = split_value(jnp.concatenate(pieces, axis=0))
        part = dot(high, high_ref[...]) + (dot(low, high_ref[...]) + dot(high, low_ref[...]))
        for index in range(together):
            turn = twiddle_ref[pl.ds(sector * BLOCKS + first + index, 1), :]
            cosine, sine = turn[:, :MODES], turn[:, MODES:]
            rows = slice(index * ROWS, index * ROWS + ROWS)
            cos_part, sin_part = part[rows, :MODES], part[rows, MODES:]
            cos_sum += cosine * cos_part - sine * sin_part
            sin_sum += sine * cos_part + cosine * sin_part
    spectra_ref[:, :MODES] = cos_sum * cell_step
    spectra_ref[:, MODES:] = sin_sum * cell_step
    whole.wait()


def field_kernel(members_ref, radius_ref, angles_ref, *refs, second):
    radial_ref, azim_ref, gap_ref, chord_ref, lift_ref, side_ref = refs[-6:]
    many = CHUNKS // 2
    base = many * second
    if second:
        rows = slice(0, 8 * base)
        radial_ref[:, rows, :] = refs[0][:, rows, :]
        azim_ref[:, rows, :] = refs[1][:, rows, :]
    sector = lax.axis_index(AZ)
    half_cos = angles_ref[sector * 4, base : base + many, :]
    half_sin = angles_ref[sector * 4 + 1, base : base + many, :]
    radius = radius_ref[...]
    halves = 0.5 / radius

    @pl.loop(0, EMB, unroll=4)
    def _(member):
        embryo_radius = members_ref[0, member]
        scale = members_ref[1, member]
        cosine = members_ref[2, member]
        sine = members_ref[3, member]
        gap = radius - embryo_radius
        soft = softening * embryo_radius
        rows = pl.ds(pl.multiple_of(member * 32, 32), 32)
        gap_ref[rows, :] = (gap * gap + soft * soft) * halves * scale
        near = half_sin * cosine - half_cos * sine
        far = half_cos * cosine + half_sin * sine
        chord = (2.0 * embryo_radius) * (near * near)
        columns = pl.ds(pl.multiple_of(member * many, many), many)
        chord_ref[columns, :] = chord * scale
        lift_ref[columns, :] = chord - embryo_radius
        side_ref[columns, :] = (2.0 * embryo_radius) * (near * far)

    pieces = [radius[8 * g : 8 * g + 8] for g in range(GROUPS)]
    ends = []
    for g in range(GROUPS):
        root = lax.rsqrt(2.0 * pieces[g])
        ends.append(root * root * root)
    together = 2

    @pl.loop(0, many // together)
    def _(part):
        zero = jnp.zeros((8, 128), F32)

        def visit(member, carried):
            radial, azim = list(carried[0]), list(carried[1])
            rows = []
            for k in range(together):
                row = pl.ds(member * many + part * together + k, 1)
                rows.append(
                    [jnp.broadcast_to(ref[row, :], (8, 128)) for ref in (chord_ref, lift_ref, side_ref)]
                )
            for g in range(GROUPS):
                gap = gap_ref[pl.ds(pl.multiple_of(member * 32 + 8 * g, 8), 8), :]
                for k in range(together):
                    chord, lift, side = rows[k]
                    inverse = lax.rsqrt(gap + chord)
                    cubed = inverse * inverse * inverse
                    at = k * GROUPS + g
                    radial[at] = radial[at] + cubed * (pieces[g] + lift)
                    azim[at] = azim[at] + cubed * side
            return tuple(radial), tuple(azim)

        count = together * GROUPS
        radial, azim = lax.fori_loop(0, EMB, visit, ((zero,) * count, (zero,) * count), unroll=4)
        for k in range(together):
            where = pl.ds(pl.multiple_of((base + part * together + k) * 8, 8), 8)
            for g in range(GROUPS):
                radial_ref[g, where, :] = radial[k * GROUPS + g] * ends[g]
                azim_ref[g, where, :] = azim[k * GROUPS + g] * ends[g]


def push_kernel(
    members_ref, radius_ref, angles_ref, dens_ref, spectra_ref, out_ref, mass_ref, chord_ref, push_ref
):
    for part in range(4):
        out_ref[ROWS * part : ROWS * part + ROWS, :] = spectra_ref[:, 128 * part : 128 * part + 128]
    sector = lax.axis_index(AZ)
    radius = radius_ref[...]
    pieces = [radius[8 * g : 8 * g + 8] for g in range(GROUPS)]
    halves = [0.5 / piece for piece in pieces]
    for g in range(GROUPS):
        scale = lax.rsqrt(2.0 * pieces[g])
        area = pieces[g] * pieces[g] * (cell_step * cell_step) * (scale * scale * scale)
        mass_ref[g] = (dens_ref[g].reshape(CHUNKS, 8, 128) * area[None]).reshape(SPAN, 128)
    half_cos = angles_ref[sector * 4]
    half_sin = angles_ref[sector * 4 + 1]

    @pl.loop(0, EMB)
    def _(member):
        embryo_radius = members_ref[0, member]
        cosine = members_ref[2, member]
        sine = members_ref[3, member]
        soft = softening * embryo_radius
        gaps = []
        for g in range(GROUPS):
            gap = pieces[g] - embryo_radius
            gaps.append((gap * gap + soft * soft) * halves[g])
        near = half_sin * cosine - half_cos * sine
        chord_ref[...] = (2.0 * embryo_radius) * (near * near)
        push_x = jnp.zeros((8, 128), F32)
        push_y = jnp.zeros((8, 128), F32)
        total = jnp.zeros((8, 128), F32)
        for chunk in range(CHUNKS):
            chord = jnp.broadcast_to(chord_ref[chunk : chunk + 1, :], (8, 128))
            plain, moved = None, None
            for g in range(GROUPS):
                inverse = lax.rsqrt(gaps[g] + chord)
                cubed = inverse * inverse * inverse
                term = cubed * mass_ref[g, 8 * chunk : 8 * chunk + 8, :]
                plain = term if g == 0 else plain + term
                moved = pieces[g] * term if g == 0 else moved + pieces[g] * term
            row = slice(chunk, chunk + 1)
            push_x = push_x + moved * jnp.broadcast_to(angles_ref[sector * 4 + 2, row, :], (8, 128))
            push_y = push_y + moved * jnp.broadcast_to(angles_ref[sector * 4 + 3, row, :], (8, 128))
            total = total + plain
        place_x = embryo_radius * members_ref[4, member]
        place_y = embryo_radius * members_ref[5, member]
        push_ref[pl.ds(member, 1), :] = jnp.sum(push_x - place_x * total, axis=0, keepdims=True)
        push_ref[pl.ds(EMB + member, 1), :] = jnp.sum(push_y - place_y * total, axis=0, keepdims=True)

    push = jnp.broadcast_to(jnp.sum(push_ref[...], axis=1, keepdims=True), (2 * EMB, 128))
    row = lax.broadcasted_iota(jnp.int32, (2 * EMB, 128), 0)
    lane = lax.broadcasted_iota(jnp.int32, (2 * EMB, 128), 1)
    push = jnp.sum(jnp.where(row == lane, push, 0.0), axis=0, keepdims=True)
    out_ref[4 * ROWS : 4 * ROWS + 8, :] = jnp.broadcast_to(push, (8, 128))


def moment_kernel(a_ref, b_ref, lift_ref, drop_ref, vectors_ref, spectra_ref, packed_ref, one_ref):
    total = a_ref[...] + b_ref[...]
    for part in range(4):
        columns = slice(128 * part, 128 * part + 128)
        spectra = total[ROWS * part : ROWS * part + ROWS]
        spectra_ref[:, columns] = spectra
        factor = vectors_ref[0:1, columns]
        up = jnp.sum(spectra * drop_ref[:, columns], axis=0, keepdims=True) / factor
        down = jnp.sum(spectra * lift_ref[:, columns], axis=0, keepdims=True) / factor
        one_ref[part : part + 1, :] = up
        one_ref[4 + part : 5 + part, :] = down
    one_ref[8:16, :] = total[4 * ROWS :]
    one = one_ref[...]
    for copy in range(packed_ref.shape[0]):
        packed_ref[copy] = one


def kick_kernel(
    spectra_ref, moments_ref, rate_ref, radius_ref, vectors_ref, lift_ref, drop_ref, twiddle_ref, high_ref, low_ref,
    radial_ref, azim_ref, vrad_ref, vphi_ref,
    whole_radial_ref, whole_azim_ref, out_push_ref,
    lower_ref, upper_ref, out_radial_ref, out_azim_ref, sems,
):
    own_index = lax.axis_index(RAD)
    row = lax.broadcasted_iota(jnp.int32, (8, 128), 0)
    outside = jnp.zeros((8, 128), F32)
    push = jnp.zeros((1, 128), F32)
    for source in range(moments_ref.shape[0]):
        many = jnp.where(row < 4, own_index - 1 - source, source - own_index - 1)
        weight = jnp.exp(-rate_ref[...] * jnp.maximum(many, 0).astype(F32))
        outside += jnp.where(many >= 0, weight, 0.0) * moments_ref[source, 0:8, :]
        push += moments_ref[source, 8:9, :]
    out_push_ref[0:1, :] = push[:, :EMB]
    out_push_ref[1:2, :] = push[:, EMB : 2 * EMB]
    lower = jnp.concatenate([outside[k : k + 1] for k in range(4)], axis=1)
    upper = jnp.concatenate([outside[k : k + 1] for k in range(4, 8)], axis=1)
    factor = vectors_ref[0:1, :]
    spectra = spectra_ref[...]
    for row in range(ROWS):
        lower = spectra[row : row + 1] + factor * lower
        lower_ref[row : row + 1, :] = lower
        back = ROWS - 1 - row
        upper = spectra[back : back + 1] + factor * upper
        upper_ref[back : back + 1, :] = upper
    lower = lower_ref[...]
    upper = upper_ref[...]
    inverse = 1.0 / radius_ref[:, 0:1]
    even = lower + upper - spectra
    odd = lower - upper
    radial = odd * vectors_ref[1:2, :] * inverse
    swapped = jnp.concatenate([even[:, MODES:], even[:, :MODES]], axis=1)
    azim = swapped * vectors_ref[2:3, :] * inverse
    sector = lax.axis_index(AZ)
    together = 4

    def whole_copies(quarter):
        rows = pl.ds(pl.multiple_of(16 * together * quarter, 16 * together), 16 * together)
        return [
            pltpu.make_async_copy(source.at[:, rows, :], target.at[:, rows, :], sems.at[index, quarter])
            for index, (source, target) in enumerate(
                ((out_radial_ref, whole_radial_ref), (out_azim_ref, whole_azim_ref))
            )
        ]

    @pl.loop(0, BLOCKS // together)
    def _(quarter):
        pieces = []
        for index in range(together):
            turn = twiddle_ref[pl.ds(sector * BLOCKS + quarter * together + index, 1), :]
            cosine, sine = turn[:, :MODES], turn[:, MODES:]
            for coef in (radial, azim):
                cos_coef, sin_coef = coef[:, :MODES], coef[:, MODES:]
                pieces.append(
                    jnp.concatenate(
                        [cos_coef * cosine + sin_coef * sine, sin_coef * cosine - cos_coef * sine], axis=1
                    )
                )
        high, low = split_value(jnp.concatenate(pieces, axis=0))
        part = dot(high, high_ref[...]) + (dot(low, high_ref[...]) + dot(high, low_ref[...]))
        for index in range(together):
            for half in range(2):
                start = 16 * together * quarter + 8 * (2 * index + half)
                where = pl.ds(pl.multiple_of(start, 8), 8)
                columns = slice(128 * half, 128 * half + 128)
                rows = 2 * ROWS * index
                disk = part[rows : rows + ROWS, columns].reshape(GROUPS, 8, 128)
                out_radial_ref[:, where, :] = vrad_ref[:, where, :] + timestep_length * (
                    disk - radial_ref[:, where, :]
                )
                disk = part[rows + ROWS : rows + 2 * ROWS, columns].reshape(GROUPS, 8, 128)
                out_azim_ref[:, where, :] = vphi_ref[:, where, :] + timestep_length * (
                    disk - azim_ref[:, where, :]
                )
        for copy in whole_copies(quarter):
            copy.start()

    for quarter in range(BLOCKS // together):
        for copy in whole_copies(quarter):
            copy.wait()


def across(value, axis, target):
    count = lax.axis_size(axis)
    return lax.ppermute(value, axis, [(source, target(source)) for source in range(count)])


def after(value, *others):
    return lax.optimization_barrier((value, *others))[0]


def on_device(
    surface_mass,
    outward_drift,
    leftover_angular_drift,
    angular_offsets,
    planetesimal_loop_number,
    planetesimal_angle_bin,
    planetesimal_weights,
):
    (basis_high, basis_low), (back_high, back_low), twiddle, angles, lift, drop, vectors, rate = (
        constant_tables()
    )
    tiles = jax.ShapeDtypeStruct((GROUPS, SPAN, 128), F32)
    dens = to_tiles(surface_mass)
    vrad = to_tiles(outward_drift)
    vphi = to_tiles(leftover_angular_drift)

    odd = lax.axis_index(AZ) % 2 == 1
    ends = jnp.concatenate([surface_mass[:, -128:], leftover_angular_drift[:, -128:]])
    begins = jnp.concatenate([surface_mass[:, :128], leftover_angular_drift[:, :128]])
    outer = jnp.where(odd, ends, begins).reshape(2 * GROUPS, 8, 128)
    inner = jnp.where(odd, begins, ends).reshape(2 * GROUPS, 8, 128)
    border_far = across(outer, AZ, lambda i: i ^ 3)
    border_mate = across(inner, AZ, lambda i: i ^ 1)
    edge_rows = pl.pallas_call(
        border_kernel,
        out_shape=jax.ShapeDtypeStruct((2, 3 * CHUNKS, 128), F32),
        in_specs=[pl.BlockSpec(memory_space=pltpu.HBM)] * 3,
        out_specs=vmem(),
        scratch_shapes=[pltpu.VMEM((6, SPAN, 128), F32), pltpu.SemaphoreType.DMA((6,))],
        compiler_params=params(),
        cost_estimate=cost(1),
        name="borders",
    )(hbm(dens), hbm(vphi), hbm(vrad))
    edge_cross = across(edge_rows, AZ, lambda i: i ^ 2)
    edge_mate = across(edge_rows, AZ, lambda i: i ^ 1)
    vrad_cross = across(after(vrad, border_mate, border_far, edge_rows), AZ, lambda i: i ^ 2)
    vrad_mate = across(vrad, AZ, lambda i: i ^ 1)

    cell = np.float32(cell_step)
    cycles = lax.axis_index(RAD) * ROWS + jnp.arange(ROWS, dtype=jnp.int32)
    radius = jnp.broadcast_to(jnp.exp((cycles.astype(F32) + 0.5) * cell)[:, None], (ROWS, 128))
    embryo_angles = (2 * planetesimal_angle_bin + 1).astype(F32) * np.float32(np.pi / ANGULAR_BINS)
    members = jnp.stack(
        [
            jnp.exp((planetesimal_loop_number.astype(F32) + 0.5) * cell),
            jnp.exp(np.float32(-2.0 / 3.0) * jnp.log(planetesimal_weights)),
            jnp.cos(0.5 * embryo_angles),
            jnp.sin(0.5 * embryo_angles),
            jnp.cos(embryo_angles),
            jnp.sin(embryo_angles),
        ]
    )

    dens_two = pl.pallas_call(
        azimuth_kernel,
        out_shape=tiles,
        in_specs=[pl.BlockSpec(memory_space=pltpu.HBM)] * 2 + [vmem()] * 2,
        out_specs=vmem(),
        scratch_shapes=[
            pltpu.VMEM((GROUPS, SPAN, 128), F32),
            pltpu.VMEM((GROUPS, SPAN, 128), F32),
            pltpu.SemaphoreType.DMA((8,)),
        ],
        compiler_params=params(),
        cost_estimate=cost(1),
        name="azimuth",
    )(hbm(dens), hbm(vphi), border_mate, border_far)

    edge_far = across(edge_cross, AZ, lambda i: i ^ 1)
    edge = jax.ShapeDtypeStruct((2 * CHUNKS, 128), F32)
    edge_up, edge_down = pl.pallas_call(
        edge_kernel,
        out_shape=(edge, edge),
        in_specs=[smem()] + [vmem()] * 4,
        out_specs=(vmem(), vmem()),
        scratch_shapes=[
            pltpu.VMEM((3 * RING // 8, 128), F32),
            pltpu.VMEM((RING // 8 + 8, 128), F32),
            pltpu.VMEM((RING // 8, 128), F32),
        ],
        compiler_params=params(),
        cost_estimate=cost(1),
        name="edges",
    )(angular_offsets, edge_rows, edge_mate, edge_cross, edge_far)
    rad_count = lax.axis_size(RAD)
    edge_low = lax.ppermute(edge_up, RAD, [(i, i + 1) for i in range(rad_count - 1)])
    edge_high = lax.ppermute(edge_down, RAD, [(i + 1, i) for i in range(rad_count - 1)])

    def field(second, *before):
        return pl.pallas_call(
            functools.partial(field_kernel, second=second),
            out_shape=(tiles, tiles),
            in_specs=[smem(), vmem(), vmem()] + [vmem()] * len(before),
            out_specs=(vmem(), vmem()),
            scratch_shapes=[pltpu.VMEM((EMB * 32, 128), F32)] + [pltpu.VMEM((EMB * 16, 128), F32)] * 3,
            compiler_params=params(),
            cost_estimate=cost(4),
            name=f"field_{second}",
        )(members, radius, angles, *before)

    first_field = field(0)
    dens_mate = across(dens_two, AZ, lambda i: i ^ 1)
    dens_cross = across(after(dens_two, vrad_cross, edge_up, *first_field), AZ, lambda i: i ^ 2)
    vrad_far = across(after(vrad_cross, dens_two, *first_field), AZ, lambda i: i ^ 1)
    vrad_one = shifted(angular_offsets, vrad, vrad_mate, vrad_cross, vrad_far, "shift_vrad")
    radial_field, azim_field = field(1, *first_field)
    dens_cross = after(dens_cross, vrad_one, radial_field, dens_mate, edge_low, edge_high)
    dens_far = across(dens_cross, AZ, lambda i: i ^ 1)

    dens_one = shifted(
        angular_offsets, dens_two, dens_mate, dens_cross, dens_far, "shift_dens"
    )
    vphi_later = after(vphi, dens_cross)
    vphi_cross = across(vphi_later, AZ, lambda i: i ^ 2)
    vphi_mate = across(vphi_later, AZ, lambda i: i ^ 1)

    transported, stepped, part = pl.pallas_call(
        transport_kernel,
        out_shape=(tiles, tiles, jax.ShapeDtypeStruct((ROWS, 2 * MODES), F32)),
        in_specs=[vmem()] * 7,
        out_specs=(anywhere(), vmem(), vmem()),
        scratch_shapes=[
            pltpu.VMEM((2, SPAN, 128), F32),
            pltpu.VMEM((2, SPAN, 128), F32),
            pltpu.SemaphoreType.DMA,
        ],
        compiler_params=params(),
        cost_estimate=cost(3),
        name="transport",
    )(
        dens_one, edge_low, edge_high,
        vrad_one, basis_high, basis_low, twiddle,
    )

    joined_shape = jax.ShapeDtypeStruct((4 * ROWS + 8, 128), F32)
    joined = pl.pallas_call(
        push_kernel,
        out_shape=joined_shape,
        in_specs=[smem()] + [vmem()] * 4,
        out_specs=vmem(),
        scratch_shapes=[
            pltpu.VMEM((GROUPS, SPAN, 128), F32),
            pltpu.VMEM((CHUNKS, 128), F32),
            pltpu.VMEM((2 * EMB, 128), F32),
        ],
        compiler_params=params(),
        cost_estimate=cost(6),
        name="push",
    )(members, radius, angles, stepped, part)
    chip = joined + across(joined, AZ, lambda i: i ^ 1)
    chip_other = across(chip, AZ, lambda i: i ^ 2)

    vphi_far = across(after(vphi_cross, chip), AZ, lambda i: i ^ 1)
    vphi_one = shifted(angular_offsets, vphi_later, vphi_mate, vphi_cross, vphi_far, "shift_vphi")

    chip_later = after(chip, vphi_one)
    spectra, packed = pl.pallas_call(
        moment_kernel,
        out_shape=(
            jax.ShapeDtypeStruct((ROWS, 2 * MODES), F32),
            jax.ShapeDtypeStruct((rad_count, 16, 128), F32),
        ),
        in_specs=[vmem()] * 5,
        out_specs=(vmem(), vmem()),
        scratch_shapes=[pltpu.VMEM((16, 128), F32)],
        compiler_params=params(),
        cost_estimate=cost(1),
        name="moments",
    )(chip_later, chip_other, lift, drop, vectors)
    gathered = lax.all_to_all(packed, RAD, split_axis=0, concat_axis=0, tiled=True)

    kicked_radial, kicked_azim, embryo_disk_acceleration = pl.pallas_call(
        kick_kernel,
        out_shape=(tiles, tiles, jax.ShapeDtypeStruct((2, EMB), F32)),
        in_specs=[vmem()] * 14,
        out_specs=(anywhere(), anywhere(), vmem()),
        scratch_shapes=[
            pltpu.VMEM((ROWS, 2 * MODES), F32),
            pltpu.VMEM((ROWS, 2 * MODES), F32),
            pltpu.VMEM((GROUPS, SPAN, 128), F32),
            pltpu.VMEM((GROUPS, SPAN, 128), F32),
            pltpu.SemaphoreType.DMA((2, 4)),
        ],
        compiler_params=params(),
        cost_estimate=cost(5),
        name="kick",
    )(
        spectra, gathered, rate, radius, vectors, lift, drop, twiddle, back_high, back_low,
        radial_field, azim_field, vrad_one, vphi_one,
    )
    return (
        from_tiles(transported),
        from_tiles(kicked_radial),
        from_tiles(kicked_azim),
        embryo_disk_acceleration,
    )


def solution(mesh):
    torus = Mesh(mesh.devices.reshape(4, 2, 4, 2, 2), RAD + AZ)
    placed = (P(RAD, AZ), P(RAD, AZ), P(RAD, AZ), P(RAD), P(), P(), P())
    return jax.shard_map(
        on_device,
        mesh=torus,
        in_specs=placed,
        out_specs=(P(RAD, AZ), P(RAD, AZ), P(RAD, AZ), P()),
        check_vma=False,
    )
```

```python
import functools

import jax
import jax.numpy as jnp
import ml_dtypes
import numpy as np
from jax import lax
from jax.experimental import pallas as pl
from jax.experimental.pallas import tpu as pltpu
from jax.sharding import Mesh
from jax.sharding import PartitionSpec as P

ANGULAR_BINS = 16384
MODES = 256
EMB = 32
RAD = ("rad_0", "rad_1", "rad_2")
AZ = ("az_0", "az_1")
F32 = jnp.float32
BF16 = jnp.bfloat16

gravity = 1.0
timestep_length = 0.05
courant = 0.4
softening = 0.02
cell_step = 2.0 * np.pi / ANGULAR_BINS

ROWS = 32
CHUNKS = 32
GROUPS = 4
SPAN = 8 * CHUNKS
RING = 8 * (5 * CHUNKS + 8)
WIDE = 256
BLOCKS = 16


def split_bf16(table):
    high = table.astype(np.float32).astype(ml_dtypes.bfloat16)
    low = (table - high.astype(np.float64)).astype(np.float32).astype(ml_dtypes.bfloat16)
    return high, low


def constant_tables():
    orders = np.arange(MODES)
    inner = np.arange(WIDE)
    phases = orders[None, :] * (2 * inner[:, None] + 1) % (2 * ANGULAR_BINS) * (np.pi / ANGULAR_BINS)
    basis = np.concatenate([np.cos(phases), np.sin(phases)], axis=1)
    starts = np.arange(ANGULAR_BINS // WIDE) * WIDE
    turns = orders[None, :] * starts[:, None] % ANGULAR_BINS * (2 * np.pi / ANGULAR_BINS)
    twiddle = np.concatenate([np.cos(turns), np.sin(turns)], axis=1).astype(np.float32)
    halves = (2 * np.arange(ANGULAR_BINS) + 1) * (0.5 * np.pi / ANGULAR_BINS)
    wholes = 2 * halves
    angles = np.stack([np.cos(halves), np.sin(halves), np.cos(wholes), np.sin(wholes)])
    angles = angles.reshape(4, 4, CHUNKS, 128).transpose(1, 0, 2, 3).reshape(16, CHUNKS, 128)
    decays = np.tile((orders + 0.5) * cell_step, 2)
    rows = np.arange(ROWS)
    lift = np.exp(-decays[None, :] * (rows[:, None] + 1))
    drop = np.exp(-decays[None, :] * (ROWS - rows[:, None]))
    doubled = np.tile(np.where(orders > 0, 2.0, 1.0), 2)
    radial = -(gravity / cell_step) * doubled * decays * decays
    azim = gravity * np.concatenate([orders * doubled[:MODES], -orders * doubled[:MODES]])
    azim = azim * decays
    vectors = np.zeros((8, 2 * MODES))
    vectors[0] = np.exp(-decays)
    vectors[1] = radial
    vectors[2] = azim
    return (
        split_bf16(basis),
        split_bf16(basis.T),
        twiddle,
        angles.astype(np.float32),
        lift.astype(np.float32),
        drop.astype(np.float32),
        vectors.astype(np.float32),
        np.tile((decays * ROWS).astype(np.float32).reshape(4, 128), (2, 1)),
    )


def to_tiles(value):
    return value.reshape(GROUPS, 8, CHUNKS, 128).transpose(0, 2, 1, 3).reshape(GROUPS, SPAN, 128)


def from_tiles(value):
    return value.reshape(GROUPS, CHUNKS, 8, 128).transpose(0, 2, 1, 3).reshape(ROWS, CHUNKS * 128)


def vmem():
    return pl.BlockSpec(memory_space=pltpu.VMEM)


def smem():
    return pl.BlockSpec(memory_space=pltpu.SMEM)


def anywhere():
    return pl.BlockSpec(memory_space=pl.ANY)


def hbm(value):
    return pltpu.with_memory_space_constraint(value, pltpu.HBM)


def params():
    return pltpu.CompilerParams(vmem_limit_bytes=14 * 1024 * 1024)


def cost(us):
    return pl.CostEstimate(flops=int(us * 1e6), bytes_accessed=int(us * 2.5e6), transcendentals=0)


def donor_flux(speeds, upstream, downstream):
    return jnp.where(speeds > 0, speeds * upstream, speeds * downstream)


def border_kernel(dens_ref, phi_ref, vrad_ref, outer_ref, inner_ref, out_ref, buf_ref, sems):
    odd = lax.axis_index(AZ) % 2
    copies = []
    for index, ref in enumerate((dens_ref, phi_ref)):
        where = slice(GROUPS * index, GROUPS * index + GROUPS)
        outer = pl.ds(pl.multiple_of(odd * (SPAN - 8), 8), 8)
        inner = pl.ds(pl.multiple_of((1 - odd) * (SPAN - 8), 8), 8)
        copies.append((ref.at[:, outer, :], outer_ref.at[where]))
        copies.append((ref.at[:, inner, :], inner_ref.at[where]))
    for index, ref in enumerate((dens_ref, phi_ref, vrad_ref)):
        for side, group in enumerate((0, GROUPS - 1)):
            copies.append((ref.at[group], buf_ref.at[2 * index + side]))
    copies = [pltpu.make_async_copy(*copy, sems.at[index]) for index, copy in enumerate(copies)]
    for copy in copies:
        copy.start()
    for copy in copies:
        copy.wait()
    for side, row in enumerate((0, 7)):
        for index in range(3):
            rows = buf_ref[2 * index + side, pl.ds(row, CHUNKS, stride=8), :]
            out_ref[side, pl.ds(index, CHUNKS, stride=3), :] = rows


def azimuth_kernel(dens_ref, phi_ref, mate_ref, far_ref, out_ref, dens_buf, phi_buf, sems):
    lane = lax.broadcasted_iota(jnp.int32, (1, 8, 128), 2)
    copies = []
    for group in range(GROUPS):
        copies.append(
            (
                pltpu.make_async_copy(dens_ref.at[group], dens_buf.at[group], sems.at[2 * group]),
                pltpu.make_async_copy(phi_ref.at[group], phi_buf.at[group], sems.at[2 * group + 1]),
            )
        )
    for pair in copies:
        for copy in pair:
            copy.start()

    odd = lax.axis_index(AZ) % 2 == 1

    def following(value):
        turned = pltpu.roll(value, 127, 2)
        return jnp.where(lane == 127, turned[1:], turned[:-1])

    def widened(ref, group, base):
        middle = ref[group].reshape(CHUNKS, 8, 128)
        mate, far = mate_ref[base + group][None], far_ref[base + group][None]
        return jnp.concatenate(
            [jnp.where(odd, mate, far), middle, jnp.where(odd, far, mate)], axis=0
        )

    for group in range(GROUPS):
        for copy in copies[group]:
            copy.wait()
        dens = widened(dens_buf, group, 0)
        phi = widened(phi_buf, group, GROUPS)
        speeds = 0.5 * (phi[:-1] + following(phi))
        flux = donor_flux(speeds, dens[:-1], following(dens))
        turned = pltpu.roll(flux, 1, 2)
        before = jnp.where(lane == 0, turned[:-1], turned[1:])
        stepped = dens[1:-1] - courant * (flux[1:] - before)
        out_ref[group] = stepped.reshape(SPAN, 128)


def fill_ring(group, own_ref, mate_ref, cross_ref, far_ref, ring_ref, unit):
    odd = lax.axis_index(AZ) % 2
    places = ((own_ref, 0), (own_ref, 4), (cross_ref, 2), (mate_ref, 1 + 2 * odd), (far_ref, 3 - 2 * odd))
    for source, place in places:
        where = pl.ds(pl.multiple_of(place * unit, unit), unit)
        ring_ref[where, :] = source[group, 0:unit, :]


def shift_row(ring_ref, step, row, offset):
    start = ANGULAR_BINS - offset
    chunk = start // 128
    turn = (128 - start % 128) % 128
    lane = lax.broadcasted_iota(jnp.int32, (CHUNKS, 128), 1)
    first = ring_ref[pl.ds(chunk * step + row, CHUNKS, stride=step), :]
    second = ring_ref[pl.ds((chunk + 1) * step + row, CHUNKS, stride=step), :]
    return jnp.where(
        lane < 128 - start % 128, pltpu.roll(first, turn, 1), pltpu.roll(second, turn, 1)
    )


def shift_kernel(offs_ref, own_ref, mate_ref, cross_ref, far_ref, out_ref, ring_ref):
    @pl.loop(0, GROUPS)
    def _(group):
        fill_ring(group, own_ref, mate_ref, cross_ref, far_ref, ring_ref, SPAN)
        for row in range(8):
            moved = shift_row(ring_ref, 8, row, offs_ref[group * 8 + row])
            out_ref[group, pl.ds(row, CHUNKS, stride=8), :] = moved


def shifted(offsets, own, mate, cross, far, name):
    return pl.pallas_call(
        shift_kernel,
        out_shape=jax.ShapeDtypeStruct((GROUPS, SPAN, 128), F32),
        in_specs=[smem(), vmem(), vmem(), vmem(), vmem()],
        out_specs=vmem(),
        scratch_shapes=[pltpu.VMEM((RING, 128), F32)],
        compiler_params=params(),
        cost_estimate=cost(2),
        name=name,
    )(offsets, own, mate, cross, far)


def share_kernel(offs_ref, own_ref, mate_ref, *refs, kinds):
    odd = lax.axis_index(AZ) % 2
    sent = (own_ref, 2), (mate_ref, 3 - 2 * odd)
    kept = (own_ref, 0), (own_ref, 4), (mate_ref, 1 + 2 * odd)
    out_refs, ring_refs = refs[: len(kinds)], refs[len(kinds) :]
    for ring_ref in ring_refs:
        ring_ref[...] = jnp.zeros_like(ring_ref)

    @pl.loop(0, GROUPS)
    def _(group):
        for kind, out_ref, ring_ref in zip(kinds, out_refs, ring_refs):
            for source, place in sent if kind else kept:
                where = pl.ds(pl.multiple_of(place * SPAN, SPAN), SPAN)
                ring_ref[where, :] = source[group]
            for row in range(8):
                moved = shift_row(ring_ref, 8, row, offs_ref[group * 8 + row])
                out_ref[group, pl.ds(row, CHUNKS, stride=8), :] = moved


def share(offsets, own, mate, kinds, name):
    return pl.pallas_call(
        functools.partial(share_kernel, kinds=kinds),
        out_shape=tuple(jax.ShapeDtypeStruct((GROUPS, SPAN, 128), F32) for _ in kinds),
        in_specs=[smem(), vmem(), vmem()],
        out_specs=tuple(vmem() for _ in kinds),
        scratch_shapes=[pltpu.VMEM((RING, 128), F32) for _ in kinds],
        compiler_params=params(),
        cost_estimate=cost(2),
        name=name,
    )(offsets, own, mate)


def edge_kernel(
    offs_ref, own_ref, mate_ref, cross_ref, far_ref, first_ref, second_ref, ring_ref, flux_ref, line_ref
):
    unit = 3 * CHUNKS
    length = 5 * CHUNKS
    lane = lax.broadcasted_iota(jnp.int32, (length, 128), 1)
    sides = []
    for side in range(2):
        fill_ring(side, own_ref, mate_ref, cross_ref, far_ref, ring_ref, unit)
        ring_ref[5 * unit : 5 * unit + 24, :] = ring_ref[unit : unit + 24, :]
        offset = offs_ref[(ROWS - 1) * side]

        def following(index):
            here = pltpu.roll(ring_ref[pl.ds(index, length, stride=3), :], 127, 1)
            there = pltpu.roll(ring_ref[pl.ds(index + 3, length, stride=3), :], 127, 1)
            return jnp.where(lane == 127, there, here)

        dens = ring_ref[pl.ds(0, length, stride=3), :]
        phi = ring_ref[pl.ds(1, length, stride=3), :]
        flux = donor_flux(0.5 * (phi + following(1)), dens, following(0))
        flux_ref[8 : 8 + length, :] = flux
        before = pltpu.roll(flux_ref[7 : 7 + length, :], 1, 1)
        before = jnp.where(lane == 0, before, pltpu.roll(flux, 1, 1))
        line_ref[0:length, :] = dens - courant * (flux - before)
        sides.append((shift_row(line_ref, 1, 0, offset), shift_row(ring_ref, 3, 2, offset)))
    even = lax.axis_index(RAD) % 2 == 0
    for index in range(2):
        where = slice(CHUNKS * index, CHUNKS * index + CHUNKS)
        down, up = sides[0][index], sides[1][index]
        first_ref[where, :] = jnp.where(even, up, down)
        second_ref[where, :] = jnp.where(even, down, up)


def split_value(value):
    high = value.astype(BF16)
    return high, (value - high.astype(F32)).astype(BF16)


def dot(left, right):
    return jnp.dot(left, right, preferred_element_type=F32)


def transport_kernel(
    kept_ref, sent_ref, first_ref, second_ref, vrad_ref, high_ref, low_ref, twiddle_ref,
    whole_ref, dens_ref, spectra_ref,
    moved_ref, other_ref, speed_ref, whole_sem,
):
    for group in range(GROUPS):
        moved_ref[group] = kept_ref[group] + sent_ref[group]
    even = lax.axis_index(RAD) % 2 == 0
    first, second = first_ref[...], second_ref[...]
    for side, row in enumerate((7, 0)):
        edge = jnp.where(even, second, first) if side == 0 else jnp.where(even, first, second)
        other_ref[side, pl.ds(row, CHUNKS, stride=8), :] = edge[0:CHUNKS]
        speed_ref[side, pl.ds(row, CHUNKS, stride=8), :] = edge[CHUNKS:]

    sub = lax.broadcasted_iota(jnp.int32, (1, 8, 128), 1)
    own_index = lax.axis_index(RAD)
    bottom = own_index == 0
    top = own_index == lax.axis_size(RAD) - 1

    def above(value, following):
        return jnp.where(sub == 7, pltpu.roll(following, 7, 1), pltpu.roll(value, 7, 1))

    def below(value, previous):
        return jnp.where(sub == 0, pltpu.roll(previous, 1, 1), pltpu.roll(value, 1, 1))

    step = 4
    for group in range(GROUPS):

        @pl.loop(0, CHUNKS // step)
        def _(part):
            where = pl.ds(pl.multiple_of(part * 8 * step, 8 * step), 8 * step)

            def tiles(ref, index):
                return ref[index, where, :].reshape(step, 8, 128)

            dens = tiles(moved_ref, group)
            upper = tiles(moved_ref, group + 1) if group < 3 else tiles(other_ref, 1)
            lower = tiles(moved_ref, group - 1) if group > 0 else tiles(other_ref, 0)
            dens_above = above(dens, upper)
            dens_below = below(dens, lower)
            speed = tiles(vrad_ref, group)
            upper = tiles(vrad_ref, group + 1) if group < 3 else tiles(speed_ref, 1)
            lower = tiles(vrad_ref, group - 1) if group > 0 else tiles(speed_ref, 0)
            flux_above = donor_flux(0.5 * (speed + above(speed, upper)), dens, dens_above)
            flux_below = donor_flux(0.5 * (below(speed, lower) + speed), dens_below, dens)
            if group == 3:
                flux_above = jnp.where((sub == 7) & top, 0.0, flux_above)
            if group == 0:
                flux_below = jnp.where((sub == 0) & bottom, 0.0, flux_below)
            stepped = dens - courant * (flux_above - flux_below)
            dens_ref[group, where, :] = stepped.reshape(8 * step, 128)

    whole = pltpu.make_async_copy(dens_ref, whole_ref, whole_sem)
    whole.start()
    sector = lax.axis_index(AZ)
    cos_sum = jnp.zeros((ROWS, MODES), F32)
    sin_sum = jnp.zeros((ROWS, MODES), F32)
    together = 8
    for first in range(0, BLOCKS, together):
        pieces = []
        for block in range(first, first + together):
            halves = [
                dens_ref[:, 8 * chunk : 8 * chunk + 8, :].reshape(ROWS, 128)
                for chunk in (2 * block, 2 * block + 1)
            ]
            pieces.append(jnp.concatenate(halves, axis=1))
        high, low = split_value(jnp.concatenate(pieces, axis=0))
        part = dot(high, high_ref[...]) + (dot(low, high_ref[...]) + dot(high, low_ref[...]))
        for index in range(together):
            turn = twiddle_ref[pl.ds(sector * BLOCKS + first + index, 1), :]
            cosine, sine = turn[:, :MODES], turn[:, MODES:]
            rows = slice(index * ROWS, index * ROWS + ROWS)
            cos_part, sin_part = part[rows, :MODES], part[rows, MODES:]
            cos_sum += cosine * cos_part - sine * sin_part
            sin_sum += sine * cos_part + cosine * sin_part
    spectra_ref[:, :MODES] = cos_sum * cell_step
    spectra_ref[:, MODES:] = sin_sum * cell_step
    whole.wait()


def field_kernel(members_ref, radius_ref, angles_ref, *refs, second):
    radial_ref, azim_ref, gap_ref, chord_ref, lift_ref, side_ref = refs[-6:]
    many = CHUNKS // 2
    base = many * second
    if second:
        rows = slice(0, 8 * base)
        radial_ref[:, rows, :] = refs[0][:, rows, :]
        azim_ref[:, rows, :] = refs[1][:, rows, :]
    sector = lax.axis_index(AZ)
    half_cos = angles_ref[sector * 4, base : base + many, :]
    half_sin = angles_ref[sector * 4 + 1, base : base + many, :]
    radius = radius_ref[...]
    halves = 0.5 / radius

    @pl.loop(0, EMB, unroll=4)
    def _(member):
        embryo_radius = members_ref[0, member]
        scale = members_ref[1, member]
        cosine = members_ref[2, member]
        sine = members_ref[3, member]
        gap = radius - embryo_radius
        soft = softening * embryo_radius
        rows = pl.ds(pl.multiple_of(member * 32, 32), 32)
        gap_ref[rows, :] = (gap * gap + soft * soft) * halves * scale
        near = half_sin * cosine - half_cos * sine
        far = half_cos * cosine + half_sin * sine
        chord = (2.0 * embryo_radius) * (near * near)
        columns = pl.ds(pl.multiple_of(member * many, many), many)
        chord_ref[columns, :] = chord * scale
        lift_ref[columns, :] = chord - embryo_radius
        side_ref[columns, :] = (2.0 * embryo_radius) * (near * far)

    pieces = [radius[8 * g : 8 * g + 8] for g in range(GROUPS)]
    ends = []
    for g in range(GROUPS):
        root = lax.rsqrt(2.0 * pieces[g])
        ends.append(root * root * root)
    together = 2

    @pl.loop(0, many // together)
    def _(part):
        zero = jnp.zeros((8, 128), F32)

        def visit(member, carried):
            radial, azim = list(carried[0]), list(carried[1])
            rows = []
            for k in range(together):
                row = pl.ds(member * many + part * together + k, 1)
                rows.append(
                    [jnp.broadcast_to(ref[row, :], (8, 128)) for ref in (chord_ref, lift_ref, side_ref)]
                )
            for g in range(GROUPS):
                gap = gap_ref[pl.ds(pl.multiple_of(member * 32 + 8 * g, 8), 8), :]
                for k in range(together):
                    chord, lift, side = rows[k]
                    inverse = lax.rsqrt(gap + chord)
                    cubed = inverse * inverse * inverse
                    at = k * GROUPS + g
                    radial[at] = radial[at] + cubed * (pieces[g] + lift)
                    azim[at] = azim[at] + cubed * side
            return tuple(radial), tuple(azim)

        count = together * GROUPS
        radial, azim = lax.fori_loop(0, EMB, visit, ((zero,) * count, (zero,) * count), unroll=8)
        for k in range(together):
            where = pl.ds(pl.multiple_of((base + part * together + k) * 8, 8), 8)
            for g in range(GROUPS):
                radial_ref[g, where, :] = radial[k * GROUPS + g] * ends[g]
                azim_ref[g, where, :] = azim[k * GROUPS + g] * ends[g]


def push_kernel(
    members_ref, radius_ref, angles_ref, dens_ref, spectra_ref, out_ref, mass_ref, chord_ref, push_ref
):
    for part in range(4):
        out_ref[ROWS * part : ROWS * part + ROWS, :] = spectra_ref[:, 128 * part : 128 * part + 128]
    sector = lax.axis_index(AZ)
    radius = radius_ref[...]
    pieces = [radius[8 * g : 8 * g + 8] for g in range(GROUPS)]
    halves = [0.5 / piece for piece in pieces]
    for g in range(GROUPS):
        scale = lax.rsqrt(2.0 * pieces[g])
        area = pieces[g] * pieces[g] * (cell_step * cell_step) * (scale * scale * scale)
        mass_ref[g] = (dens_ref[g].reshape(CHUNKS, 8, 128) * area[None]).reshape(SPAN, 128)
    half_cos = angles_ref[sector * 4]
    half_sin = angles_ref[sector * 4 + 1]

    @pl.loop(0, EMB)
    def _(member):
        embryo_radius = members_ref[0, member]
        cosine = members_ref[2, member]
        sine = members_ref[3, member]
        soft = softening * embryo_radius
        gaps = []
        for g in range(GROUPS):
            gap = pieces[g] - embryo_radius
            gaps.append((gap * gap + soft * soft) * halves[g])
        near = half_sin * cosine - half_cos * sine
        chord_ref[...] = (2.0 * embryo_radius) * (near * near)
        push_x = jnp.zeros((8, 128), F32)
        push_y = jnp.zeros((8, 128), F32)
        total = jnp.zeros((8, 128), F32)
        for chunk in range(CHUNKS):
            chord = jnp.broadcast_to(chord_ref[chunk : chunk + 1, :], (8, 128))
            plain, moved = None, None
            for g in range(GROUPS):
                inverse = lax.rsqrt(gaps[g] + chord)
                cubed = inverse * inverse * inverse
                term = cubed * mass_ref[g, 8 * chunk : 8 * chunk + 8, :]
                plain = term if g == 0 else plain + term
                moved = pieces[g] * term if g == 0 else moved + pieces[g] * term
            row = slice(chunk, chunk + 1)
            push_x = push_x + moved * jnp.broadcast_to(angles_ref[sector * 4 + 2, row, :], (8, 128))
            push_y = push_y + moved * jnp.broadcast_to(angles_ref[sector * 4 + 3, row, :], (8, 128))
            total = total + plain
        place_x = embryo_radius * members_ref[4, member]
        place_y = embryo_radius * members_ref[5, member]
        push_ref[pl.ds(member, 1), :] = jnp.sum(push_x - place_x * total, axis=0, keepdims=True)
        push_ref[pl.ds(EMB + member, 1), :] = jnp.sum(push_y - place_y * total, axis=0, keepdims=True)

    push = jnp.broadcast_to(jnp.sum(push_ref[...], axis=1, keepdims=True), (2 * EMB, 128))
    row = lax.broadcasted_iota(jnp.int32, (2 * EMB, 128), 0)
    lane = lax.broadcasted_iota(jnp.int32, (2 * EMB, 128), 1)
    push = jnp.sum(jnp.where(row == lane, push, 0.0), axis=0, keepdims=True)
    out_ref[4 * ROWS : 4 * ROWS + 8, :] = jnp.broadcast_to(push, (8, 128))


def moment_kernel(a_ref, b_ref, lift_ref, drop_ref, vectors_ref, spectra_ref, packed_ref, one_ref):
    total = a_ref[...] + b_ref[...]
    for part in range(4):
        columns = slice(128 * part, 128 * part + 128)
        spectra = total[ROWS * part : ROWS * part + ROWS]
        spectra_ref[:, columns] = spectra
        factor = vectors_ref[0:1, columns]
        up = jnp.sum(spectra * drop_ref[:, columns], axis=0, keepdims=True) / factor
        down = jnp.sum(spectra * lift_ref[:, columns], axis=0, keepdims=True) / factor
        one_ref[part : part + 1, :] = up
        one_ref[4 + part : 5 + part, :] = down
    one_ref[8:16, :] = total[4 * ROWS :]
    one = one_ref[...]
    for copy in range(packed_ref.shape[0]):
        packed_ref[copy] = one


def kick_kernel(
    spectra_ref, moments_ref, rate_ref, radius_ref, vectors_ref, lift_ref, drop_ref, twiddle_ref, high_ref, low_ref,
    radial_ref, azim_ref, vrad_ref, vphi_kept_ref, vphi_sent_ref,
    whole_radial_ref, whole_azim_ref, out_push_ref,
    lower_ref, upper_ref, out_radial_ref, out_azim_ref, sems,
):
    own_index = lax.axis_index(RAD)
    row = lax.broadcasted_iota(jnp.int32, (8, 128), 0)
    outside = jnp.zeros((8, 128), F32)
    push = jnp.zeros((1, 128), F32)
    for source in range(moments_ref.shape[0]):
        many = jnp.where(row < 4, own_index - 1 - source, source - own_index - 1)
        weight = jnp.exp(-rate_ref[...] * jnp.maximum(many, 0).astype(F32))
        outside += jnp.where(many >= 0, weight, 0.0) * moments_ref[source, 0:8, :]
        push += moments_ref[source, 8:9, :]
    out_push_ref[0:1, :] = push[:, :EMB]
    out_push_ref[1:2, :] = push[:, EMB : 2 * EMB]
    lower = jnp.concatenate([outside[k : k + 1] for k in range(4)], axis=1)
    upper = jnp.concatenate([outside[k : k + 1] for k in range(4, 8)], axis=1)
    factor = vectors_ref[0:1, :]
    spectra = spectra_ref[...]
    for row in range(ROWS):
        lower = spectra[row : row + 1] + factor * lower
        lower_ref[row : row + 1, :] = lower
        back = ROWS - 1 - row
        upper = spectra[back : back + 1] + factor * upper
        upper_ref[back : back + 1, :] = upper
    lower = lower_ref[...]
    upper = upper_ref[...]
    inverse = 1.0 / radius_ref[:, 0:1]
    even = lower + upper - spectra
    odd = lower - upper
    radial = odd * vectors_ref[1:2, :] * inverse
    swapped = jnp.concatenate([even[:, MODES:], even[:, :MODES]], axis=1)
    azim = swapped * vectors_ref[2:3, :] * inverse
    sector = lax.axis_index(AZ)
    together = 4

    def whole_copies(quarter):
        rows = pl.ds(pl.multiple_of(16 * together * quarter, 16 * together), 16 * together)
        return [
            pltpu.make_async_copy(source.at[:, rows, :], target.at[:, rows, :], sems.at[index, quarter])
            for index, (source, target) in enumerate(
                ((out_radial_ref, whole_radial_ref), (out_azim_ref, whole_azim_ref))
            )
        ]

    @pl.loop(0, BLOCKS // together)
    def _(quarter):
        pieces = []
        for index in range(together):
            turn = twiddle_ref[pl.ds(sector * BLOCKS + quarter * together + index, 1), :]
            cosine, sine = turn[:, :MODES], turn[:, MODES:]
            for coef in (radial, azim):
                cos_coef, sin_coef = coef[:, :MODES], coef[:, MODES:]
                pieces.append(
                    jnp.concatenate(
                        [cos_coef * cosine + sin_coef * sine, sin_coef * cosine - cos_coef * sine], axis=1
                    )
                )
        high, low = split_value(jnp.concatenate(pieces, axis=0))
        part = dot(high, high_ref[...]) + (dot(low, high_ref[...]) + dot(high, low_ref[...]))
        for index in range(together):
            for half in range(2):
                start = 16 * together * quarter + 8 * (2 * index + half)
                where = pl.ds(pl.multiple_of(start, 8), 8)
                columns = slice(128 * half, 128 * half + 128)
                rows = 2 * ROWS * index
                disk = part[rows : rows + ROWS, columns].reshape(GROUPS, 8, 128)
                out_radial_ref[:, where, :] = vrad_ref[:, where, :] + timestep_length * (
                    disk - radial_ref[:, where, :]
                )
                disk = part[rows + ROWS : rows + 2 * ROWS, columns].reshape(GROUPS, 8, 128)
                vphi = vphi_kept_ref[:, where, :] + vphi_sent_ref[:, where, :]
                out_azim_ref[:, where, :] = vphi + timestep_length * (
                    disk - azim_ref[:, where, :]
                )
        for copy in whole_copies(quarter):
            copy.start()

    for quarter in range(BLOCKS // together):
        for copy in whole_copies(quarter):
            copy.wait()


def across(value, axis, target):
    count = lax.axis_size(axis)
    return lax.ppermute(value, axis, [(source, target(source)) for source in range(count)])


def after(value, *others):
    return lax.optimization_barrier((value, *others))[0]


def on_device(
    surface_mass,
    outward_drift,
    leftover_angular_drift,
    angular_offsets,
    planetesimal_loop_number,
    planetesimal_angle_bin,
    planetesimal_weights,
):
    (basis_high, basis_low), (back_high, back_low), twiddle, angles, lift, drop, vectors, rate = (
        constant_tables()
    )
    tiles = jax.ShapeDtypeStruct((GROUPS, SPAN, 128), F32)
    dens = to_tiles(surface_mass)
    vrad = to_tiles(outward_drift)
    vphi = to_tiles(leftover_angular_drift)

    halo = jax.ShapeDtypeStruct((2 * GROUPS, 8, 128), F32)
    outer, inner, edge_rows = pl.pallas_call(
        border_kernel,
        out_shape=(halo, halo, jax.ShapeDtypeStruct((2, 3 * CHUNKS, 128), F32)),
        in_specs=[pl.BlockSpec(memory_space=pltpu.HBM)] * 3,
        out_specs=(vmem(), vmem(), vmem()),
        scratch_shapes=[pltpu.VMEM((6, SPAN, 128), F32), pltpu.SemaphoreType.DMA((10,))],
        compiler_params=params(),
        cost_estimate=cost(1),
        name="borders",
    )(hbm(dens), hbm(vphi), hbm(vrad))
    border_far = across(outer, AZ, lambda i: i ^ 3)
    border_mate = across(inner, AZ, lambda i: i ^ 1)
    edge_cross = across(edge_rows, AZ, lambda i: i ^ 2)
    edge_mate = across(edge_rows, AZ, lambda i: i ^ 1)
    vrad_cross = across(after(vrad, edge_rows), AZ, lambda i: i ^ 2)
    vrad_mate = across(vrad, AZ, lambda i: i ^ 1)

    cell = np.float32(cell_step)
    cycles = lax.axis_index(RAD) * ROWS + jnp.arange(ROWS, dtype=jnp.int32)
    radius = jnp.broadcast_to(jnp.exp((cycles.astype(F32) + 0.5) * cell)[:, None], (ROWS, 128))
    embryo_angles = (2 * planetesimal_angle_bin + 1).astype(F32) * np.float32(np.pi / ANGULAR_BINS)
    members = jnp.stack(
        [
            jnp.exp((planetesimal_loop_number.astype(F32) + 0.5) * cell),
            jnp.exp(np.float32(-2.0 / 3.0) * jnp.log(planetesimal_weights)),
            jnp.cos(0.5 * embryo_angles),
            jnp.sin(0.5 * embryo_angles),
            jnp.cos(embryo_angles),
            jnp.sin(embryo_angles),
        ]
    )

    dens_two = pl.pallas_call(
        azimuth_kernel,
        out_shape=tiles,
        in_specs=[pl.BlockSpec(memory_space=pltpu.HBM)] * 2 + [vmem()] * 2,
        out_specs=vmem(),
        scratch_shapes=[
            pltpu.VMEM((GROUPS, SPAN, 128), F32),
            pltpu.VMEM((GROUPS, SPAN, 128), F32),
            pltpu.SemaphoreType.DMA((8,)),
        ],
        compiler_params=params(),
        cost_estimate=cost(1),
        name="azimuth",
    )(hbm(dens), hbm(vphi), border_mate, border_far)

    edge_far = across(edge_cross, AZ, lambda i: i ^ 1)
    edge = jax.ShapeDtypeStruct((2 * CHUNKS, 128), F32)
    edge_first, edge_second = pl.pallas_call(
        edge_kernel,
        out_shape=(edge, edge),
        in_specs=[smem()] + [vmem()] * 4,
        out_specs=(vmem(), vmem()),
        scratch_shapes=[
            pltpu.VMEM((3 * RING // 8, 128), F32),
            pltpu.VMEM((RING // 8 + 8, 128), F32),
            pltpu.VMEM((RING // 8, 128), F32),
        ],
        compiler_params=params(),
        cost_estimate=cost(1),
        name="edges",
    )(angular_offsets, edge_rows, edge_mate, edge_cross, edge_far)
    rad_count = lax.axis_size(RAD)
    inside = range(1, rad_count - 1)
    edge_second = lax.ppermute(edge_second, RAD, [(i, i + 1 if i % 2 else i - 1) for i in inside])
    edge_first_in = across(edge_first, RAD, lambda i: i ^ 1)

    def field(second, *before):
        return pl.pallas_call(
            functools.partial(field_kernel, second=second),
            out_shape=(tiles, tiles),
            in_specs=[smem(), vmem(), vmem()] + [vmem()] * len(before),
            out_specs=(vmem(), vmem()),
            scratch_shapes=[pltpu.VMEM((EMB * 32, 128), F32)] + [pltpu.VMEM((EMB * 16, 128), F32)] * 3,
            compiler_params=params(),
            cost_estimate=cost(4),
            name=f"field_{second}",
        )(members, radius, angles, *before)

    first_field = field(0)
    dens_mate = across(dens_two, AZ, lambda i: i ^ 1)
    (dens_sent,) = share(angular_offsets, dens_two, dens_mate, (True,), "share_dens")
    vphi_mate = across(vphi, AZ, lambda i: i ^ 1)
    vphi_sent, vphi_kept = share(angular_offsets, vphi, vphi_mate, (True, False), "share_vphi")
    early = (dens_sent, *first_field, edge_first, vphi_sent, vphi_kept)
    vrad_far = across(after(vrad_cross, *early), AZ, lambda i: i ^ 1)
    dens_cross = across(after(dens_sent, vrad_cross, *early), AZ, lambda i: i ^ 2)
    (dens_kept,) = share(angular_offsets, dens_two, dens_mate, (False,), "keep_dens")
    vrad_one = shifted(angular_offsets, vrad, vrad_mate, vrad_cross, vrad_far, "shift_vrad")
    radial_field, azim_field = field(1, *first_field)
    dens_cross = after(
        dens_cross, vrad_one, radial_field, dens_kept, vphi_sent, vphi_kept, edge_first_in, edge_second
    )
    vphi_cross = across(after(vphi_sent, vrad_cross), AZ, lambda i: i ^ 2)

    transported, stepped, part = pl.pallas_call(
        transport_kernel,
        out_shape=(tiles, tiles, jax.ShapeDtypeStruct((ROWS, 2 * MODES), F32)),
        in_specs=[vmem()] * 8,
        out_specs=(anywhere(), vmem(), vmem()),
        scratch_shapes=[
            pltpu.VMEM((GROUPS, SPAN, 128), F32),
            pltpu.VMEM((2, SPAN, 128), F32),
            pltpu.VMEM((2, SPAN, 128), F32),
            pltpu.SemaphoreType.DMA,
        ],
        compiler_params=params(),
        cost_estimate=cost(3),
        name="transport",
    )(
        dens_kept, dens_cross, edge_first_in, edge_second,
        vrad_one, basis_high, basis_low, twiddle,
    )

    joined_shape = jax.ShapeDtypeStruct((4 * ROWS + 8, 128), F32)
    joined = pl.pallas_call(
        push_kernel,
        out_shape=joined_shape,
        in_specs=[smem()] + [vmem()] * 4,
        out_specs=vmem(),
        scratch_shapes=[
            pltpu.VMEM((GROUPS, SPAN, 128), F32),
            pltpu.VMEM((CHUNKS, 128), F32),
            pltpu.VMEM((2 * EMB, 128), F32),
        ],
        compiler_params=params(),
        cost_estimate=cost(6),
        name="push",
    )(members, radius, angles, stepped, part)
    chip = joined + across(joined, AZ, lambda i: i ^ 1)
    chip_other = across(chip, AZ, lambda i: i ^ 2)

    chip_later = after(chip, vphi_cross)
    spectra, packed = pl.pallas_call(
        moment_kernel,
        out_shape=(
            jax.ShapeDtypeStruct((ROWS, 2 * MODES), F32),
            jax.ShapeDtypeStruct((rad_count, 16, 128), F32),
        ),
        in_specs=[vmem()] * 5,
        out_specs=(vmem(), vmem()),
        scratch_shapes=[pltpu.VMEM((16, 128), F32)],
        compiler_params=params(),
        cost_estimate=cost(1),
        name="moments",
    )(chip_later, chip_other, lift, drop, vectors)
    gathered = lax.all_to_all(packed, RAD, split_axis=0, concat_axis=0, tiled=True)

    kicked_radial, kicked_azim, embryo_disk_acceleration = pl.pallas_call(
        kick_kernel,
        out_shape=(tiles, tiles, jax.ShapeDtypeStruct((2, EMB), F32)),
        in_specs=[vmem()] * 15,
        out_specs=(anywhere(), anywhere(), vmem()),
        scratch_shapes=[
            pltpu.VMEM((ROWS, 2 * MODES), F32),
            pltpu.VMEM((ROWS, 2 * MODES), F32),
            pltpu.VMEM((GROUPS, SPAN, 128), F32),
            pltpu.VMEM((GROUPS, SPAN, 128), F32),
            pltpu.SemaphoreType.DMA((2, 4)),
        ],
        compiler_params=params(),
        cost_estimate=cost(5),
        name="kick",
    )(
        spectra, gathered, rate, radius, vectors, lift, drop, twiddle, back_high, back_low,
        radial_field, azim_field, vrad_one, vphi_kept, vphi_cross,
    )
    return (
        from_tiles(transported),
        from_tiles(kicked_radial),
        from_tiles(kicked_azim),
        embryo_disk_acceleration,
    )


def solution(mesh):
    torus = Mesh(mesh.devices.reshape(4, 2, 4, 2, 2), RAD + AZ)
    placed = (P(RAD, AZ), P(RAD, AZ), P(RAD, AZ), P(RAD), P(), P(), P())
    return jax.shard_map(
        on_device,
        mesh=torus,
        in_specs=placed,
        out_specs=(P(RAD, AZ), P(RAD, AZ), P(RAD, AZ), P()),
        check_vma=False,
    )
```

```python
import functools

import jax
import jax.numpy as jnp
import ml_dtypes
import numpy as np
from jax import lax
from jax.experimental import pallas as pl
from jax.experimental.pallas import tpu as pltpu
from jax.sharding import Mesh
from jax.sharding import PartitionSpec as P

ANGULAR_BINS = 16384
MODES = 256
EMB = 32
RAD = ("rad_0", "rad_1", "rad_2")
AZ = ("az_0", "az_1")
F32 = jnp.float32
BF16 = jnp.bfloat16

gravity = 1.0
timestep_length = 0.05
courant = 0.4
softening = 0.02
cell_step = 2.0 * np.pi / ANGULAR_BINS

ROWS = 32
CHUNKS = 32
GROUPS = 4
SPAN = 8 * CHUNKS
RING = 8 * (5 * CHUNKS + 8)
WIDE = 256
BLOCKS = 16


def split_bf16(table):
    high = table.astype(np.float32).astype(ml_dtypes.bfloat16)
    low = (table - high.astype(np.float64)).astype(np.float32).astype(ml_dtypes.bfloat16)
    return high, low


def constant_tables():
    orders = np.arange(MODES)
    inner = np.arange(WIDE)
    phases = orders[None, :] * (2 * inner[:, None] + 1) % (2 * ANGULAR_BINS) * (np.pi / ANGULAR_BINS)
    basis = np.concatenate([np.cos(phases), np.sin(phases)], axis=1)
    starts = np.arange(ANGULAR_BINS // WIDE) * WIDE
    turns = orders[None, :] * starts[:, None] % ANGULAR_BINS * (2 * np.pi / ANGULAR_BINS)
    twiddle = np.concatenate([np.cos(turns), np.sin(turns)], axis=1).astype(np.float32)
    halves = (2 * np.arange(ANGULAR_BINS) + 1) * (0.5 * np.pi / ANGULAR_BINS)
    wholes = 2 * halves
    angles = np.stack([np.cos(halves), np.sin(halves), np.cos(wholes), np.sin(wholes)])
    angles = angles.reshape(4, 4, CHUNKS, 128).transpose(1, 0, 2, 3).reshape(16, CHUNKS, 128)
    decays = np.tile((orders + 0.5) * cell_step, 2)
    rows = np.arange(ROWS)
    lift = np.exp(-decays[None, :] * (rows[:, None] + 1))
    drop = np.exp(-decays[None, :] * (ROWS - rows[:, None]))
    doubled = np.tile(np.where(orders > 0, 2.0, 1.0), 2)
    radial = -(gravity / cell_step) * doubled * decays * decays
    azim = gravity * np.concatenate([orders * doubled[:MODES], -orders * doubled[:MODES]])
    azim = azim * decays
    vectors = np.zeros((8, 2 * MODES))
    vectors[0] = np.exp(-decays)
    vectors[1] = radial
    vectors[2] = azim
    return (
        split_bf16(basis),
        split_bf16(basis.T),
        twiddle,
        angles.astype(np.float32),
        lift.astype(np.float32),
        drop.astype(np.float32),
        vectors.astype(np.float32),
        np.tile((decays * ROWS).astype(np.float32).reshape(4, 128), (2, 1)),
    )


def to_tiles(value):
    return value.reshape(GROUPS, 8, CHUNKS, 128).transpose(0, 2, 1, 3).reshape(GROUPS, SPAN, 128)


def from_tiles(value):
    return value.reshape(GROUPS, CHUNKS, 8, 128).transpose(0, 2, 1, 3).reshape(ROWS, CHUNKS * 128)


def vmem():
    return pl.BlockSpec(memory_space=pltpu.VMEM)


def smem():
    return pl.BlockSpec(memory_space=pltpu.SMEM)


def anywhere():
    return pl.BlockSpec(memory_space=pl.ANY)


def hbm(value):
    return pltpu.with_memory_space_constraint(value, pltpu.HBM)


def params():
    return pltpu.CompilerParams(vmem_limit_bytes=14 * 1024 * 1024)


def cost(us):
    return pl.CostEstimate(flops=int(us * 1e6), bytes_accessed=int(us * 2.5e6), transcendentals=0)


def donor_flux(speeds, upstream, downstream):
    return jnp.where(speeds > 0, speeds * upstream, speeds * downstream)


def border_kernel(dens_ref, phi_ref, vrad_ref, outer_ref, inner_ref, out_ref, buf_ref, sems):
    odd = lax.axis_index(AZ) % 2
    copies = []
    for index, ref in enumerate((dens_ref, phi_ref)):
        where = slice(GROUPS * index, GROUPS * index + GROUPS)
        outer = pl.ds(pl.multiple_of(odd * (SPAN - 8), 8), 8)
        inner = pl.ds(pl.multiple_of((1 - odd) * (SPAN - 8), 8), 8)
        copies.append((ref.at[:, outer, :], outer_ref.at[where]))
        copies.append((ref.at[:, inner, :], inner_ref.at[where]))
    for index, ref in enumerate((dens_ref, phi_ref, vrad_ref)):
        for side, group in enumerate((0, GROUPS - 1)):
            copies.append((ref.at[group], buf_ref.at[2 * index + side]))
    copies = [pltpu.make_async_copy(*copy, sems.at[index]) for index, copy in enumerate(copies)]
    for copy in copies:
        copy.start()
    for copy in copies:
        copy.wait()
    for side, row in enumerate((0, 7)):
        for index in range(3):
            rows = buf_ref[2 * index + side, pl.ds(row, CHUNKS, stride=8), :]
            out_ref[side, pl.ds(index, CHUNKS, stride=3), :] = rows


def azimuth_kernel(dens_ref, phi_ref, mate_ref, far_ref, out_ref, dens_buf, phi_buf, sems):
    lane = lax.broadcasted_iota(jnp.int32, (1, 8, 128), 2)
    copies = []
    for group in range(GROUPS):
        copies.append(
            (
                pltpu.make_async_copy(dens_ref.at[group], dens_buf.at[group], sems.at[2 * group]),
                pltpu.make_async_copy(phi_ref.at[group], phi_buf.at[group], sems.at[2 * group + 1]),
            )
        )
    for pair in copies:
        for copy in pair:
            copy.start()

    odd = lax.axis_index(AZ) % 2 == 1

    def following(value):
        turned = pltpu.roll(value, 127, 2)
        return jnp.where(lane == 127, turned[1:], turned[:-1])

    def widened(ref, group, base):
        middle = ref[group].reshape(CHUNKS, 8, 128)
        mate, far = mate_ref[base + group][None], far_ref[base + group][None]
        return jnp.concatenate(
            [jnp.where(odd, mate, far), middle, jnp.where(odd, far, mate)], axis=0
        )

    for group in range(GROUPS):
        for copy in copies[group]:
            copy.wait()
        dens = widened(dens_buf, group, 0)
        phi = widened(phi_buf, group, GROUPS)
        speeds = 0.5 * (phi[:-1] + following(phi))
        flux = donor_flux(speeds, dens[:-1], following(dens))
        turned = pltpu.roll(flux, 1, 2)
        before = jnp.where(lane == 0, turned[:-1], turned[1:])
        stepped = dens[1:-1] - courant * (flux[1:] - before)
        out_ref[group] = stepped.reshape(SPAN, 128)


def fill_ring(group, own_ref, mate_ref, cross_ref, far_ref, ring_ref, unit):
    odd = lax.axis_index(AZ) % 2
    places = ((own_ref, 0), (own_ref, 4), (cross_ref, 2), (mate_ref, 1 + 2 * odd), (far_ref, 3 - 2 * odd))
    for source, place in places:
        where = pl.ds(pl.multiple_of(place * unit, unit), unit)
        ring_ref[where, :] = source[group, 0:unit, :]


def shift_row(ring_ref, step, row, offset):
    start = ANGULAR_BINS - offset
    chunk = start // 128
    turn = (128 - start % 128) % 128
    lane = lax.broadcasted_iota(jnp.int32, (CHUNKS, 128), 1)
    first = ring_ref[pl.ds(chunk * step + row, CHUNKS, stride=step), :]
    second = ring_ref[pl.ds((chunk + 1) * step + row, CHUNKS, stride=step), :]
    return jnp.where(
        lane < 128 - start % 128, pltpu.roll(first, turn, 1), pltpu.roll(second, turn, 1)
    )


def shift_kernel(offs_ref, own_ref, mate_ref, cross_ref, far_ref, out_ref, ring_ref):
    @pl.loop(0, GROUPS)
    def _(group):
        fill_ring(group, own_ref, mate_ref, cross_ref, far_ref, ring_ref, SPAN)
        for row in range(8):
            moved = shift_row(ring_ref, 8, row, offs_ref[group * 8 + row])
            out_ref[group, pl.ds(row, CHUNKS, stride=8), :] = moved


def shifted(offsets, own, mate, cross, far, name):
    return pl.pallas_call(
        shift_kernel,
        out_shape=jax.ShapeDtypeStruct((GROUPS, SPAN, 128), F32),
        in_specs=[smem(), vmem(), vmem(), vmem(), vmem()],
        out_specs=vmem(),
        scratch_shapes=[pltpu.VMEM((RING, 128), F32)],
        compiler_params=params(),
        cost_estimate=cost(2),
        name=name,
    )(offsets, own, mate, cross, far)


def share_kernel(offs_ref, own_ref, mate_ref, *refs, kinds):
    odd = lax.axis_index(AZ) % 2
    sent = (own_ref, 2), (mate_ref, 3 - 2 * odd)
    kept = (own_ref, 0), (own_ref, 4), (mate_ref, 1 + 2 * odd)
    out_refs, ring_refs = refs[: len(kinds)], refs[len(kinds) :]
    for ring_ref in ring_refs:
        ring_ref[...] = jnp.zeros_like(ring_ref)

    @pl.loop(0, GROUPS)
    def _(group):
        for kind, out_ref, ring_ref in zip(kinds, out_refs, ring_refs):
            for source, place in sent if kind else kept:
                where = pl.ds(pl.multiple_of(place * SPAN, SPAN), SPAN)
                ring_ref[where, :] = source[group]
            for row in range(8):
                moved = shift_row(ring_ref, 8, row, offs_ref[group * 8 + row])
                out_ref[group, pl.ds(row, CHUNKS, stride=8), :] = moved


def share(offsets, own, mate, kinds, name):
    return pl.pallas_call(
        functools.partial(share_kernel, kinds=kinds),
        out_shape=tuple(jax.ShapeDtypeStruct((GROUPS, SPAN, 128), F32) for _ in kinds),
        in_specs=[smem(), vmem(), vmem()],
        out_specs=tuple(vmem() for _ in kinds),
        scratch_shapes=[pltpu.VMEM((RING, 128), F32) for _ in kinds],
        compiler_params=params(),
        cost_estimate=cost(2),
        name=name,
    )(offsets, own, mate)


def edge_kernel(
    offs_ref, own_ref, mate_ref, cross_ref, far_ref, first_ref, second_ref, ring_ref, flux_ref, line_ref
):
    unit = 3 * CHUNKS
    length = 5 * CHUNKS
    lane = lax.broadcasted_iota(jnp.int32, (length, 128), 1)
    sides = []
    for side in range(2):
        fill_ring(side, own_ref, mate_ref, cross_ref, far_ref, ring_ref, unit)
        ring_ref[5 * unit : 5 * unit + 24, :] = ring_ref[unit : unit + 24, :]
        offset = offs_ref[(ROWS - 1) * side]

        def following(index):
            here = pltpu.roll(ring_ref[pl.ds(index, length, stride=3), :], 127, 1)
            there = pltpu.roll(ring_ref[pl.ds(index + 3, length, stride=3), :], 127, 1)
            return jnp.where(lane == 127, there, here)

        dens = ring_ref[pl.ds(0, length, stride=3), :]
        phi = ring_ref[pl.ds(1, length, stride=3), :]
        flux = donor_flux(0.5 * (phi + following(1)), dens, following(0))
        flux_ref[8 : 8 + length, :] = flux
        before = pltpu.roll(flux_ref[7 : 7 + length, :], 1, 1)
        before = jnp.where(lane == 0, before, pltpu.roll(flux, 1, 1))
        line_ref[0:length, :] = dens - courant * (flux - before)
        sides.append((shift_row(line_ref, 1, 0, offset), shift_row(ring_ref, 3, 2, offset)))
    even = lax.axis_index(RAD) % 2 == 0
    for index in range(2):
        where = slice(CHUNKS * index, CHUNKS * index + CHUNKS)
        down, up = sides[0][index], sides[1][index]
        first_ref[where, :] = jnp.where(even, up, down)
        second_ref[where, :] = jnp.where(even, down, up)


def split_value(value):
    high = value.astype(BF16)
    return high, (value - high.astype(F32)).astype(BF16)


def dot(left, right):
    return jnp.dot(left, right, preferred_element_type=F32)


def transport_kernel(
    kept_ref, sent_ref, first_ref, second_ref, vrad_ref, high_ref, low_ref, twiddle_ref,
    whole_ref, dens_ref, spectra_ref,
    moved_ref, other_ref, speed_ref, whole_sem,
):
    for group in range(GROUPS):
        moved_ref[group] = kept_ref[group] + sent_ref[group]
    even = lax.axis_index(RAD) % 2 == 0
    first, second = first_ref[...], second_ref[...]
    for side, row in enumerate((7, 0)):
        edge = jnp.where(even, second, first) if side == 0 else jnp.where(even, first, second)
        other_ref[side, pl.ds(row, CHUNKS, stride=8), :] = edge[0:CHUNKS]
        speed_ref[side, pl.ds(row, CHUNKS, stride=8), :] = edge[CHUNKS:]

    sub = lax.broadcasted_iota(jnp.int32, (1, 8, 128), 1)
    own_index = lax.axis_index(RAD)
    bottom = own_index == 0
    top = own_index == lax.axis_size(RAD) - 1

    def above(value, following):
        return jnp.where(sub == 7, pltpu.roll(following, 7, 1), pltpu.roll(value, 7, 1))

    def below(value, previous):
        return jnp.where(sub == 0, pltpu.roll(previous, 1, 1), pltpu.roll(value, 1, 1))

    step = 4
    for group in range(GROUPS):

        @pl.loop(0, CHUNKS // step)
        def _(part):
            where = pl.ds(pl.multiple_of(part * 8 * step, 8 * step), 8 * step)

            def tiles(ref, index):
                return ref[index, where, :].reshape(step, 8, 128)

            dens = tiles(moved_ref, group)
            upper = tiles(moved_ref, group + 1) if group < 3 else tiles(other_ref, 1)
            lower = tiles(moved_ref, group - 1) if group > 0 else tiles(other_ref, 0)
            dens_above = above(dens, upper)
            dens_below = below(dens, lower)
            speed = tiles(vrad_ref, group)
            upper = tiles(vrad_ref, group + 1) if group < 3 else tiles(speed_ref, 1)
            lower = tiles(vrad_ref, group - 1) if group > 0 else tiles(speed_ref, 0)
            flux_above = donor_flux(0.5 * (speed + above(speed, upper)), dens, dens_above)
            flux_below = donor_flux(0.5 * (below(speed, lower) + speed), dens_below, dens)
            if group == 3:
                flux_above = jnp.where((sub == 7) & top, 0.0, flux_above)
            if group == 0:
                flux_below = jnp.where((sub == 0) & bottom, 0.0, flux_below)
            stepped = dens - courant * (flux_above - flux_below)
            dens_ref[group, where, :] = stepped.reshape(8 * step, 128)

    whole = pltpu.make_async_copy(dens_ref, whole_ref, whole_sem)
    whole.start()
    sector = lax.axis_index(AZ)
    cos_sum = jnp.zeros((ROWS, MODES), F32)
    sin_sum = jnp.zeros((ROWS, MODES), F32)
    together = 8
    for first in range(0, BLOCKS, together):
        pieces = []
        for block in range(first, first + together):
            halves = [
                dens_ref[:, 8 * chunk : 8 * chunk + 8, :].reshape(ROWS, 128)
                for chunk in (2 * block, 2 * block + 1)
            ]
            pieces.append(jnp.concatenate(halves, axis=1))
        high, low = split_value(jnp.concatenate(pieces, axis=0))
        part = dot(high, high_ref[...]) + (dot(low, high_ref[...]) + dot(high, low_ref[...]))
        for index in range(together):
            turn = twiddle_ref[pl.ds(sector * BLOCKS + first + index, 1), :]
            cosine, sine = turn[:, :MODES], turn[:, MODES:]
            rows = slice(index * ROWS, index * ROWS + ROWS)
            cos_part, sin_part = part[rows, :MODES], part[rows, MODES:]
            cos_sum += cosine * cos_part - sine * sin_part
            sin_sum += sine * cos_part + cosine * sin_part
    spectra_ref[:, :MODES] = cos_sum * cell_step
    spectra_ref[:, MODES:] = sin_sum * cell_step
    whole.wait()


def field_kernel(members_ref, radius_ref, angles_ref, *refs, base, many):
    radial_ref, azim_ref, gap_ref, chord_ref, lift_ref, side_ref = refs[-6:]
    if base:
        rows = slice(0, 8 * base)
        radial_ref[:, rows, :] = refs[0][:, rows, :]
        azim_ref[:, rows, :] = refs[1][:, rows, :]
    sector = lax.axis_index(AZ)
    half_cos = angles_ref[sector * 4, base : base + many, :]
    half_sin = angles_ref[sector * 4 + 1, base : base + many, :]
    radius = radius_ref[...]
    halves = 0.5 / radius

    @pl.loop(0, EMB, unroll=4)
    def _(member):
        embryo_radius = members_ref[0, member]
        scale = members_ref[1, member]
        cosine = members_ref[2, member]
        sine = members_ref[3, member]
        gap = radius - embryo_radius
        soft = softening * embryo_radius
        rows = pl.ds(pl.multiple_of(member * 32, 32), 32)
        gap_ref[rows, :] = (gap * gap + soft * soft) * halves * scale
        near = half_sin * cosine - half_cos * sine
        far = half_cos * cosine + half_sin * sine
        chord = (2.0 * embryo_radius) * (near * near)
        columns = pl.ds(pl.multiple_of(member * many, many), many)
        chord_ref[columns, :] = chord * scale
        lift_ref[columns, :] = chord - embryo_radius
        side_ref[columns, :] = (2.0 * embryo_radius) * (near * far)

    pieces = [radius[8 * g : 8 * g + 8] for g in range(GROUPS)]
    ends = []
    for g in range(GROUPS):
        root = lax.rsqrt(2.0 * pieces[g])
        ends.append(root * root * root)
    together = 2

    @pl.loop(0, many // together)
    def _(part):
        zero = jnp.zeros((8, 128), F32)

        def visit(member, carried):
            radial, azim = list(carried[0]), list(carried[1])
            rows = []
            for k in range(together):
                row = pl.ds(member * many + part * together + k, 1)
                rows.append(
                    [jnp.broadcast_to(ref[row, :], (8, 128)) for ref in (chord_ref, lift_ref, side_ref)]
                )
            for g in range(GROUPS):
                gap = gap_ref[pl.ds(pl.multiple_of(member * 32 + 8 * g, 8), 8), :]
                for k in range(together):
                    chord, lift, side = rows[k]
                    inverse = lax.rsqrt(gap + chord)
                    cubed = inverse * inverse * inverse
                    at = k * GROUPS + g
                    radial[at] = radial[at] + cubed * (pieces[g] + lift)
                    azim[at] = azim[at] + cubed * side
            return tuple(radial), tuple(azim)

        count = together * GROUPS
        radial, azim = lax.fori_loop(0, EMB, visit, ((zero,) * count, (zero,) * count), unroll=8)
        for k in range(together):
            where = pl.ds(pl.multiple_of((base + part * together + k) * 8, 8), 8)
            for g in range(GROUPS):
                radial_ref[g, where, :] = radial[k * GROUPS + g] * ends[g]
                azim_ref[g, where, :] = azim[k * GROUPS + g] * ends[g]


def push_kernel(
    members_ref, radius_ref, angles_ref, dens_ref, spectra_ref, out_ref, mass_ref, chord_ref, push_ref
):
    for part in range(4):
        out_ref[ROWS * part : ROWS * part + ROWS, :] = spectra_ref[:, 128 * part : 128 * part + 128]
    sector = lax.axis_index(AZ)
    radius = radius_ref[...]
    pieces = [radius[8 * g : 8 * g + 8] for g in range(GROUPS)]
    halves = [0.5 / piece for piece in pieces]
    for g in range(GROUPS):
        scale = lax.rsqrt(2.0 * pieces[g])
        area = pieces[g] * pieces[g] * (cell_step * cell_step) * (scale * scale * scale)
        mass_ref[g] = (dens_ref[g].reshape(CHUNKS, 8, 128) * area[None]).reshape(SPAN, 128)
    half_cos = angles_ref[sector * 4]
    half_sin = angles_ref[sector * 4 + 1]

    @pl.loop(0, EMB)
    def _(member):
        embryo_radius = members_ref[0, member]
        cosine = members_ref[2, member]
        sine = members_ref[3, member]
        soft = softening * embryo_radius
        gaps = []
        for g in range(GROUPS):
            gap = pieces[g] - embryo_radius
            gaps.append((gap * gap + soft * soft) * halves[g])
        near = half_sin * cosine - half_cos * sine
        chord_ref[...] = (2.0 * embryo_radius) * (near * near)
        push_x = jnp.zeros((8, 128), F32)
        push_y = jnp.zeros((8, 128), F32)
        total = jnp.zeros((8, 128), F32)
        for chunk in range(CHUNKS):
            chord = jnp.broadcast_to(chord_ref[chunk : chunk + 1, :], (8, 128))
            plain, moved = None, None
            for g in range(GROUPS):
                inverse = lax.rsqrt(gaps[g] + chord)
                cubed = inverse * inverse * inverse
                term = cubed * mass_ref[g, 8 * chunk : 8 * chunk + 8, :]
                plain = term if g == 0 else plain + term
                moved = pieces[g] * term if g == 0 else moved + pieces[g] * term
            row = slice(chunk, chunk + 1)
            push_x = push_x + moved * jnp.broadcast_to(angles_ref[sector * 4 + 2, row, :], (8, 128))
            push_y = push_y + moved * jnp.broadcast_to(angles_ref[sector * 4 + 3, row, :], (8, 128))
            total = total + plain
        place_x = embryo_radius * members_ref[4, member]
        place_y = embryo_radius * members_ref[5, member]
        push_ref[pl.ds(member, 1), :] = jnp.sum(push_x - place_x * total, axis=0, keepdims=True)
        push_ref[pl.ds(EMB + member, 1), :] = jnp.sum(push_y - place_y * total, axis=0, keepdims=True)

    push = jnp.broadcast_to(jnp.sum(push_ref[...], axis=1, keepdims=True), (2 * EMB, 128))
    row = lax.broadcasted_iota(jnp.int32, (2 * EMB, 128), 0)
    lane = lax.broadcasted_iota(jnp.int32, (2 * EMB, 128), 1)
    push = jnp.sum(jnp.where(row == lane, push, 0.0), axis=0, keepdims=True)
    out_ref[4 * ROWS : 4 * ROWS + 8, :] = jnp.broadcast_to(push, (8, 128))


def moment_kernel(a_ref, b_ref, lift_ref, drop_ref, vectors_ref, spectra_ref, packed_ref, one_ref):
    total = a_ref[...] + b_ref[...]
    for part in range(4):
        columns = slice(128 * part, 128 * part + 128)
        spectra = total[ROWS * part : ROWS * part + ROWS]
        spectra_ref[:, columns] = spectra
        factor = vectors_ref[0:1, columns]
        up = jnp.sum(spectra * drop_ref[:, columns], axis=0, keepdims=True) / factor
        down = jnp.sum(spectra * lift_ref[:, columns], axis=0, keepdims=True) / factor
        one_ref[part : part + 1, :] = up
        one_ref[4 + part : 5 + part, :] = down
    one_ref[8:16, :] = total[4 * ROWS :]
    one = one_ref[...]
    for copy in range(packed_ref.shape[0]):
        packed_ref[copy] = one


def kick_kernel(
    spectra_ref, moments_ref, rate_ref, radius_ref, vectors_ref, lift_ref, drop_ref, twiddle_ref, high_ref, low_ref,
    radial_ref, azim_ref, vrad_ref, vphi_kept_ref, vphi_sent_ref,
    whole_radial_ref, whole_azim_ref, out_push_ref,
    lower_ref, upper_ref, out_radial_ref, out_azim_ref, sems,
):
    own_index = lax.axis_index(RAD)
    row = lax.broadcasted_iota(jnp.int32, (8, 128), 0)
    outside = jnp.zeros((8, 128), F32)
    push = jnp.zeros((1, 128), F32)
    for source in range(moments_ref.shape[0]):
        many = jnp.where(row < 4, own_index - 1 - source, source - own_index - 1)
        weight = jnp.exp(-rate_ref[...] * jnp.maximum(many, 0).astype(F32))
        outside += jnp.where(many >= 0, weight, 0.0) * moments_ref[source, 0:8, :]
        push += moments_ref[source, 8:9, :]
    out_push_ref[0:1, :] = push[:, :EMB]
    out_push_ref[1:2, :] = push[:, EMB : 2 * EMB]
    lower = jnp.concatenate([outside[k : k + 1] for k in range(4)], axis=1)
    upper = jnp.concatenate([outside[k : k + 1] for k in range(4, 8)], axis=1)
    factor = vectors_ref[0:1, :]
    spectra = spectra_ref[...]
    for row in range(ROWS):
        lower = spectra[row : row + 1] + factor * lower
        lower_ref[row : row + 1, :] = lower
        back = ROWS - 1 - row
        upper = spectra[back : back + 1] + factor * upper
        upper_ref[back : back + 1, :] = upper
    lower = lower_ref[...]
    upper = upper_ref[...]
    inverse = 1.0 / radius_ref[:, 0:1]
    even = lower + upper - spectra
    odd = lower - upper
    radial = odd * vectors_ref[1:2, :] * inverse
    swapped = jnp.concatenate([even[:, MODES:], even[:, :MODES]], axis=1)
    azim = swapped * vectors_ref[2:3, :] * inverse
    sector = lax.axis_index(AZ)
    together = 8

    def whole_copies(quarter):
        rows = pl.ds(pl.multiple_of(16 * together * quarter, 16 * together), 16 * together)
        return [
            pltpu.make_async_copy(source.at[:, rows, :], target.at[:, rows, :], sems.at[index, quarter])
            for index, (source, target) in enumerate(
                ((out_radial_ref, whole_radial_ref), (out_azim_ref, whole_azim_ref))
            )
        ]

    @pl.loop(0, BLOCKS // together)
    def _(quarter):
        pieces = []
        for index in range(together):
            turn = twiddle_ref[pl.ds(sector * BLOCKS + quarter * together + index, 1), :]
            cosine, sine = turn[:, :MODES], turn[:, MODES:]
            for coef in (radial, azim):
                cos_coef, sin_coef = coef[:, :MODES], coef[:, MODES:]
                pieces.append(
                    jnp.concatenate(
                        [cos_coef * cosine + sin_coef * sine, sin_coef * cosine - cos_coef * sine], axis=1
                    )
                )
        high, low = split_value(jnp.concatenate(pieces, axis=0))
        part = dot(high, high_ref[...]) + (dot(low, high_ref[...]) + dot(high, low_ref[...]))
        for index in range(together):
            for half in range(2):
                start = 16 * together * quarter + 8 * (2 * index + half)
                where = pl.ds(pl.multiple_of(start, 8), 8)
                columns = slice(128 * half, 128 * half + 128)
                rows = 2 * ROWS * index
                disk = part[rows : rows + ROWS, columns].reshape(GROUPS, 8, 128)
                out_radial_ref[:, where, :] = vrad_ref[:, where, :] + timestep_length * (
                    disk - radial_ref[:, where, :]
                )
                disk = part[rows + ROWS : rows + 2 * ROWS, columns].reshape(GROUPS, 8, 128)
                vphi = vphi_kept_ref[:, where, :] + vphi_sent_ref[:, where, :]
                out_azim_ref[:, where, :] = vphi + timestep_length * (
                    disk - azim_ref[:, where, :]
                )
        for copy in whole_copies(quarter):
            copy.start()

    for quarter in range(BLOCKS // together):
        for copy in whole_copies(quarter):
            copy.wait()


def across(value, axis, target):
    count = lax.axis_size(axis)
    return lax.ppermute(value, axis, [(source, target(source)) for source in range(count)])


def after(value, *others):
    return lax.optimization_barrier((value, *others))[0]


def on_device(
    surface_mass,
    outward_drift,
    leftover_angular_drift,
    angular_offsets,
    planetesimal_loop_number,
    planetesimal_angle_bin,
    planetesimal_weights,
):
    (basis_high, basis_low), (back_high, back_low), twiddle, angles, lift, drop, vectors, rate = (
        constant_tables()
    )
    tiles = jax.ShapeDtypeStruct((GROUPS, SPAN, 128), F32)
    dens = to_tiles(surface_mass)
    vrad = to_tiles(outward_drift)
    vphi = to_tiles(leftover_angular_drift)

    halo = jax.ShapeDtypeStruct((2 * GROUPS, 8, 128), F32)
    outer, inner, edge_rows = pl.pallas_call(
        border_kernel,
        out_shape=(halo, halo, jax.ShapeDtypeStruct((2, 3 * CHUNKS, 128), F32)),
        in_specs=[pl.BlockSpec(memory_space=pltpu.HBM)] * 3,
        out_specs=(vmem(), vmem(), vmem()),
        scratch_shapes=[pltpu.VMEM((6, SPAN, 128), F32), pltpu.SemaphoreType.DMA((10,))],
        compiler_params=params(),
        cost_estimate=cost(1),
        name="borders",
    )(hbm(dens), hbm(vphi), hbm(vrad))
    border_far = across(outer, AZ, lambda i: i ^ 3)
    border_mate = across(inner, AZ, lambda i: i ^ 1)
    edge_cross = across(edge_rows, AZ, lambda i: i ^ 2)
    edge_mate = across(edge_rows, AZ, lambda i: i ^ 1)
    vrad_cross = across(after(vrad, edge_rows), AZ, lambda i: i ^ 2)
    vrad_mate = across(vrad, AZ, lambda i: i ^ 1)

    cell = np.float32(cell_step)
    cycles = lax.axis_index(RAD) * ROWS + jnp.arange(ROWS, dtype=jnp.int32)
    radius = jnp.broadcast_to(jnp.exp((cycles.astype(F32) + 0.5) * cell)[:, None], (ROWS, 128))
    embryo_angles = (2 * planetesimal_angle_bin + 1).astype(F32) * np.float32(np.pi / ANGULAR_BINS)
    members = jnp.stack(
        [
            jnp.exp((planetesimal_loop_number.astype(F32) + 0.5) * cell),
            jnp.exp(np.float32(-2.0 / 3.0) * jnp.log(planetesimal_weights)),
            jnp.cos(0.5 * embryo_angles),
            jnp.sin(0.5 * embryo_angles),
            jnp.cos(embryo_angles),
            jnp.sin(embryo_angles),
        ]
    )

    dens_two = pl.pallas_call(
        azimuth_kernel,
        out_shape=tiles,
        in_specs=[pl.BlockSpec(memory_space=pltpu.HBM)] * 2 + [vmem()] * 2,
        out_specs=vmem(),
        scratch_shapes=[
            pltpu.VMEM((GROUPS, SPAN, 128), F32),
            pltpu.VMEM((GROUPS, SPAN, 128), F32),
            pltpu.SemaphoreType.DMA((8,)),
        ],
        compiler_params=params(),
        cost_estimate=cost(1),
        name="azimuth",
    )(hbm(dens), hbm(vphi), border_mate, border_far)

    edge_far = across(edge_cross, AZ, lambda i: i ^ 1)
    edge = jax.ShapeDtypeStruct((2 * CHUNKS, 128), F32)
    edge_first, edge_second = pl.pallas_call(
        edge_kernel,
        out_shape=(edge, edge),
        in_specs=[smem()] + [vmem()] * 4,
        out_specs=(vmem(), vmem()),
        scratch_shapes=[
            pltpu.VMEM((3 * RING // 8, 128), F32),
            pltpu.VMEM((RING // 8 + 8, 128), F32),
            pltpu.VMEM((RING // 8, 128), F32),
        ],
        compiler_params=params(),
        cost_estimate=cost(1),
        name="edges",
    )(angular_offsets, edge_rows, edge_mate, edge_cross, edge_far)
    rad_count = lax.axis_size(RAD)
    inside = range(1, rad_count - 1)
    edge_second = lax.ppermute(edge_second, RAD, [(i, i + 1 if i % 2 else i - 1) for i in inside])
    edge_first_in = across(edge_first, RAD, lambda i: i ^ 1)

    def field(base, many, *before):
        return pl.pallas_call(
            functools.partial(field_kernel, base=base, many=many),
            out_shape=(tiles, tiles),
            in_specs=[smem(), vmem(), vmem()] + [vmem()] * len(before),
            out_specs=(vmem(), vmem()),
            scratch_shapes=[pltpu.VMEM((EMB * 32, 128), F32)] + [pltpu.VMEM((EMB * many, 128), F32)] * 3,
            compiler_params=params(),
            cost_estimate=cost(many // 4),
            name=f"field_{base}",
        )(members, radius, angles, *before)

    first_field = field(0, 16)
    dens_mate = across(dens_two, AZ, lambda i: i ^ 1)
    (dens_sent,) = share(angular_offsets, dens_two, dens_mate, (True,), "share_dens")
    vphi_mate = across(vphi, AZ, lambda i: i ^ 1)
    vphi_sent, vphi_kept = share(angular_offsets, vphi, vphi_mate, (True, False), "share_vphi")
    early = (dens_sent, *first_field, edge_first, vphi_sent, vphi_kept)
    vrad_far = across(after(vrad_cross, *early), AZ, lambda i: i ^ 1)
    dens_cross = across(after(dens_sent, vrad_cross, *early), AZ, lambda i: i ^ 2)
    (dens_kept,) = share(angular_offsets, dens_two, dens_mate, (False,), "keep_dens")
    vrad_one = shifted(angular_offsets, vrad, vrad_mate, vrad_cross, vrad_far, "shift_vrad")
    middle_field = field(16, 8, *first_field)
    dens_cross = after(
        dens_cross, vrad_one, *middle_field, dens_kept, vphi_sent, vphi_kept, edge_first_in, edge_second
    )
    vphi_cross = across(after(vphi_sent, *middle_field), AZ, lambda i: i ^ 2)

    transported, stepped, part = pl.pallas_call(
        transport_kernel,
        out_shape=(tiles, tiles, jax.ShapeDtypeStruct((ROWS, 2 * MODES), F32)),
        in_specs=[vmem()] * 8,
        out_specs=(anywhere(), vmem(), vmem()),
        scratch_shapes=[
            pltpu.VMEM((GROUPS, SPAN, 128), F32),
            pltpu.VMEM((2, SPAN, 128), F32),
            pltpu.VMEM((2, SPAN, 128), F32),
            pltpu.SemaphoreType.DMA,
        ],
        compiler_params=params(),
        cost_estimate=cost(3),
        name="transport",
    )(
        dens_kept, dens_cross, edge_first_in, edge_second,
        vrad_one, basis_high, basis_low, twiddle,
    )

    joined_shape = jax.ShapeDtypeStruct((4 * ROWS + 8, 128), F32)
    joined = pl.pallas_call(
        push_kernel,
        out_shape=joined_shape,
        in_specs=[smem()] + [vmem()] * 4,
        out_specs=vmem(),
        scratch_shapes=[
            pltpu.VMEM((GROUPS, SPAN, 128), F32),
            pltpu.VMEM((CHUNKS, 128), F32),
            pltpu.VMEM((2 * EMB, 128), F32),
        ],
        compiler_params=params(),
        cost_estimate=cost(6),
        name="push",
    )(members, radius, angles, stepped, part)
    chip = joined + across(joined, AZ, lambda i: i ^ 1)
    chip_other = across(chip, AZ, lambda i: i ^ 2)

    radial_field, azim_field = field(24, 8, *middle_field)
    chip_later = after(chip, vphi_cross, radial_field)
    spectra, packed = pl.pallas_call(
        moment_kernel,
        out_shape=(
            jax.ShapeDtypeStruct((ROWS, 2 * MODES), F32),
            jax.ShapeDtypeStruct((rad_count, 16, 128), F32),
        ),
        in_specs=[vmem()] * 5,
        out_specs=(vmem(), vmem()),
        scratch_shapes=[pltpu.VMEM((16, 128), F32)],
        compiler_params=params(),
        cost_estimate=cost(1),
        name="moments",
    )(chip_later, chip_other, lift, drop, vectors)
    gathered = lax.all_to_all(packed, RAD, split_axis=0, concat_axis=0, tiled=True)

    kicked_radial, kicked_azim, embryo_disk_acceleration = pl.pallas_call(
        kick_kernel,
        out_shape=(tiles, tiles, jax.ShapeDtypeStruct((2, EMB), F32)),
        in_specs=[vmem()] * 15,
        out_specs=(anywhere(), anywhere(), vmem()),
        scratch_shapes=[
            pltpu.VMEM((ROWS, 2 * MODES), F32),
            pltpu.VMEM((ROWS, 2 * MODES), F32),
            pltpu.VMEM((GROUPS, SPAN, 128), F32),
            pltpu.VMEM((GROUPS, SPAN, 128), F32),
            pltpu.SemaphoreType.DMA((2, 4)),
        ],
        compiler_params=params(),
        cost_estimate=cost(5),
        name="kick",
    )(
        spectra, gathered, rate, radius, vectors, lift, drop, twiddle, back_high, back_low,
        radial_field, azim_field, vrad_one, vphi_kept, vphi_cross,
    )
    return (
        from_tiles(transported),
        from_tiles(kicked_radial),
        from_tiles(kicked_azim),
        embryo_disk_acceleration,
    )


def solution(mesh):
    torus = Mesh(mesh.devices.reshape(4, 2, 4, 2, 2), RAD + AZ)
    placed = (P(RAD, AZ), P(RAD, AZ), P(RAD, AZ), P(RAD), P(), P(), P())
    return jax.shard_map(
        on_device,
        mesh=torus,
        in_specs=placed,
        out_specs=(P(RAD, AZ), P(RAD, AZ), P(RAD, AZ), P()),
        check_vma=False,
    )
```

```python
import functools

import jax
import jax.numpy as jnp
import ml_dtypes
import numpy as np
from jax import lax
from jax.experimental import pallas as pl
from jax.experimental.pallas import tpu as pltpu
from jax.sharding import Mesh
from jax.sharding import PartitionSpec as P

ANGULAR_BINS = 16384
MODES = 256
EMB = 32
RAD = ("rad_0", "rad_1", "rad_2")
AZ = ("az_0", "az_1")
F32 = jnp.float32
BF16 = jnp.bfloat16

gravity = 1.0
timestep_length = 0.05
courant = 0.4
softening = 0.02
cell_step = 2.0 * np.pi / ANGULAR_BINS

ROWS = 32
CHUNKS = 32
GROUPS = 4
SPAN = 8 * CHUNKS
RING = 8 * (5 * CHUNKS + 8)
WIDE = 256
BLOCKS = 16


def split_bf16(table):
    high = table.astype(np.float32).astype(ml_dtypes.bfloat16)
    low = (table - high.astype(np.float64)).astype(np.float32).astype(ml_dtypes.bfloat16)
    return high, low


def constant_tables():
    orders = np.arange(MODES)
    inner = np.arange(WIDE)
    phases = orders[None, :] * (2 * inner[:, None] + 1) % (2 * ANGULAR_BINS) * (np.pi / ANGULAR_BINS)
    basis = np.concatenate([np.cos(phases), np.sin(phases)], axis=1)
    starts = np.arange(ANGULAR_BINS // WIDE) * WIDE
    turns = orders[None, :] * starts[:, None] % ANGULAR_BINS * (2 * np.pi / ANGULAR_BINS)
    twiddle = np.concatenate([np.cos(turns), np.sin(turns)], axis=1).astype(np.float32)
    halves = (2 * np.arange(ANGULAR_BINS) + 1) * (0.5 * np.pi / ANGULAR_BINS)
    wholes = 2 * halves
    angles = np.stack([np.cos(halves), np.sin(halves), np.cos(wholes), np.sin(wholes)])
    angles = angles.reshape(4, 4, CHUNKS, 128).transpose(1, 0, 2, 3).reshape(16, CHUNKS, 128)
    decays = np.tile((orders + 0.5) * cell_step, 2)
    rows = np.arange(ROWS)
    lift = np.exp(-decays[None, :] * (rows[:, None] + 1))
    drop = np.exp(-decays[None, :] * (ROWS - rows[:, None]))
    doubled = np.tile(np.where(orders > 0, 2.0, 1.0), 2)
    radial = -(gravity / cell_step) * doubled * decays * decays
    azim = gravity * np.concatenate([orders * doubled[:MODES], -orders * doubled[:MODES]])
    azim = azim * decays
    vectors = np.zeros((8, 2 * MODES))
    vectors[0] = np.exp(-decays)
    vectors[1] = radial
    vectors[2] = azim
    return (
        split_bf16(basis),
        split_bf16(basis.T),
        twiddle,
        angles.astype(np.float32),
        lift.astype(np.float32),
        drop.astype(np.float32),
        vectors.astype(np.float32),
        np.tile((decays * ROWS).astype(np.float32).reshape(4, 128), (2, 1)),
    )


def to_tiles(value):
    return value.reshape(GROUPS, 8, CHUNKS, 128).transpose(0, 2, 1, 3).reshape(GROUPS, SPAN, 128)


def from_tiles(value):
    return value.reshape(GROUPS, CHUNKS, 8, 128).transpose(0, 2, 1, 3).reshape(ROWS, CHUNKS * 128)


def vmem():
    return pl.BlockSpec(memory_space=pltpu.VMEM)


def smem():
    return pl.BlockSpec(memory_space=pltpu.SMEM)


def anywhere():
    return pl.BlockSpec(memory_space=pl.ANY)


def hbm(value):
    return pltpu.with_memory_space_constraint(value, pltpu.HBM)


def params():
    return pltpu.CompilerParams(vmem_limit_bytes=14 * 1024 * 1024)


def cost(us):
    return pl.CostEstimate(flops=int(us * 1e6), bytes_accessed=int(us * 2.5e6), transcendentals=0)


def donor_flux(speeds, upstream, downstream):
    return jnp.where(speeds > 0, speeds * upstream, speeds * downstream)


def border_kernel(dens_ref, phi_ref, vrad_ref, outer_ref, inner_ref, out_ref, buf_ref, sems):
    odd = lax.axis_index(AZ) % 2
    copies = []
    for index, ref in enumerate((dens_ref, phi_ref)):
        where = slice(GROUPS * index, GROUPS * index + GROUPS)
        outer = pl.ds(pl.multiple_of(odd * (SPAN - 8), 8), 8)
        inner = pl.ds(pl.multiple_of((1 - odd) * (SPAN - 8), 8), 8)
        copies.append((ref.at[:, outer, :], outer_ref.at[where]))
        copies.append((ref.at[:, inner, :], inner_ref.at[where]))
    for index, ref in enumerate((dens_ref, phi_ref, vrad_ref)):
        for side, group in enumerate((0, GROUPS - 1)):
            copies.append((ref.at[group], buf_ref.at[2 * index + side]))
    copies = [pltpu.make_async_copy(*copy, sems.at[index]) for index, copy in enumerate(copies)]
    for copy in copies:
        copy.start()
    for copy in copies:
        copy.wait()
    for side, row in enumerate((0, 7)):
        for index in range(3):
            rows = buf_ref[2 * index + side, pl.ds(row, CHUNKS, stride=8), :]
            out_ref[side, pl.ds(index, CHUNKS, stride=3), :] = rows


def azimuth_kernel(dens_ref, phi_ref, mate_ref, far_ref, out_ref, dens_buf, phi_buf, sems):
    lane = lax.broadcasted_iota(jnp.int32, (1, 8, 128), 2)
    copies = []
    for group in range(GROUPS):
        copies.append(
            (
                pltpu.make_async_copy(dens_ref.at[group], dens_buf.at[group], sems.at[2 * group]),
                pltpu.make_async_copy(phi_ref.at[group], phi_buf.at[group], sems.at[2 * group + 1]),
            )
        )
    for pair in copies:
        for copy in pair:
            copy.start()

    odd = lax.axis_index(AZ) % 2 == 1

    def following(value):
        turned = pltpu.roll(value, 127, 2)
        return jnp.where(lane == 127, turned[1:], turned[:-1])

    def widened(ref, group, base):
        middle = ref[group].reshape(CHUNKS, 8, 128)
        mate, far = mate_ref[base + group][None], far_ref[base + group][None]
        return jnp.concatenate(
            [jnp.where(odd, mate, far), middle, jnp.where(odd, far, mate)], axis=0
        )

    for group in range(GROUPS):
        for copy in copies[group]:
            copy.wait()
        dens = widened(dens_buf, group, 0)
        phi = widened(phi_buf, group, GROUPS)
        speeds = 0.5 * (phi[:-1] + following(phi))
        flux = donor_flux(speeds, dens[:-1], following(dens))
        turned = pltpu.roll(flux, 1, 2)
        before = jnp.where(lane == 0, turned[:-1], turned[1:])
        stepped = dens[1:-1] - courant * (flux[1:] - before)
        out_ref[group] = stepped.reshape(SPAN, 128)


def fill_ring(group, own_ref, mate_ref, cross_ref, far_ref, ring_ref, unit):
    odd = lax.axis_index(AZ) % 2
    places = ((own_ref, 0), (own_ref, 4), (cross_ref, 2), (mate_ref, 1 + 2 * odd), (far_ref, 3 - 2 * odd))
    for source, place in places:
        where = pl.ds(pl.multiple_of(place * unit, unit), unit)
        ring_ref[where, :] = source[group, 0:unit, :]


def shift_row(ring_ref, step, row, offset):
    start = ANGULAR_BINS - offset
    chunk = start // 128
    turn = (128 - start % 128) % 128
    lane = lax.broadcasted_iota(jnp.int32, (CHUNKS, 128), 1)
    first = ring_ref[pl.ds(chunk * step + row, CHUNKS, stride=step), :]
    second = ring_ref[pl.ds((chunk + 1) * step + row, CHUNKS, stride=step), :]
    return jnp.where(
        lane < 128 - start % 128, pltpu.roll(first, turn, 1), pltpu.roll(second, turn, 1)
    )


def shift_kernel(offs_ref, own_ref, mate_ref, cross_ref, far_ref, out_ref, ring_ref):
    @pl.loop(0, GROUPS)
    def _(group):
        fill_ring(group, own_ref, mate_ref, cross_ref, far_ref, ring_ref, SPAN)
        for row in range(8):
            moved = shift_row(ring_ref, 8, row, offs_ref[group * 8 + row])
            out_ref[group, pl.ds(row, CHUNKS, stride=8), :] = moved


def shifted(offsets, own, mate, cross, far, name):
    return pl.pallas_call(
        shift_kernel,
        out_shape=jax.ShapeDtypeStruct((GROUPS, SPAN, 128), F32),
        in_specs=[smem(), vmem(), vmem(), vmem(), vmem()],
        out_specs=vmem(),
        scratch_shapes=[pltpu.VMEM((RING, 128), F32)],
        compiler_params=params(),
        cost_estimate=cost(2),
        name=name,
    )(offsets, own, mate, cross, far)


def share_kernel(offs_ref, own_ref, mate_ref, *refs, kinds):
    odd = lax.axis_index(AZ) % 2
    sent = (own_ref, 2), (mate_ref, 3 - 2 * odd)
    kept = (own_ref, 0), (own_ref, 4), (mate_ref, 1 + 2 * odd)
    out_refs, ring_refs = refs[: len(kinds)], refs[len(kinds) :]
    for ring_ref in ring_refs:
        ring_ref[...] = jnp.zeros_like(ring_ref)

    @pl.loop(0, GROUPS)
    def _(group):
        for kind, out_ref, ring_ref in zip(kinds, out_refs, ring_refs):
            for source, place in sent if kind else kept:
                where = pl.ds(pl.multiple_of(place * SPAN, SPAN), SPAN)
                ring_ref[where, :] = source[group]
            for row in range(8):
                moved = shift_row(ring_ref, 8, row, offs_ref[group * 8 + row])
                out_ref[group, pl.ds(row, CHUNKS, stride=8), :] = moved


def share(offsets, own, mate, kinds, name):
    return pl.pallas_call(
        functools.partial(share_kernel, kinds=kinds),
        out_shape=tuple(jax.ShapeDtypeStruct((GROUPS, SPAN, 128), F32) for _ in kinds),
        in_specs=[smem(), vmem(), vmem()],
        out_specs=tuple(vmem() for _ in kinds),
        scratch_shapes=[pltpu.VMEM((RING, 128), F32) for _ in kinds],
        compiler_params=params(),
        cost_estimate=cost(2),
        name=name,
    )(offsets, own, mate)


def edge_kernel(
    offs_ref, own_ref, mate_ref, cross_ref, far_ref, first_ref, second_ref, ring_ref, flux_ref, line_ref
):
    unit = 3 * CHUNKS
    length = 5 * CHUNKS
    lane = lax.broadcasted_iota(jnp.int32, (length, 128), 1)
    sides = []
    for side in range(2):
        fill_ring(side, own_ref, mate_ref, cross_ref, far_ref, ring_ref, unit)
        ring_ref[5 * unit : 5 * unit + 24, :] = ring_ref[unit : unit + 24, :]
        offset = offs_ref[(ROWS - 1) * side]

        def following(index):
            here = pltpu.roll(ring_ref[pl.ds(index, length, stride=3), :], 127, 1)
            there = pltpu.roll(ring_ref[pl.ds(index + 3, length, stride=3), :], 127, 1)
            return jnp.where(lane == 127, there, here)

        dens = ring_ref[pl.ds(0, length, stride=3), :]
        phi = ring_ref[pl.ds(1, length, stride=3), :]
        flux = donor_flux(0.5 * (phi + following(1)), dens, following(0))
        flux_ref[8 : 8 + length, :] = flux
        before = pltpu.roll(flux_ref[7 : 7 + length, :], 1, 1)
        before = jnp.where(lane == 0, before, pltpu.roll(flux, 1, 1))
        line_ref[0:length, :] = dens - courant * (flux - before)
        sides.append((shift_row(line_ref, 1, 0, offset), shift_row(ring_ref, 3, 2, offset)))
    even = lax.axis_index(RAD) % 2 == 0
    for index in range(2):
        where = slice(CHUNKS * index, CHUNKS * index + CHUNKS)
        down, up = sides[0][index], sides[1][index]
        first_ref[where, :] = jnp.where(even, up, down)
        second_ref[where, :] = jnp.where(even, down, up)


def split_value(value):
    high = value.astype(BF16)
    return high, (value - high.astype(F32)).astype(BF16)


def dot(left, right):
    return jnp.dot(left, right, preferred_element_type=F32)


def transport_kernel(
    kept_ref, sent_ref, first_ref, second_ref, vrad_ref, high_ref, low_ref, twiddle_ref,
    whole_ref, dens_ref, spectra_ref,
    moved_ref, other_ref, speed_ref, whole_sem,
):
    for group in range(GROUPS):
        moved_ref[group] = kept_ref[group] + sent_ref[group]
    even = lax.axis_index(RAD) % 2 == 0
    first, second = first_ref[...], second_ref[...]
    for side, row in enumerate((7, 0)):
        edge = jnp.where(even, second, first) if side == 0 else jnp.where(even, first, second)
        other_ref[side, pl.ds(row, CHUNKS, stride=8), :] = edge[0:CHUNKS]
        speed_ref[side, pl.ds(row, CHUNKS, stride=8), :] = edge[CHUNKS:]

    sub = lax.broadcasted_iota(jnp.int32, (1, 8, 128), 1)
    own_index = lax.axis_index(RAD)
    bottom = own_index == 0
    top = own_index == lax.axis_size(RAD) - 1

    def above(value, following):
        return jnp.where(sub == 7, pltpu.roll(following, 7, 1), pltpu.roll(value, 7, 1))

    def below(value, previous):
        return jnp.where(sub == 0, pltpu.roll(previous, 1, 1), pltpu.roll(value, 1, 1))

    step = 4
    for group in range(GROUPS):

        @pl.loop(0, CHUNKS // step)
        def _(part):
            where = pl.ds(pl.multiple_of(part * 8 * step, 8 * step), 8 * step)

            def tiles(ref, index):
                return ref[index, where, :].reshape(step, 8, 128)

            dens = tiles(moved_ref, group)
            upper = tiles(moved_ref, group + 1) if group < 3 else tiles(other_ref, 1)
            lower = tiles(moved_ref, group - 1) if group > 0 else tiles(other_ref, 0)
            dens_above = above(dens, upper)
            dens_below = below(dens, lower)
            speed = tiles(vrad_ref, group)
            upper = tiles(vrad_ref, group + 1) if group < 3 else tiles(speed_ref, 1)
            lower = tiles(vrad_ref, group - 1) if group > 0 else tiles(speed_ref, 0)
            flux_above = donor_flux(0.5 * (speed + above(speed, upper)), dens, dens_above)
            flux_below = donor_flux(0.5 * (below(speed, lower) + speed), dens_below, dens)
            if group == 3:
                flux_above = jnp.where((sub == 7) & top, 0.0, flux_above)
            if group == 0:
                flux_below = jnp.where((sub == 0) & bottom, 0.0, flux_below)
            stepped = dens - courant * (flux_above - flux_below)
            dens_ref[group, where, :] = stepped.reshape(8 * step, 128)

    whole = pltpu.make_async_copy(dens_ref, whole_ref, whole_sem)
    whole.start()
    sector = lax.axis_index(AZ)
    cos_sum = jnp.zeros((ROWS, MODES), F32)
    sin_sum = jnp.zeros((ROWS, MODES), F32)
    together = 8
    for first in range(0, BLOCKS, together):
        pieces = []
        for block in range(first, first + together):
            halves = [
                dens_ref[:, 8 * chunk : 8 * chunk + 8, :].reshape(ROWS, 128)
                for chunk in (2 * block, 2 * block + 1)
            ]
            pieces.append(jnp.concatenate(halves, axis=1))
        high, low = split_value(jnp.concatenate(pieces, axis=0))
        part = dot(high, high_ref[...]) + (dot(low, high_ref[...]) + dot(high, low_ref[...]))
        for index in range(together):
            turn = twiddle_ref[pl.ds(sector * BLOCKS + first + index, 1), :]
            cosine, sine = turn[:, :MODES], turn[:, MODES:]
            rows = slice(index * ROWS, index * ROWS + ROWS)
            cos_part, sin_part = part[rows, :MODES], part[rows, MODES:]
            cos_sum += cosine * cos_part - sine * sin_part
            sin_sum += sine * cos_part + cosine * sin_part
    spectra_ref[:, :MODES] = cos_sum * cell_step
    spectra_ref[:, MODES:] = sin_sum * cell_step
    whole.wait()


def field_kernel(members_ref, radius_ref, angles_ref, *refs, base, many):
    radial_ref, azim_ref, gap_ref, chord_ref, lift_ref, side_ref = refs[-6:]
    if base:
        rows = slice(0, 8 * base)
        radial_ref[:, rows, :] = refs[0][:, rows, :]
        azim_ref[:, rows, :] = refs[1][:, rows, :]
    sector = lax.axis_index(AZ)
    half_cos = angles_ref[sector * 4, base : base + many, :]
    half_sin = angles_ref[sector * 4 + 1, base : base + many, :]
    radius = radius_ref[...]
    halves = 0.5 / radius

    @pl.loop(0, EMB, unroll=4)
    def _(member):
        embryo_radius = members_ref[0, member]
        scale = members_ref[1, member]
        cosine = members_ref[2, member]
        sine = members_ref[3, member]
        gap = radius - embryo_radius
        soft = softening * embryo_radius
        rows = pl.ds(pl.multiple_of(member * 32, 32), 32)
        gap_ref[rows, :] = (gap * gap + soft * soft) * halves * scale
        near = half_sin * cosine - half_cos * sine
        far = half_cos * cosine + half_sin * sine
        chord = (2.0 * embryo_radius) * (near * near)
        columns = pl.ds(pl.multiple_of(member * many, many), many)
        chord_ref[columns, :] = chord * scale
        lift_ref[columns, :] = chord - embryo_radius
        side_ref[columns, :] = (2.0 * embryo_radius) * (near * far)

    pieces = [radius[8 * g : 8 * g + 8] for g in range(GROUPS)]
    ends = []
    for g in range(GROUPS):
        root = lax.rsqrt(2.0 * pieces[g])
        ends.append(root * root * root)
    together = 2

    @pl.loop(0, many // together)
    def _(part):
        zero = jnp.zeros((8, 128), F32)

        def visit(member, carried):
            radial, azim = list(carried[0]), list(carried[1])
            rows = []
            for k in range(together):
                row = pl.ds(member * many + part * together + k, 1)
                rows.append(
                    [jnp.broadcast_to(ref[row, :], (8, 128)) for ref in (chord_ref, lift_ref, side_ref)]
                )
            for g in range(GROUPS):
                gap = gap_ref[pl.ds(pl.multiple_of(member * 32 + 8 * g, 8), 8), :]
                for k in range(together):
                    chord, lift, side = rows[k]
                    inverse = lax.rsqrt(gap + chord)
                    cubed = inverse * inverse * inverse
                    at = k * GROUPS + g
                    radial[at] = radial[at] + cubed * (pieces[g] + lift)
                    azim[at] = azim[at] + cubed * side
            return tuple(radial), tuple(azim)

        count = together * GROUPS
        radial, azim = lax.fori_loop(0, EMB, visit, ((zero,) * count, (zero,) * count), unroll=8)
        for k in range(together):
            where = pl.ds(pl.multiple_of((base + part * together + k) * 8, 8), 8)
            for g in range(GROUPS):
                radial_ref[g, where, :] = radial[k * GROUPS + g] * ends[g]
                azim_ref[g, where, :] = azim[k * GROUPS + g] * ends[g]


def push_kernel(
    members_ref, radius_ref, angles_ref, dens_ref, spectra_ref, out_ref, mass_ref, chord_ref, push_ref
):
    for part in range(4):
        out_ref[ROWS * part : ROWS * part + ROWS, :] = spectra_ref[:, 128 * part : 128 * part + 128]
    sector = lax.axis_index(AZ)
    radius = radius_ref[...]
    pieces = [radius[8 * g : 8 * g + 8] for g in range(GROUPS)]
    halves = [0.5 / piece for piece in pieces]
    for g in range(GROUPS):
        scale = lax.rsqrt(2.0 * pieces[g])
        area = pieces[g] * pieces[g] * (cell_step * cell_step) * (scale * scale * scale)
        mass_ref[g] = (dens_ref[g].reshape(CHUNKS, 8, 128) * area[None]).reshape(SPAN, 128)
    half_cos = angles_ref[sector * 4]
    half_sin = angles_ref[sector * 4 + 1]

    @pl.loop(0, EMB, unroll=4)
    def _(member):
        near = half_sin * members_ref[2, member] - half_cos * members_ref[3, member]
        rows = pl.ds(pl.multiple_of(member * CHUNKS, CHUNKS), CHUNKS)
        chord_ref[rows, :] = (2.0 * members_ref[0, member]) * (near * near)

    @pl.loop(0, EMB, unroll=2)
    def _(member):
        embryo_radius = members_ref[0, member]
        soft = softening * embryo_radius
        gaps = []
        for g in range(GROUPS):
            gap = pieces[g] - embryo_radius
            gaps.append((gap * gap + soft * soft) * halves[g])
        push_x = jnp.zeros((8, 128), F32)
        push_y = jnp.zeros((8, 128), F32)
        total = jnp.zeros((8, 128), F32)
        for chunk in range(CHUNKS):
            chord = jnp.broadcast_to(chord_ref[pl.ds(member * CHUNKS + chunk, 1), :], (8, 128))
            plain, moved = None, None
            for g in range(GROUPS):
                inverse = lax.rsqrt(gaps[g] + chord)
                cubed = inverse * inverse * inverse
                term = cubed * mass_ref[g, 8 * chunk : 8 * chunk + 8, :]
                plain = term if g == 0 else plain + term
                moved = pieces[g] * term if g == 0 else moved + pieces[g] * term
            row = slice(chunk, chunk + 1)
            push_x = push_x + moved * jnp.broadcast_to(angles_ref[sector * 4 + 2, row, :], (8, 128))
            push_y = push_y + moved * jnp.broadcast_to(angles_ref[sector * 4 + 3, row, :], (8, 128))
            total = total + plain
        place_x = embryo_radius * members_ref[4, member]
        place_y = embryo_radius * members_ref[5, member]
        push_ref[member] = push_x - place_x * total
        push_ref[EMB + member] = push_y - place_y * total

    push = jnp.sum(jnp.sum(push_ref[...], axis=1), axis=1, keepdims=True)
    push = jnp.broadcast_to(push, (2 * EMB, 128))
    row = lax.broadcasted_iota(jnp.int32, (2 * EMB, 128), 0)
    lane = lax.broadcasted_iota(jnp.int32, (2 * EMB, 128), 1)
    push = jnp.sum(jnp.where(row == lane, push, 0.0), axis=0, keepdims=True)
    out_ref[4 * ROWS : 4 * ROWS + 8, :] = jnp.broadcast_to(push, (8, 128))


def moment_kernel(a_ref, b_ref, lift_ref, drop_ref, vectors_ref, spectra_ref, packed_ref, one_ref):
    total = a_ref[...] + b_ref[...]
    for part in range(4):
        columns = slice(128 * part, 128 * part + 128)
        spectra = total[ROWS * part : ROWS * part + ROWS]
        spectra_ref[:, columns] = spectra
        factor = vectors_ref[0:1, columns]
        up = jnp.sum(spectra * drop_ref[:, columns], axis=0, keepdims=True) / factor
        down = jnp.sum(spectra * lift_ref[:, columns], axis=0, keepdims=True) / factor
        one_ref[part : part + 1, :] = up
        one_ref[4 + part : 5 + part, :] = down
    one_ref[8:16, :] = total[4 * ROWS :]
    one = one_ref[...]
    for copy in range(packed_ref.shape[0]):
        packed_ref[copy] = one


def kick_kernel(
    spectra_ref, moments_ref, rate_ref, radius_ref, vectors_ref, lift_ref, drop_ref, twiddle_ref, high_ref, low_ref,
    radial_ref, azim_ref, vrad_ref, vphi_kept_ref, vphi_sent_ref,
    whole_radial_ref, whole_azim_ref, out_push_ref,
    lower_ref, upper_ref, out_radial_ref, out_azim_ref, sems,
):
    own_index = lax.axis_index(RAD)
    row = lax.broadcasted_iota(jnp.int32, (8, 128), 0)
    outside = jnp.zeros((8, 128), F32)
    push = jnp.zeros((1, 128), F32)
    for source in range(moments_ref.shape[0]):
        many = jnp.where(row < 4, own_index - 1 - source, source - own_index - 1)
        weight = jnp.exp(-rate_ref[...] * jnp.maximum(many, 0).astype(F32))
        outside += jnp.where(many >= 0, weight, 0.0) * moments_ref[source, 0:8, :]
        push += moments_ref[source, 8:9, :]
    out_push_ref[0:1, :] = push[:, :EMB]
    out_push_ref[1:2, :] = push[:, EMB : 2 * EMB]
    lower = jnp.concatenate([outside[k : k + 1] for k in range(4)], axis=1)
    upper = jnp.concatenate([outside[k : k + 1] for k in range(4, 8)], axis=1)
    factor = vectors_ref[0:1, :]
    spectra = spectra_ref[...]
    for row in range(ROWS):
        lower = spectra[row : row + 1] + factor * lower
        lower_ref[row : row + 1, :] = lower
        back = ROWS - 1 - row
        upper = spectra[back : back + 1] + factor * upper
        upper_ref[back : back + 1, :] = upper
    lower = lower_ref[...]
    upper = upper_ref[...]
    inverse = 1.0 / radius_ref[:, 0:1]
    even = lower + upper - spectra
    odd = lower - upper
    radial = odd * vectors_ref[1:2, :] * inverse
    swapped = jnp.concatenate([even[:, MODES:], even[:, :MODES]], axis=1)
    azim = swapped * vectors_ref[2:3, :] * inverse
    sector = lax.axis_index(AZ)
    together = 8

    def whole_copies(quarter):
        rows = pl.ds(pl.multiple_of(16 * together * quarter, 16 * together), 16 * together)
        return [
            pltpu.make_async_copy(source.at[:, rows, :], target.at[:, rows, :], sems.at[index, quarter])
            for index, (source, target) in enumerate(
                ((out_radial_ref, whole_radial_ref), (out_azim_ref, whole_azim_ref))
            )
        ]

    @pl.loop(0, BLOCKS // together)
    def _(quarter):
        pieces = []
        for index in range(together):
            turn = twiddle_ref[pl.ds(sector * BLOCKS + quarter * together + index, 1), :]
            cosine, sine = turn[:, :MODES], turn[:, MODES:]
            for coef in (radial, azim):
                cos_coef, sin_coef = coef[:, :MODES], coef[:, MODES:]
                pieces.append(
                    jnp.concatenate(
                        [cos_coef * cosine + sin_coef * sine, sin_coef * cosine - cos_coef * sine], axis=1
                    )
                )
        high, low = split_value(jnp.concatenate(pieces, axis=0))
        part = dot(high, high_ref[...]) + (dot(low, high_ref[...]) + dot(high, low_ref[...]))
        for index in range(together):
            for half in range(2):
                start = 16 * together * quarter + 8 * (2 * index + half)
                where = pl.ds(pl.multiple_of(start, 8), 8)
                columns = slice(128 * half, 128 * half + 128)
                rows = 2 * ROWS * index
                disk = part[rows : rows + ROWS, columns].reshape(GROUPS, 8, 128)
                out_radial_ref[:, where, :] = vrad_ref[:, where, :] + timestep_length * (
                    disk - radial_ref[:, where, :]
                )
                disk = part[rows + ROWS : rows + 2 * ROWS, columns].reshape(GROUPS, 8, 128)
                vphi = vphi_kept_ref[:, where, :] + vphi_sent_ref[:, where, :]
                out_azim_ref[:, where, :] = vphi + timestep_length * (
                    disk - azim_ref[:, where, :]
                )
        for copy in whole_copies(quarter):
            copy.start()

    for quarter in range(BLOCKS // together):
        for copy in whole_copies(quarter):
            copy.wait()


def across(value, axis, target):
    count = lax.axis_size(axis)
    return lax.ppermute(value, axis, [(source, target(source)) for source in range(count)])


def after(value, *others):
    return lax.optimization_barrier((value, *others))[0]


def on_device(
    surface_mass,
    outward_drift,
    leftover_angular_drift,
    angular_offsets,
    planetesimal_loop_number,
    planetesimal_angle_bin,
    planetesimal_weights,
):
    (basis_high, basis_low), (back_high, back_low), twiddle, angles, lift, drop, vectors, rate = (
        constant_tables()
    )
    tiles = jax.ShapeDtypeStruct((GROUPS, SPAN, 128), F32)
    dens = to_tiles(surface_mass)
    vrad = to_tiles(outward_drift)
    vphi = to_tiles(leftover_angular_drift)

    halo = jax.ShapeDtypeStruct((2 * GROUPS, 8, 128), F32)
    outer, inner, edge_rows = pl.pallas_call(
        border_kernel,
        out_shape=(halo, halo, jax.ShapeDtypeStruct((2, 3 * CHUNKS, 128), F32)),
        in_specs=[pl.BlockSpec(memory_space=pltpu.HBM)] * 3,
        out_specs=(vmem(), vmem(), vmem()),
        scratch_shapes=[pltpu.VMEM((6, SPAN, 128), F32), pltpu.SemaphoreType.DMA((10,))],
        compiler_params=params(),
        cost_estimate=cost(1),
        name="borders",
    )(hbm(dens), hbm(vphi), hbm(vrad))
    border_far = across(outer, AZ, lambda i: i ^ 3)
    border_mate = across(inner, AZ, lambda i: i ^ 1)
    edge_cross = across(edge_rows, AZ, lambda i: i ^ 2)
    edge_mate = across(edge_rows, AZ, lambda i: i ^ 1)
    vrad_cross = across(after(vrad, edge_rows), AZ, lambda i: i ^ 2)
    vrad_mate = across(vrad, AZ, lambda i: i ^ 1)

    cell = np.float32(cell_step)
    cycles = lax.axis_index(RAD) * ROWS + jnp.arange(ROWS, dtype=jnp.int32)
    radius = jnp.broadcast_to(jnp.exp((cycles.astype(F32) + 0.5) * cell)[:, None], (ROWS, 128))
    embryo_angles = (2 * planetesimal_angle_bin + 1).astype(F32) * np.float32(np.pi / ANGULAR_BINS)
    members = jnp.stack(
        [
            jnp.exp((planetesimal_loop_number.astype(F32) + 0.5) * cell),
            jnp.exp(np.float32(-2.0 / 3.0) * jnp.log(planetesimal_weights)),
            jnp.cos(0.5 * embryo_angles),
            jnp.sin(0.5 * embryo_angles),
            jnp.cos(embryo_angles),
            jnp.sin(embryo_angles),
        ]
    )

    dens_two = pl.pallas_call(
        azimuth_kernel,
        out_shape=tiles,
        in_specs=[pl.BlockSpec(memory_space=pltpu.HBM)] * 2 + [vmem()] * 2,
        out_specs=vmem(),
        scratch_shapes=[
            pltpu.VMEM((GROUPS, SPAN, 128), F32),
            pltpu.VMEM((GROUPS, SPAN, 128), F32),
            pltpu.SemaphoreType.DMA((8,)),
        ],
        compiler_params=params(),
        cost_estimate=cost(1),
        name="azimuth",
    )(hbm(dens), hbm(vphi), border_mate, border_far)

    edge_far = across(edge_cross, AZ, lambda i: i ^ 1)
    edge = jax.ShapeDtypeStruct((2 * CHUNKS, 128), F32)
    edge_first, edge_second = pl.pallas_call(
        edge_kernel,
        out_shape=(edge, edge),
        in_specs=[smem()] + [vmem()] * 4,
        out_specs=(vmem(), vmem()),
        scratch_shapes=[
            pltpu.VMEM((3 * RING // 8, 128), F32),
            pltpu.VMEM((RING // 8 + 8, 128), F32),
            pltpu.VMEM((RING // 8, 128), F32),
        ],
        compiler_params=params(),
        cost_estimate=cost(1),
        name="edges",
    )(angular_offsets, edge_rows, edge_mate, edge_cross, edge_far)
    rad_count = lax.axis_size(RAD)
    inside = range(1, rad_count - 1)
    edge_second = lax.ppermute(edge_second, RAD, [(i, i + 1 if i % 2 else i - 1) for i in inside])
    edge_first_in = across(edge_first, RAD, lambda i: i ^ 1)

    def field(base, many, *before):
        return pl.pallas_call(
            functools.partial(field_kernel, base=base, many=many),
            out_shape=(tiles, tiles),
            in_specs=[smem(), vmem(), vmem()] + [vmem()] * len(before),
            out_specs=(vmem(), vmem()),
            scratch_shapes=[pltpu.VMEM((EMB * 32, 128), F32)] + [pltpu.VMEM((EMB * many, 128), F32)] * 3,
            compiler_params=params(),
            cost_estimate=cost(many // 4),
            name=f"field_{base}",
        )(members, radius, angles, *before)

    first_field = field(0, 16)
    dens_mate = across(dens_two, AZ, lambda i: i ^ 1)
    (dens_sent,) = share(angular_offsets, dens_two, dens_mate, (True,), "share_dens")
    vphi_mate = across(vphi, AZ, lambda i: i ^ 1)
    vphi_sent, vphi_kept = share(angular_offsets, vphi, vphi_mate, (True, False), "share_vphi")
    early = (dens_sent, *first_field, edge_first, vphi_sent, vphi_kept)
    vrad_far = across(after(vrad_cross, *early), AZ, lambda i: i ^ 1)
    dens_cross = across(after(dens_sent, vrad_cross, *early), AZ, lambda i: i ^ 2)
    (dens_kept,) = share(angular_offsets, dens_two, dens_mate, (False,), "keep_dens")
    vrad_one = shifted(angular_offsets, vrad, vrad_mate, vrad_cross, vrad_far, "shift_vrad")
    middle_field = field(16, 8, *first_field)
    dens_cross = after(
        dens_cross, vrad_one, *middle_field, dens_kept, vphi_sent, vphi_kept, edge_first_in, edge_second
    )
    vphi_cross = across(after(vphi_sent, *middle_field), AZ, lambda i: i ^ 2)

    transported, stepped, part = pl.pallas_call(
        transport_kernel,
        out_shape=(tiles, tiles, jax.ShapeDtypeStruct((ROWS, 2 * MODES), F32)),
        in_specs=[vmem()] * 8,
        out_specs=(anywhere(), vmem(), vmem()),
        scratch_shapes=[
            pltpu.VMEM((GROUPS, SPAN, 128), F32),
            pltpu.VMEM((2, SPAN, 128), F32),
            pltpu.VMEM((2, SPAN, 128), F32),
            pltpu.SemaphoreType.DMA,
        ],
        compiler_params=params(),
        cost_estimate=cost(3),
        name="transport",
    )(
        dens_kept, dens_cross, edge_first_in, edge_second,
        vrad_one, basis_high, basis_low, twiddle,
    )

    joined_shape = jax.ShapeDtypeStruct((4 * ROWS + 8, 128), F32)
    joined = pl.pallas_call(
        push_kernel,
        out_shape=joined_shape,
        in_specs=[smem()] + [vmem()] * 4,
        out_specs=vmem(),
        scratch_shapes=[
            pltpu.VMEM((GROUPS, SPAN, 128), F32),
            pltpu.VMEM((EMB * CHUNKS, 128), F32),
            pltpu.VMEM((2 * EMB, 8, 128), F32),
        ],
        compiler_params=params(),
        cost_estimate=cost(6),
        name="push",
    )(members, radius, angles, stepped, part)
    chip = joined + across(joined, AZ, lambda i: i ^ 1)
    chip_other = across(chip, AZ, lambda i: i ^ 2)

    radial_field, azim_field = field(24, 8, *middle_field)
    chip_later = after(chip, vphi_cross, radial_field)
    spectra, packed = pl.pallas_call(
        moment_kernel,
        out_shape=(
            jax.ShapeDtypeStruct((ROWS, 2 * MODES), F32),
            jax.ShapeDtypeStruct((rad_count, 16, 128), F32),
        ),
        in_specs=[vmem()] * 5,
        out_specs=(vmem(), vmem()),
        scratch_shapes=[pltpu.VMEM((16, 128), F32)],
        compiler_params=params(),
        cost_estimate=cost(1),
        name="moments",
    )(chip_later, chip_other, lift, drop, vectors)
    gathered = lax.all_to_all(packed, RAD, split_axis=0, concat_axis=0, tiled=True)

    kicked_radial, kicked_azim, embryo_disk_acceleration = pl.pallas_call(
        kick_kernel,
        out_shape=(tiles, tiles, jax.ShapeDtypeStruct((2, EMB), F32)),
        in_specs=[vmem()] * 15,
        out_specs=(anywhere(), anywhere(), vmem()),
        scratch_shapes=[
            pltpu.VMEM((ROWS, 2 * MODES), F32),
            pltpu.VMEM((ROWS, 2 * MODES), F32),
            pltpu.VMEM((GROUPS, SPAN, 128), F32),
            pltpu.VMEM((GROUPS, SPAN, 128), F32),
            pltpu.SemaphoreType.DMA((2, 4)),
        ],
        compiler_params=params(),
        cost_estimate=cost(5),
        name="kick",
    )(
        spectra, gathered, rate, radius, vectors, lift, drop, twiddle, back_high, back_low,
        radial_field, azim_field, vrad_one, vphi_kept, vphi_cross,
    )
    return (
        from_tiles(transported),
        from_tiles(kicked_radial),
        from_tiles(kicked_azim),
        embryo_disk_acceleration,
    )


def solution(mesh):
    torus = Mesh(mesh.devices.reshape(4, 2, 4, 2, 2), RAD + AZ)
    placed = (P(RAD, AZ), P(RAD, AZ), P(RAD, AZ), P(RAD), P(), P(), P())
    return jax.shard_map(
        on_device,
        mesh=torus,
        in_specs=placed,
        out_specs=(P(RAD, AZ), P(RAD, AZ), P(RAD, AZ), P()),
        check_vma=False,
    )
```

```python
import functools

import jax
import jax.numpy as jnp
import ml_dtypes
import numpy as np
from jax import lax
from jax.experimental import pallas as pl
from jax.experimental.pallas import tpu as pltpu
from jax.sharding import Mesh
from jax.sharding import PartitionSpec as P

ANGULAR_BINS = 16384
MODES = 256
EMB = 32
RAD = ("rad_0", "rad_1", "rad_2")
AZ = ("az_0", "az_1")
F32 = jnp.float32
BF16 = jnp.bfloat16

gravity = 1.0
timestep_length = 0.05
courant = 0.4
softening = 0.02
cell_step = 2.0 * np.pi / ANGULAR_BINS

ROWS = 32
CHUNKS = 32
GROUPS = 4
SPAN = 8 * CHUNKS
RING = 8 * (5 * CHUNKS + 8)
WIDE = 256
BLOCKS = 16


def split_bf16(table):
    high = table.astype(np.float32).astype(ml_dtypes.bfloat16)
    low = (table - high.astype(np.float64)).astype(np.float32).astype(ml_dtypes.bfloat16)
    return high, low


def constant_tables():
    orders = np.arange(MODES)
    inner = np.arange(WIDE)
    phases = orders[None, :] * (2 * inner[:, None] + 1) % (2 * ANGULAR_BINS) * (np.pi / ANGULAR_BINS)
    basis = np.concatenate([np.cos(phases), np.sin(phases)], axis=1)
    starts = np.arange(ANGULAR_BINS // WIDE) * WIDE
    turns = orders[None, :] * starts[:, None] % ANGULAR_BINS * (2 * np.pi / ANGULAR_BINS)
    twiddle = np.concatenate([np.cos(turns), np.sin(turns)], axis=1).astype(np.float32)
    halves = (2 * np.arange(ANGULAR_BINS) + 1) * (0.5 * np.pi / ANGULAR_BINS)
    wholes = 2 * halves
    angles = np.stack([np.cos(halves), np.sin(halves), np.cos(wholes), np.sin(wholes)])
    angles = angles.reshape(4, 4, CHUNKS, 128).transpose(1, 0, 2, 3).reshape(16, CHUNKS, 128)
    decays = np.tile((orders + 0.5) * cell_step, 2)
    rows = np.arange(ROWS)
    lift = np.exp(-decays[None, :] * (rows[:, None] + 1))
    drop = np.exp(-decays[None, :] * (ROWS - rows[:, None]))
    doubled = np.tile(np.where(orders > 0, 2.0, 1.0), 2)
    radial = -(gravity / cell_step) * doubled * decays * decays
    azim = gravity * np.concatenate([orders * doubled[:MODES], -orders * doubled[:MODES]])
    azim = azim * decays
    vectors = np.zeros((8, 2 * MODES))
    vectors[0] = np.exp(-decays)
    vectors[1] = radial
    vectors[2] = azim
    return (
        split_bf16(basis),
        split_bf16(basis.T),
        twiddle,
        angles.astype(np.float32),
        lift.astype(np.float32),
        drop.astype(np.float32),
        vectors.astype(np.float32),
        np.tile((decays * ROWS).astype(np.float32).reshape(4, 128), (2, 1)),
    )


def to_tiles(value):
    return value.reshape(GROUPS, 8, CHUNKS, 128).transpose(0, 2, 1, 3).reshape(GROUPS, SPAN, 128)


def from_tiles(value):
    return value.reshape(GROUPS, CHUNKS, 8, 128).transpose(0, 2, 1, 3).reshape(ROWS, CHUNKS * 128)


def vmem():
    return pl.BlockSpec(memory_space=pltpu.VMEM)


def smem():
    return pl.BlockSpec(memory_space=pltpu.SMEM)


def anywhere():
    return pl.BlockSpec(memory_space=pl.ANY)


def hbm(value):
    return pltpu.with_memory_space_constraint(value, pltpu.HBM)


def params():
    return pltpu.CompilerParams(vmem_limit_bytes=14 * 1024 * 1024)


def cost(us):
    return pl.CostEstimate(flops=int(us * 1e6), bytes_accessed=int(us * 2.5e6), transcendentals=0)


def donor_flux(speeds, upstream, downstream):
    return jnp.where(speeds > 0, speeds * upstream, speeds * downstream)


def border_kernel(dens_ref, phi_ref, vrad_ref, outer_ref, inner_ref, out_ref, buf_ref, sems):
    odd = lax.axis_index(AZ) % 2
    copies = []
    for index, ref in enumerate((dens_ref, phi_ref)):
        where = slice(GROUPS * index, GROUPS * index + GROUPS)
        outer = pl.ds(pl.multiple_of(odd * (SPAN - 8), 8), 8)
        inner = pl.ds(pl.multiple_of((1 - odd) * (SPAN - 8), 8), 8)
        copies.append((ref.at[:, outer, :], outer_ref.at[where]))
        copies.append((ref.at[:, inner, :], inner_ref.at[where]))
    for index, ref in enumerate((dens_ref, phi_ref, vrad_ref)):
        for side, group in enumerate((0, GROUPS - 1)):
            copies.append((ref.at[group], buf_ref.at[2 * index + side]))
    copies = [pltpu.make_async_copy(*copy, sems.at[index]) for index, copy in enumerate(copies)]
    for copy in copies:
        copy.start()
    for copy in copies:
        copy.wait()
    for side, row in enumerate((0, 7)):
        for index in range(3):
            rows = buf_ref[2 * index + side, pl.ds(row, CHUNKS, stride=8), :]
            out_ref[side, pl.ds(index, CHUNKS, stride=3), :] = rows


def azimuth_kernel(dens_ref, phi_ref, mate_ref, far_ref, out_ref, dens_buf, phi_buf, sems):
    lane = lax.broadcasted_iota(jnp.int32, (1, 8, 128), 2)
    copies = []
    for group in range(GROUPS):
        copies.append(
            (
                pltpu.make_async_copy(dens_ref.at[group], dens_buf.at[group], sems.at[2 * group]),
                pltpu.make_async_copy(phi_ref.at[group], phi_buf.at[group], sems.at[2 * group + 1]),
            )
        )
    for pair in copies:
        for copy in pair:
            copy.start()

    odd = lax.axis_index(AZ) % 2 == 1

    def following(value):
        turned = pltpu.roll(value, 127, 2)
        return jnp.where(lane == 127, turned[1:], turned[:-1])

    def widened(ref, group, base):
        middle = ref[group].reshape(CHUNKS, 8, 128)
        mate, far = mate_ref[base + group][None], far_ref[base + group][None]
        return jnp.concatenate(
            [jnp.where(odd, mate, far), middle, jnp.where(odd, far, mate)], axis=0
        )

    for group in range(GROUPS):
        for copy in copies[group]:
            copy.wait()
        dens = widened(dens_buf, group, 0)
        phi = widened(phi_buf, group, GROUPS)
        speeds = 0.5 * (phi[:-1] + following(phi))
        flux = donor_flux(speeds, dens[:-1], following(dens))
        turned = pltpu.roll(flux, 1, 2)
        before = jnp.where(lane == 0, turned[:-1], turned[1:])
        stepped = dens[1:-1] - courant * (flux[1:] - before)
        out_ref[group] = stepped.reshape(SPAN, 128)


def fill_ring(group, own_ref, mate_ref, cross_ref, far_ref, ring_ref, unit):
    odd = lax.axis_index(AZ) % 2
    places = ((own_ref, 0), (own_ref, 4), (cross_ref, 2), (mate_ref, 1 + 2 * odd), (far_ref, 3 - 2 * odd))
    for source, place in places:
        where = pl.ds(pl.multiple_of(place * unit, unit), unit)
        ring_ref[where, :] = source[group, 0:unit, :]


def shift_row(ring_ref, step, row, offset):
    start = ANGULAR_BINS - offset
    chunk = start // 128
    turn = (128 - start % 128) % 128
    lane = lax.broadcasted_iota(jnp.int32, (CHUNKS, 128), 1)
    first = ring_ref[pl.ds(chunk * step + row, CHUNKS, stride=step), :]
    second = ring_ref[pl.ds((chunk + 1) * step + row, CHUNKS, stride=step), :]
    return jnp.where(
        lane < 128 - start % 128, pltpu.roll(first, turn, 1), pltpu.roll(second, turn, 1)
    )


def shift_kernel(offs_ref, own_ref, mate_ref, cross_ref, far_ref, out_ref, ring_ref):
    @pl.loop(0, GROUPS)
    def _(group):
        fill_ring(group, own_ref, mate_ref, cross_ref, far_ref, ring_ref, SPAN)
        for row in range(8):
            moved = shift_row(ring_ref, 8, row, offs_ref[group * 8 + row])
            out_ref[group, pl.ds(row, CHUNKS, stride=8), :] = moved


def shifted(offsets, own, mate, cross, far, name):
    return pl.pallas_call(
        shift_kernel,
        out_shape=jax.ShapeDtypeStruct((GROUPS, SPAN, 128), F32),
        in_specs=[smem(), vmem(), vmem(), vmem(), vmem()],
        out_specs=vmem(),
        scratch_shapes=[pltpu.VMEM((RING, 128), F32)],
        compiler_params=params(),
        cost_estimate=cost(2),
        name=name,
    )(offsets, own, mate, cross, far)


def share_kernel(offs_ref, own_ref, mate_ref, *refs, kinds):
    odd = lax.axis_index(AZ) % 2
    sent = (own_ref, 2), (mate_ref, 3 - 2 * odd)
    kept = (own_ref, 0), (own_ref, 4), (mate_ref, 1 + 2 * odd)
    out_refs, ring_refs = refs[: len(kinds)], refs[len(kinds) :]
    for ring_ref in ring_refs:
        ring_ref[...] = jnp.zeros_like(ring_ref)

    @pl.loop(0, GROUPS)
    def _(group):
        for kind, out_ref, ring_ref in zip(kinds, out_refs, ring_refs):
            for source, place in sent if kind else kept:
                where = pl.ds(pl.multiple_of(place * SPAN, SPAN), SPAN)
                ring_ref[where, :] = source[group]
            for row in range(8):
                moved = shift_row(ring_ref, 8, row, offs_ref[group * 8 + row])
                out_ref[group, pl.ds(row, CHUNKS, stride=8), :] = moved


def share(offsets, own, mate, kinds, name):
    return pl.pallas_call(
        functools.partial(share_kernel, kinds=kinds),
        out_shape=tuple(jax.ShapeDtypeStruct((GROUPS, SPAN, 128), F32) for _ in kinds),
        in_specs=[smem(), vmem(), vmem()],
        out_specs=tuple(vmem() for _ in kinds),
        scratch_shapes=[pltpu.VMEM((RING, 128), F32) for _ in kinds],
        compiler_params=params(),
        cost_estimate=cost(2),
        name=name,
    )(offsets, own, mate)


def edge_kernel(
    offs_ref, own_ref, mate_ref, cross_ref, far_ref, first_ref, second_ref, ring_ref, flux_ref, line_ref
):
    unit = 3 * CHUNKS
    length = 5 * CHUNKS
    lane = lax.broadcasted_iota(jnp.int32, (length, 128), 1)
    sides = []
    for side in range(2):
        fill_ring(side, own_ref, mate_ref, cross_ref, far_ref, ring_ref, unit)
        ring_ref[5 * unit : 5 * unit + 24, :] = ring_ref[unit : unit + 24, :]
        offset = offs_ref[(ROWS - 1) * side]

        def following(index):
            here = pltpu.roll(ring_ref[pl.ds(index, length, stride=3), :], 127, 1)
            there = pltpu.roll(ring_ref[pl.ds(index + 3, length, stride=3), :], 127, 1)
            return jnp.where(lane == 127, there, here)

        dens = ring_ref[pl.ds(0, length, stride=3), :]
        phi = ring_ref[pl.ds(1, length, stride=3), :]
        flux = donor_flux(0.5 * (phi + following(1)), dens, following(0))
        flux_ref[8 : 8 + length, :] = flux
        before = pltpu.roll(flux_ref[7 : 7 + length, :], 1, 1)
        before = jnp.where(lane == 0, before, pltpu.roll(flux, 1, 1))
        line_ref[0:length, :] = dens - courant * (flux - before)
        sides.append((shift_row(line_ref, 1, 0, offset), shift_row(ring_ref, 3, 2, offset)))
    even = lax.axis_index(RAD) % 2 == 0
    for index in range(2):
        where = slice(CHUNKS * index, CHUNKS * index + CHUNKS)
        down, up = sides[0][index], sides[1][index]
        first_ref[where, :] = jnp.where(even, up, down)
        second_ref[where, :] = jnp.where(even, down, up)


def split_value(value):
    high = value.astype(BF16)
    return high, (value - high.astype(F32)).astype(BF16)


def dot(left, right):
    return jnp.dot(left, right, preferred_element_type=F32)


def transport_kernel(
    kept_ref, sent_ref, first_ref, second_ref, vrad_ref, high_ref, low_ref, twiddle_ref,
    whole_ref, dens_ref, spectra_ref,
    moved_ref, other_ref, speed_ref, whole_sem,
):
    for group in range(GROUPS):
        moved_ref[group] = kept_ref[group] + sent_ref[group]
    even = lax.axis_index(RAD) % 2 == 0
    first, second = first_ref[...], second_ref[...]
    for side, row in enumerate((7, 0)):
        edge = jnp.where(even, second, first) if side == 0 else jnp.where(even, first, second)
        other_ref[side, pl.ds(row, CHUNKS, stride=8), :] = edge[0:CHUNKS]
        speed_ref[side, pl.ds(row, CHUNKS, stride=8), :] = edge[CHUNKS:]

    sub = lax.broadcasted_iota(jnp.int32, (1, 8, 128), 1)
    own_index = lax.axis_index(RAD)
    bottom = own_index == 0
    top = own_index == lax.axis_size(RAD) - 1

    def above(value, following):
        return jnp.where(sub == 7, pltpu.roll(following, 7, 1), pltpu.roll(value, 7, 1))

    def below(value, previous):
        return jnp.where(sub == 0, pltpu.roll(previous, 1, 1), pltpu.roll(value, 1, 1))

    step = 4
    for group in range(GROUPS):

        @pl.loop(0, CHUNKS // step)
        def _(part):
            where = pl.ds(pl.multiple_of(part * 8 * step, 8 * step), 8 * step)

            def tiles(ref, index):
                return ref[index, where, :].reshape(step, 8, 128)

            dens = tiles(moved_ref, group)
            upper = tiles(moved_ref, group + 1) if group < 3 else tiles(other_ref, 1)
            lower = tiles(moved_ref, group - 1) if group > 0 else tiles(other_ref, 0)
            dens_above = above(dens, upper)
            dens_below = below(dens, lower)
            speed = tiles(vrad_ref, group)
            upper = tiles(vrad_ref, group + 1) if group < 3 else tiles(speed_ref, 1)
            lower = tiles(vrad_ref, group - 1) if group > 0 else tiles(speed_ref, 0)
            flux_above = donor_flux(0.5 * (speed + above(speed, upper)), dens, dens_above)
            flux_below = donor_flux(0.5 * (below(speed, lower) + speed), dens_below, dens)
            if group == 3:
                flux_above = jnp.where((sub == 7) & top, 0.0, flux_above)
            if group == 0:
                flux_below = jnp.where((sub == 0) & bottom, 0.0, flux_below)
            stepped = dens - courant * (flux_above - flux_below)
            dens_ref[group, where, :] = stepped.reshape(8 * step, 128)

    whole = pltpu.make_async_copy(dens_ref, whole_ref, whole_sem)
    whole.start()
    sector = lax.axis_index(AZ)
    cos_sum = jnp.zeros((ROWS, MODES), F32)
    sin_sum = jnp.zeros((ROWS, MODES), F32)
    together = 8
    for first in range(0, BLOCKS, together):
        pieces = []
        for block in range(first, first + together):
            halves = [
                dens_ref[:, 8 * chunk : 8 * chunk + 8, :].reshape(ROWS, 128)
                for chunk in (2 * block, 2 * block + 1)
            ]
            pieces.append(jnp.concatenate(halves, axis=1))
        high, low = split_value(jnp.concatenate(pieces, axis=0))
        part = dot(high, high_ref[...]) + (dot(low, high_ref[...]) + dot(high, low_ref[...]))
        for index in range(together):
            turn = twiddle_ref[pl.ds(sector * BLOCKS + first + index, 1), :]
            cosine, sine = turn[:, :MODES], turn[:, MODES:]
            rows = slice(index * ROWS, index * ROWS + ROWS)
            cos_part, sin_part = part[rows, :MODES], part[rows, MODES:]
            cos_sum += cosine * cos_part - sine * sin_part
            sin_sum += sine * cos_part + cosine * sin_part
    spectra_ref[:, :MODES] = cos_sum * cell_step
    spectra_ref[:, MODES:] = sin_sum * cell_step
    whole.wait()


def field_kernel(members_ref, radius_ref, angles_ref, *refs, base, many):
    radial_ref, azim_ref, gap_ref, chord_ref, lift_ref, side_ref = refs[-6:]
    if base:
        rows = slice(0, 8 * base)
        radial_ref[:, rows, :] = refs[0][:, rows, :]
        azim_ref[:, rows, :] = refs[1][:, rows, :]
    sector = lax.axis_index(AZ)
    half_cos = angles_ref[sector * 4, base : base + many, :]
    half_sin = angles_ref[sector * 4 + 1, base : base + many, :]
    radius = radius_ref[...]
    halves = 0.5 / radius

    @pl.loop(0, EMB, unroll=4)
    def _(member):
        embryo_radius = members_ref[0, member]
        scale = members_ref[1, member]
        cosine = members_ref[2, member]
        sine = members_ref[3, member]
        gap = radius - embryo_radius
        soft = softening * embryo_radius
        rows = pl.ds(pl.multiple_of(member * 32, 32), 32)
        gap_ref[rows, :] = (gap * gap + soft * soft) * halves * scale
        near = half_sin * cosine - half_cos * sine
        far = half_cos * cosine + half_sin * sine
        chord = (2.0 * embryo_radius) * (near * near)
        columns = pl.ds(pl.multiple_of(member * many, many), many)
        chord_ref[columns, :] = chord * scale
        lift_ref[columns, :] = chord - embryo_radius
        side_ref[columns, :] = (2.0 * embryo_radius) * (near * far)

    pieces = [radius[8 * g : 8 * g + 8] for g in range(GROUPS)]
    ends = []
    for g in range(GROUPS):
        root = lax.rsqrt(2.0 * pieces[g])
        ends.append(root * root * root)
    together = 2

    @pl.loop(0, many // together)
    def _(part):
        zero = jnp.zeros((8, 128), F32)

        def visit(member, carried):
            radial, azim = list(carried[0]), list(carried[1])
            rows = []
            for k in range(together):
                row = pl.ds(member * many + part * together + k, 1)
                rows.append(
                    [jnp.broadcast_to(ref[row, :], (8, 128)) for ref in (chord_ref, lift_ref, side_ref)]
                )
            for g in range(GROUPS):
                gap = gap_ref[pl.ds(pl.multiple_of(member * 32 + 8 * g, 8), 8), :]
                for k in range(together):
                    chord, lift, side = rows[k]
                    inverse = lax.rsqrt(gap + chord)
                    cubed = inverse * inverse * inverse
                    at = k * GROUPS + g
                    radial[at] = radial[at] + cubed * (pieces[g] + lift)
                    azim[at] = azim[at] + cubed * side
            return tuple(radial), tuple(azim)

        count = together * GROUPS
        radial, azim = lax.fori_loop(0, EMB, visit, ((zero,) * count, (zero,) * count), unroll=8)
        for k in range(together):
            where = pl.ds(pl.multiple_of((base + part * together + k) * 8, 8), 8)
            for g in range(GROUPS):
                radial_ref[g, where, :] = radial[k * GROUPS + g] * ends[g]
                azim_ref[g, where, :] = azim[k * GROUPS + g] * ends[g]


def push_kernel(
    members_ref, radius_ref, angles_ref, dens_ref, spectra_ref, out_ref, mass_ref, chord_ref, push_ref
):
    for part in range(4):
        out_ref[ROWS * part : ROWS * part + ROWS, :] = spectra_ref[:, 128 * part : 128 * part + 128]
    sector = lax.axis_index(AZ)
    radius = radius_ref[...]
    pieces = [radius[8 * g : 8 * g + 8] for g in range(GROUPS)]
    halves = [0.5 / piece for piece in pieces]
    for g in range(GROUPS):
        scale = lax.rsqrt(2.0 * pieces[g])
        area = pieces[g] * pieces[g] * (cell_step * cell_step) * (scale * scale * scale)
        mass_ref[g] = (dens_ref[g].reshape(CHUNKS, 8, 128) * area[None]).reshape(SPAN, 128)
    half_cos = angles_ref[sector * 4]
    half_sin = angles_ref[sector * 4 + 1]

    @pl.loop(0, EMB, unroll=4)
    def _(member):
        near = half_sin * members_ref[2, member] - half_cos * members_ref[3, member]
        rows = pl.ds(pl.multiple_of(member * CHUNKS, CHUNKS), CHUNKS)
        chord_ref[rows, :] = (2.0 * members_ref[0, member]) * (near * near)

    @pl.loop(0, EMB, unroll=4)
    def _(member):
        embryo_radius = members_ref[0, member]
        soft = softening * embryo_radius
        gaps = []
        for g in range(GROUPS):
            gap = pieces[g] - embryo_radius
            gaps.append((gap * gap + soft * soft) * halves[g])
        push_x = jnp.zeros((8, 128), F32)
        push_y = jnp.zeros((8, 128), F32)
        total = jnp.zeros((8, 128), F32)
        for chunk in range(CHUNKS):
            chord = jnp.broadcast_to(chord_ref[pl.ds(member * CHUNKS + chunk, 1), :], (8, 128))
            plain, moved = None, None
            for g in range(GROUPS):
                inverse = lax.rsqrt(gaps[g] + chord)
                cubed = inverse * inverse * inverse
                term = cubed * mass_ref[g, 8 * chunk : 8 * chunk + 8, :]
                plain = term if g == 0 else plain + term
                moved = pieces[g] * term if g == 0 else moved + pieces[g] * term
            row = slice(chunk, chunk + 1)
            push_x = push_x + moved * jnp.broadcast_to(angles_ref[sector * 4 + 2, row, :], (8, 128))
            push_y = push_y + moved * jnp.broadcast_to(angles_ref[sector * 4 + 3, row, :], (8, 128))
            total = total + plain
        place_x = embryo_radius * members_ref[4, member]
        place_y = embryo_radius * members_ref[5, member]
        push_ref[member] = push_x - place_x * total
        push_ref[EMB + member] = push_y - place_y * total

    push = jnp.sum(jnp.sum(push_ref[...], axis=1), axis=1, keepdims=True)
    push = jnp.broadcast_to(push, (2 * EMB, 128))
    row = lax.broadcasted_iota(jnp.int32, (2 * EMB, 128), 0)
    lane = lax.broadcasted_iota(jnp.int32, (2 * EMB, 128), 1)
    push = jnp.sum(jnp.where(row == lane, push, 0.0), axis=0, keepdims=True)
    out_ref[4 * ROWS : 4 * ROWS + 8, :] = jnp.broadcast_to(push, (8, 128))


def moment_kernel(a_ref, b_ref, lift_ref, drop_ref, vectors_ref, spectra_ref, packed_ref, one_ref):
    total = a_ref[...] + b_ref[...]
    for part in range(4):
        columns = slice(128 * part, 128 * part + 128)
        spectra = total[ROWS * part : ROWS * part + ROWS]
        spectra_ref[:, columns] = spectra
        factor = vectors_ref[0:1, columns]
        up = jnp.sum(spectra * drop_ref[:, columns], axis=0, keepdims=True) / factor
        down = jnp.sum(spectra * lift_ref[:, columns], axis=0, keepdims=True) / factor
        one_ref[part : part + 1, :] = up
        one_ref[4 + part : 5 + part, :] = down
    one_ref[8:16, :] = total[4 * ROWS :]
    one = one_ref[...]
    for copy in range(packed_ref.shape[0]):
        packed_ref[copy] = one


def kick_kernel(
    spectra_ref, moments_ref, rate_ref, radius_ref, vectors_ref, lift_ref, drop_ref, twiddle_ref, high_ref, low_ref,
    radial_ref, azim_ref, vrad_ref, vphi_kept_ref, vphi_sent_ref,
    whole_radial_ref, whole_azim_ref, out_push_ref,
    lower_ref, upper_ref, out_radial_ref, out_azim_ref, sems,
):
    own_index = lax.axis_index(RAD)
    row = lax.broadcasted_iota(jnp.int32, (8, 128), 0)
    outside = jnp.zeros((8, 128), F32)
    push = jnp.zeros((1, 128), F32)
    for source in range(moments_ref.shape[0]):
        many = jnp.where(row < 4, own_index - 1 - source, source - own_index - 1)
        weight = jnp.exp(-rate_ref[...] * jnp.maximum(many, 0).astype(F32))
        outside += jnp.where(many >= 0, weight, 0.0) * moments_ref[source, 0:8, :]
        push += moments_ref[source, 8:9, :]
    out_push_ref[0:1, :] = push[:, :EMB]
    out_push_ref[1:2, :] = push[:, EMB : 2 * EMB]
    lower = jnp.concatenate([outside[k : k + 1] for k in range(4)], axis=1)
    upper = jnp.concatenate([outside[k : k + 1] for k in range(4, 8)], axis=1)
    factor = vectors_ref[0:1, :]
    spectra = spectra_ref[...]
    for row in range(ROWS):
        lower = spectra[row : row + 1] + factor * lower
        lower_ref[row : row + 1, :] = lower
        back = ROWS - 1 - row
        upper = spectra[back : back + 1] + factor * upper
        upper_ref[back : back + 1, :] = upper
    lower = lower_ref[...]
    upper = upper_ref[...]
    inverse = 1.0 / radius_ref[:, 0:1]
    even = lower + upper - spectra
    odd = lower - upper
    radial = odd * vectors_ref[1:2, :] * inverse
    swapped = jnp.concatenate([even[:, MODES:], even[:, :MODES]], axis=1)
    azim = swapped * vectors_ref[2:3, :] * inverse
    sector = lax.axis_index(AZ)
    together = 8

    def whole_copies(quarter):
        rows = pl.ds(pl.multiple_of(16 * together * quarter, 16 * together), 16 * together)
        return [
            pltpu.make_async_copy(source.at[:, rows, :], target.at[:, rows, :], sems.at[index, quarter])
            for index, (source, target) in enumerate(
                ((out_radial_ref, whole_radial_ref), (out_azim_ref, whole_azim_ref))
            )
        ]

    @pl.loop(0, BLOCKS // together)
    def _(quarter):
        pieces = []
        for index in range(together):
            turn = twiddle_ref[pl.ds(sector * BLOCKS + quarter * together + index, 1), :]
            cosine, sine = turn[:, :MODES], turn[:, MODES:]
            for coef in (radial, azim):
                cos_coef, sin_coef = coef[:, :MODES], coef[:, MODES:]
                pieces.append(
                    jnp.concatenate(
                        [cos_coef * cosine + sin_coef * sine, sin_coef * cosine - cos_coef * sine], axis=1
                    )
                )
        high, low = split_value(jnp.concatenate(pieces, axis=0))
        part = dot(high, high_ref[...]) + (dot(low, high_ref[...]) + dot(high, low_ref[...]))
        for index in range(together):
            for half in range(2):
                start = 16 * together * quarter + 8 * (2 * index + half)
                where = pl.ds(pl.multiple_of(start, 8), 8)
                columns = slice(128 * half, 128 * half + 128)
                rows = 2 * ROWS * index
                disk = part[rows : rows + ROWS, columns].reshape(GROUPS, 8, 128)
                out_radial_ref[:, where, :] = vrad_ref[:, where, :] + timestep_length * (
                    disk - radial_ref[:, where, :]
                )
                disk = part[rows + ROWS : rows + 2 * ROWS, columns].reshape(GROUPS, 8, 128)
                vphi = vphi_kept_ref[:, where, :] + vphi_sent_ref[:, where, :]
                out_azim_ref[:, where, :] = vphi + timestep_length * (
                    disk - azim_ref[:, where, :]
                )
        for copy in whole_copies(quarter):
            copy.start()

    for quarter in range(BLOCKS // together):
        for copy in whole_copies(quarter):
            copy.wait()


def across(value, axis, target):
    count = lax.axis_size(axis)
    return lax.ppermute(value, axis, [(source, target(source)) for source in range(count)])


def after(value, *others):
    return lax.optimization_barrier((value, *others))[0]


def on_device(
    surface_mass,
    outward_drift,
    leftover_angular_drift,
    angular_offsets,
    planetesimal_loop_number,
    planetesimal_angle_bin,
    planetesimal_weights,
):
    (basis_high, basis_low), (back_high, back_low), twiddle, angles, lift, drop, vectors, rate = (
        constant_tables()
    )
    tiles = jax.ShapeDtypeStruct((GROUPS, SPAN, 128), F32)
    dens = to_tiles(surface_mass)
    vrad = to_tiles(outward_drift)
    vphi = to_tiles(leftover_angular_drift)

    halo = jax.ShapeDtypeStruct((2 * GROUPS, 8, 128), F32)
    outer, inner, edge_rows = pl.pallas_call(
        border_kernel,
        out_shape=(halo, halo, jax.ShapeDtypeStruct((2, 3 * CHUNKS, 128), F32)),
        in_specs=[pl.BlockSpec(memory_space=pltpu.HBM)] * 3,
        out_specs=(vmem(), vmem(), vmem()),
        scratch_shapes=[pltpu.VMEM((6, SPAN, 128), F32), pltpu.SemaphoreType.DMA((10,))],
        compiler_params=params(),
        cost_estimate=cost(1),
        name="borders",
    )(hbm(dens), hbm(vphi), hbm(vrad))
    border_far = across(outer, AZ, lambda i: i ^ 3)
    border_mate = across(inner, AZ, lambda i: i ^ 1)
    edge_cross = across(edge_rows, AZ, lambda i: i ^ 2)
    edge_mate = across(edge_rows, AZ, lambda i: i ^ 1)
    vrad_cross = across(after(vrad, edge_rows), AZ, lambda i: i ^ 2)
    vrad_mate = across(vrad, AZ, lambda i: i ^ 1)

    cell = np.float32(cell_step)
    cycles = lax.axis_index(RAD) * ROWS + jnp.arange(ROWS, dtype=jnp.int32)
    radius = jnp.broadcast_to(jnp.exp((cycles.astype(F32) + 0.5) * cell)[:, None], (ROWS, 128))
    embryo_angles = (2 * planetesimal_angle_bin + 1).astype(F32) * np.float32(np.pi / ANGULAR_BINS)
    members = jnp.stack(
        [
            jnp.exp((planetesimal_loop_number.astype(F32) + 0.5) * cell),
            jnp.exp(np.float32(-2.0 / 3.0) * jnp.log(planetesimal_weights)),
            jnp.cos(0.5 * embryo_angles),
            jnp.sin(0.5 * embryo_angles),
            jnp.cos(embryo_angles),
            jnp.sin(embryo_angles),
        ]
    )

    dens_two = pl.pallas_call(
        azimuth_kernel,
        out_shape=tiles,
        in_specs=[pl.BlockSpec(memory_space=pltpu.HBM)] * 2 + [vmem()] * 2,
        out_specs=vmem(),
        scratch_shapes=[
            pltpu.VMEM((GROUPS, SPAN, 128), F32),
            pltpu.VMEM((GROUPS, SPAN, 128), F32),
            pltpu.SemaphoreType.DMA((8,)),
        ],
        compiler_params=params(),
        cost_estimate=cost(1),
        name="azimuth",
    )(hbm(dens), hbm(vphi), border_mate, border_far)

    edge_far = across(edge_cross, AZ, lambda i: i ^ 1)
    edge = jax.ShapeDtypeStruct((2 * CHUNKS, 128), F32)
    edge_first, edge_second = pl.pallas_call(
        edge_kernel,
        out_shape=(edge, edge),
        in_specs=[smem()] + [vmem()] * 4,
        out_specs=(vmem(), vmem()),
        scratch_shapes=[
            pltpu.VMEM((3 * RING // 8, 128), F32),
            pltpu.VMEM((RING // 8 + 8, 128), F32),
            pltpu.VMEM((RING // 8, 128), F32),
        ],
        compiler_params=params(),
        cost_estimate=cost(1),
        name="edges",
    )(angular_offsets, edge_rows, edge_mate, edge_cross, edge_far)
    rad_count = lax.axis_size(RAD)
    inside = range(1, rad_count - 1)
    edge_second = lax.ppermute(edge_second, RAD, [(i, i + 1 if i % 2 else i - 1) for i in inside])
    edge_first_in = across(edge_first, RAD, lambda i: i ^ 1)

    def field(base, many, *before):
        return pl.pallas_call(
            functools.partial(field_kernel, base=base, many=many),
            out_shape=(tiles, tiles),
            in_specs=[smem(), vmem(), vmem()] + [vmem()] * len(before),
            out_specs=(vmem(), vmem()),
            scratch_shapes=[pltpu.VMEM((EMB * 32, 128), F32)] + [pltpu.VMEM((EMB * many, 128), F32)] * 3,
            compiler_params=params(),
            cost_estimate=cost(many // 4),
            name=f"field_{base}",
        )(members, radius, angles, *before)

    first_field = field(0, 16)
    dens_mate = across(dens_two, AZ, lambda i: i ^ 1)
    (dens_sent,) = share(angular_offsets, dens_two, dens_mate, (True,), "share_dens")
    vphi_mate = across(vphi, AZ, lambda i: i ^ 1)
    vphi_sent, vphi_kept = share(angular_offsets, vphi, vphi_mate, (True, False), "share_vphi")
    early = (dens_sent, *first_field, edge_first, vphi_sent, vphi_kept)
    vrad_far = across(after(vrad_cross, *early), AZ, lambda i: i ^ 1)
    dens_cross = across(after(dens_sent, vrad_cross, *early), AZ, lambda i: i ^ 2)
    (dens_kept,) = share(angular_offsets, dens_two, dens_mate, (False,), "keep_dens")
    vrad_one = shifted(angular_offsets, vrad, vrad_mate, vrad_cross, vrad_far, "shift_vrad")
    middle_field = field(16, 8, *first_field)
    dens_cross = after(
        dens_cross, vrad_one, *middle_field, dens_kept, vphi_sent, vphi_kept, edge_first_in, edge_second
    )
    vphi_cross = across(after(vphi_sent, vrad_one), AZ, lambda i: i ^ 2)

    transported, stepped, part = pl.pallas_call(
        transport_kernel,
        out_shape=(tiles, tiles, jax.ShapeDtypeStruct((ROWS, 2 * MODES), F32)),
        in_specs=[vmem()] * 8,
        out_specs=(anywhere(), vmem(), vmem()),
        scratch_shapes=[
            pltpu.VMEM((GROUPS, SPAN, 128), F32),
            pltpu.VMEM((2, SPAN, 128), F32),
            pltpu.VMEM((2, SPAN, 128), F32),
            pltpu.SemaphoreType.DMA,
        ],
        compiler_params=params(),
        cost_estimate=cost(3),
        name="transport",
    )(
        dens_kept, dens_cross, edge_first_in, edge_second,
        vrad_one, basis_high, basis_low, twiddle,
    )

    joined_shape = jax.ShapeDtypeStruct((4 * ROWS + 8, 128), F32)
    joined = pl.pallas_call(
        push_kernel,
        out_shape=joined_shape,
        in_specs=[smem()] + [vmem()] * 4,
        out_specs=vmem(),
        scratch_shapes=[
            pltpu.VMEM((GROUPS, SPAN, 128), F32),
            pltpu.VMEM((EMB * CHUNKS, 128), F32),
            pltpu.VMEM((2 * EMB, 8, 128), F32),
        ],
        compiler_params=params(),
        cost_estimate=cost(6),
        name="push",
    )(members, radius, angles, stepped, part)
    chip = joined + across(joined, AZ, lambda i: i ^ 1)
    chip_other = across(chip, AZ, lambda i: i ^ 2)

    radial_field, azim_field = field(24, 8, *middle_field)
    chip_later = after(chip, vphi_cross, radial_field)
    spectra, packed = pl.pallas_call(
        moment_kernel,
        out_shape=(
            jax.ShapeDtypeStruct((ROWS, 2 * MODES), F32),
            jax.ShapeDtypeStruct((rad_count, 16, 128), F32),
        ),
        in_specs=[vmem()] * 5,
        out_specs=(vmem(), vmem()),
        scratch_shapes=[pltpu.VMEM((16, 128), F32)],
        compiler_params=params(),
        cost_estimate=cost(1),
        name="moments",
    )(chip_later, chip_other, lift, drop, vectors)
    gathered = lax.all_to_all(packed, RAD, split_axis=0, concat_axis=0, tiled=True)

    kicked_radial, kicked_azim, embryo_disk_acceleration = pl.pallas_call(
        kick_kernel,
        out_shape=(tiles, tiles, jax.ShapeDtypeStruct((2, EMB), F32)),
        in_specs=[vmem()] * 15,
        out_specs=(anywhere(), anywhere(), vmem()),
        scratch_shapes=[
            pltpu.VMEM((ROWS, 2 * MODES), F32),
            pltpu.VMEM((ROWS, 2 * MODES), F32),
            pltpu.VMEM((GROUPS, SPAN, 128), F32),
            pltpu.VMEM((GROUPS, SPAN, 128), F32),
            pltpu.SemaphoreType.DMA((2, 4)),
        ],
        compiler_params=params(),
        cost_estimate=cost(5),
        name="kick",
    )(
        spectra, gathered, rate, radius, vectors, lift, drop, twiddle, back_high, back_low,
        radial_field, azim_field, vrad_one, vphi_kept, vphi_cross,
    )
    return (
        from_tiles(transported),
        from_tiles(kicked_radial),
        from_tiles(kicked_azim),
        embryo_disk_acceleration,
    )


def solution(mesh):
    torus = Mesh(mesh.devices.reshape(4, 2, 4, 2, 2), RAD + AZ)
    placed = (P(RAD, AZ), P(RAD, AZ), P(RAD, AZ), P(RAD), P(), P(), P())
    return jax.shard_map(
        on_device,
        mesh=torus,
        in_specs=placed,
        out_specs=(P(RAD, AZ), P(RAD, AZ), P(RAD, AZ), P()),
        check_vma=False,
    )
```
